32 devices in a mesh: expert: 32 (over z, y, x, core), dp: 1.
Axes of the slice: x: 2, y: 2, z: 4, core: 2. Of those that a mesh axis runs over, the one named last changes fastest.
Arguments:
- tokens: bfloat16 [2048, 2048], P(('expert', 'dp')), may hold values from -6 to 6
- attn_partials: bfloat16 [1, 2048, 2048], P('dp', 'expert'), may hold values from -5 to 5
- expert_ids: int32 [2048], P(('expert', 'dp')), may hold values from 0 to 1, as said below
- gate: float32 [2048], P(('expert', 'dp')), may hold values from 0.2 to 1
- w_in: float32 [2048, 10240], P('dp', 'expert'), may hold values from -6 to 6
- w_out: float32 [2048, 10240], P('dp', 'expert'), may hold values from -6 to 6
Outputs:
- token_grad: bfloat16 [2048, 2048], P(('expert', 'dp'))
- new_w_in: float32 [2048, 10240], P('dp', 'expert')
- new_w_out: float32 [2048, 10240], P('dp', 'expert')
The draws below stay inside these ranges and needn't reach their ends.
Inputs may be any that keep to these rules, and one draw needn't show every extreme that they name: `expert_ids`: one expert, the same for all devices, is chosen by half of the 64 rows of every device; the other experts share the remaining rows of a device as evenly as whole numbers allow.
All inputs are finite; a program needn't handle non-finite values.
Results may differ from the reference program's by a relative error of at most 0.025.
Values may be sent and summed in bfloat16 or wider, within the bound.
No kernel may reach another device: no remote copies, remote signals or barrier semaphores. Data moves between devices by JAX's collectives and lax.ppermute only.
A program may use at most 64 MiB of HBM per device.

```python
import jax
import jax.numpy as jnp
from jax import lax

D = 2048
FF = 5120
SHARDS = 16
TOK_DEV = 64
EXPERTS = 2
CAP = 20
TOKENS = 2048
N_EXPERT = 32
N_DP = 1


def draw_expert_ids(key, part):
    blocks = TOKENS // TOK_DEV
    spread = max(EXPERTS - 1, 1)
    popular = TOK_DEV // 2
    hot_key, shift_key, order_key = jax.random.split(key, 3)
    hot_expert = jax.random.randint(hot_key, (), 0, EXPERTS)
    shifts = jax.random.randint(shift_key, (blocks, 1), 0, spread)
    positions = jnp.arange(TOK_DEV)[None, :]
    others = (hot_expert + 1 + (positions - popular + shifts) % spread) % EXPERTS
    labels = jnp.where(positions < popular, hot_expert, others)
    block_keys = jax.random.split(order_key, blocks)
    shuffles = jax.vmap(lambda one_key: jax.random.permutation(one_key, TOK_DEV))(block_keys)
    shuffled_ids = jnp.take_along_axis(labels, shuffles, axis=1)
    return shuffled_ids.reshape(TOKENS).astype(jnp.int32)


def block_levels(own_key, dims, shards, low, largest):
    gain = 1.0
    for dim, parts in shards:
        heights = jax.random.uniform(jax.random.fold_in(jax.random.fold_in(own_key, 6), dim), (parts,), jnp.float32, low / len(shards), largest / len(shards))
        gain = gain * jnp.repeat(jnp.exp(heights), dims[dim] // parts).reshape((-1,) + (1,) * (len(dims) - 1 - dim))
    return gain


def gaussian(rng, shape, width, reach, pieces=(), kind=jnp.bfloat16):
    entries = width * jax.random.normal(rng, shape, jnp.float32)
    if pieces:
        entries = entries * block_levels(rng, shape, pieces, -0.22, 0.18)
    return jnp.clip(entries, -reach, reach).astype(kind)


def setup_inputs(seed: int = 0) -> dict:
    key_list = jax.random.split(jax.random.key(seed), 7)
    return {
        "tokens": gaussian(key_list[0], (TOKENS, D), 1.0, 6.0, ((0, 32),)),
        "attn_partials": gaussian(key_list[1], (N_DP, TOKENS, D), 0.35, 5.0, ((1, 32),)),
        "expert_ids": draw_expert_ids(jax.random.fold_in(key_list[6], 71), 0),
        "gate": jnp.clip(0.2 + 0.8 * jax.random.uniform(key_list[3], (TOKENS,), jnp.float32) ** block_levels(key_list[3], (TOKENS,), ((0, 32),), -0.2, 0.2), 0.2, 1.0),
        "w_in": gaussian(key_list[4], (D, EXPERTS * FF), 1.0, 6.0, ((1, 32),), jnp.float32),
        "w_out": gaussian(key_list[5], (D, EXPERTS * FF), 1.0, 6.0, ((1, 32),), jnp.float32),
    }


gelu_coef = 0.7978845608028654
cubic_coef = 0.044715
step_rate = 0.5


def gelu_value(inputs):
    return 0.5 * inputs * (1.0 + jnp.tanh(gelu_coef * (inputs + cubic_coef * inputs * inputs * inputs)))


def gelu_slope(inputs):
    tangent = jnp.tanh(gelu_coef * (inputs + cubic_coef * inputs * inputs * inputs))
    return 0.5 * (1.0 + tangent) + 0.5 * inputs * (1.0 - tangent * tangent) * gelu_coef * (1.0 + 3.0 * cubic_coef * inputs * inputs)


def contract_rows(left, right):
    return lax.dot_general(left, right, (((0,), (0,)), ((), ())), preferred_element_type=jnp.float32)


def contract_cols(left, right):
    return lax.dot_general(left, right, (((1,), (1,)), ((), ())), preferred_element_type=jnp.float32)


def reference(tokens, attn_partials, expert_ids, gate, w_in, w_out):
    out_grad = jnp.sum(attn_partials, axis=0, dtype=jnp.float32)
    gated = (gate[:, None] * out_grad).astype(jnp.bfloat16)
    weights_in = w_in.astype(jnp.bfloat16)
    weights_out = w_out.astype(jnp.bfloat16)
    scale_in = D ** -0.5
    scale_out = FF ** -0.5
    window = N_EXPERT * CAP
    hidden_units = FF // SHARDS
    blocks = TOKENS // TOK_DEV
    id_blocks = expert_ids.astype(jnp.int32).reshape(blocks, TOK_DEV)
    expert_range = jnp.arange(EXPERTS, dtype=jnp.int32)
    member = (id_blocks[:, :, None] == expert_range[None, None, :]).astype(jnp.int32)
    ranks = jnp.sum(member * (jnp.cumsum(member, axis=1) - 1), axis=2).reshape(TOKENS)
    kept = ranks < CAP
    token_index = jnp.arange(TOKENS, dtype=jnp.int32)
    groups = (token_index // TOK_DEV) % N_DP
    segment = jnp.where(kept, expert_ids.astype(jnp.int32) * N_DP + groups, EXPERTS * N_DP).astype(jnp.int32)
    ordering = jnp.argsort(segment, stable=True).astype(jnp.int32)
    segment_range = jnp.arange(EXPERTS * N_DP, dtype=jnp.int32)
    counts = jnp.sum((segment[None, :] == segment_range[:, None]).astype(jnp.int32), axis=1)
    starts = (jnp.cumsum(counts) - counts).astype(jnp.int32)
    padded_order = jnp.concatenate([ordering, jnp.full((window,), TOKENS, jnp.int32)])
    padded_tokens = jnp.concatenate([tokens, jnp.zeros((1, D), jnp.bfloat16)])
    padded_gated = jnp.concatenate([gated, jnp.zeros((1, D), jnp.bfloat16)])

    def one_expert(expert):
        cols_in = lax.dynamic_slice_in_dim(weights_in, expert * FF, FF, 1)
        cols_out = lax.dynamic_slice_in_dim(weights_out, expert * FF, FF, 1)

        def one_group(totals, group):
            seg_index = expert * N_DP + group
            picked = lax.dynamic_slice_in_dim(padded_order, starts[seg_index], window, 0)
            live = jnp.arange(window, dtype=jnp.int32) < counts[seg_index]
            picked = jnp.where(live, picked, TOKENS).astype(jnp.int32)
            source_rows = jnp.take(padded_tokens, picked, axis=0)
            grad_rows = jnp.take(padded_gated, picked, axis=0)
            pre_act = jnp.dot(source_rows, cols_in, preferred_element_type=jnp.float32) * scale_in
            hidden = gelu_value(pre_act).astype(jnp.bfloat16)
            hidden_grad = jnp.dot(grad_rows, cols_out, preferred_element_type=jnp.float32) * scale_out
            pre_grad = (hidden_grad * gelu_slope(pre_act)).astype(jnp.bfloat16)
            x_total = jnp.zeros((window, D), jnp.float32)
            for shard in range(SHARDS):
                first = shard * hidden_units
                share = contract_cols(pre_grad[:, first:first + hidden_units], cols_in[:, first:first + hidden_units]) * scale_in
                x_total = x_total + share.astype(jnp.bfloat16).astype(jnp.float32)
            grad_in = (contract_rows(source_rows, pre_grad) * scale_in).astype(jnp.bfloat16)
            grad_out = (contract_rows(grad_rows, hidden) * scale_out).astype(jnp.bfloat16)
            totals = (totals[0] + grad_in.astype(jnp.float32), totals[1] + grad_out.astype(jnp.float32))
            return totals, (x_total.astype(jnp.bfloat16), picked)

        zeros_block = jnp.zeros((D, FF), jnp.float32)
        totals, outputs = lax.scan(one_group, (zeros_block, zeros_block), jnp.arange(N_DP, dtype=jnp.int32))
        return totals[0], totals[1], outputs[0], outputs[1]

    grads_in, grads_out, x_blocks, picks = lax.map(one_expert, jnp.arange(EXPERTS, dtype=jnp.int32))
    token_grad = jnp.zeros((TOKENS + 1, D), jnp.bfloat16)
    token_grad = token_grad.at[picks.reshape(-1)].set(x_blocks.reshape(-1, D))[:TOKENS]
    step_in = jnp.transpose(grads_in, (1, 0, 2)).reshape(D, EXPERTS * FF)
    step_out = jnp.transpose(grads_out, (1, 0, 2)).reshape(D, EXPERTS * FF)
    new_w_in = w_in - step_rate * step_in
    new_w_out = w_out - step_rate * step_out
    return token_grad, new_w_in, new_w_out
```

```python
import jax
import jax.numpy as jnp
from jax import lax
from jax.sharding import PartitionSpec as P

FF = 5120
SHARDS = 16


gelu_coef = 0.7978845608028654
cubic_coef = 0.044715
step_rate = 0.5


def gelu_value(inputs):
    return (
        0.5
        * inputs
        * (1.0 + jnp.tanh(gelu_coef * (inputs + cubic_coef * inputs * inputs * inputs)))
    )


def gelu_slope(inputs):
    tangent = jnp.tanh(gelu_coef * (inputs + cubic_coef * inputs * inputs * inputs))
    return 0.5 * (1.0 + tangent) + 0.5 * inputs * (1.0 - tangent * tangent) * gelu_coef * (
        1.0 + 3.0 * cubic_coef * inputs * inputs
    )


def contract_rows(left, right):
    return lax.dot_general(
        left, right, (((0,), (0,)), ((), ())), preferred_element_type=jnp.float32
    )


def contract_cols(left, right):
    return lax.dot_general(
        left, right, (((1,), (1,)), ((), ())), preferred_element_type=jnp.float32
    )


def summed_grads(attn_partials, gate):
    if lax.axis_size("dp") == 1:
        out_grad = attn_partials[0].astype(jnp.float32)
    else:
        out_grad = lax.psum_scatter(
            attn_partials[0], "dp", scatter_dimension=0, tiled=True
        ).astype(jnp.float32)
    return (gate[:, None] * out_grad).astype(jnp.bfloat16)


def whole_weights(shard):
    if lax.axis_size("dp") == 1:
        return shard.astype(jnp.bfloat16)
    return lax.all_gather(shard.astype(jnp.bfloat16), "dp", axis=0, tiled=True)


def stepped(weights, grads):
    if lax.axis_size("dp") > 1:
        grads = lax.psum_scatter(
            grads.astype(jnp.bfloat16), "dp", scatter_dimension=0, tiled=True
        ).astype(jnp.float32)
    return weights - step_rate * grads


def shards(tokens, attn_partials, expert_ids, gate, w_in, w_out):
    tok_rows, width = tokens.shape
    n_expert = lax.axis_size("expert")
    experts = n_expert // SHARDS
    capacity = 5 * tok_rows // (8 * experts)
    scale_in = width ** (-0.5)
    scale_out = FF ** (-0.5)
    groups = [[e * SHARDS + k for k in range(SHARDS)] for e in range(experts)]

    def shifted(rows, hops):
        pairs = [(i, (i + SHARDS * hops) % n_expert) for i in range(n_expert)]
        return lax.ppermute(rows, "expert", pairs)

    my_expert = lax.axis_index("expert") // SHARDS
    relative = lax.rem(expert_ids - my_expert + experts, experts)
    expert_range = jnp.arange(experts, dtype=jnp.int32)
    member = (relative[:, None] == expert_range[None, :]).astype(jnp.int32)
    slot_rank = jnp.sum(member * (jnp.cumsum(member, axis=0) - 1), axis=1)
    flat_slot = jnp.where(slot_rank < capacity, relative * capacity + slot_rank, -1)
    slot_range = jnp.arange(experts * capacity, dtype=jnp.int32)
    dispatch = (slot_range[:, None] == flat_slot[None, :]).astype(jnp.bfloat16)

    gated = summed_grads(attn_partials, gate)
    both = jnp.concatenate([tokens, gated], axis=1)
    packed = jnp.dot(dispatch, both, preferred_element_type=jnp.float32).astype(jnp.bfloat16)
    packed = packed.reshape(experts, capacity, 2 * width)
    arrived = [packed[0]] + [shifted(packed[s], s) for s in range(1, experts)]
    own_rows = jnp.concatenate(arrived, axis=0)
    rows = lax.all_gather(own_rows, "expert", axis=0, tiled=True, axis_index_groups=groups)
    expert_rows = rows[:, :width]
    grad_rows = rows[:, width:]

    weights_in = whole_weights(w_in)
    weights_out = whole_weights(w_out)
    pre_act = jnp.dot(expert_rows, weights_in, preferred_element_type=jnp.float32) * scale_in
    hidden = gelu_value(pre_act).astype(jnp.bfloat16)
    hidden_grad = jnp.dot(grad_rows, weights_out, preferred_element_type=jnp.float32) * scale_out
    pre_grad = (hidden_grad * gelu_slope(pre_act)).astype(jnp.bfloat16)
    partial_x = (contract_cols(pre_grad, weights_in) * scale_in).astype(jnp.bfloat16)
    sums = lax.psum_scatter(
        partial_x, "expert", scatter_dimension=0, tiled=True, axis_index_groups=groups
    ).reshape(experts, capacity, width)
    back = [sums[0]] + [shifted(sums[s], -s) for s in range(1, experts)]
    slot_sums = jnp.concatenate(back, axis=0)
    token_grad = contract_rows(dispatch, slot_sums).astype(jnp.bfloat16)
    new_w_in = stepped(w_in, contract_rows(expert_rows, pre_grad) * scale_in)
    new_w_out = stepped(w_out, contract_rows(grad_rows, hidden) * scale_out)
    return (token_grad, new_w_in, new_w_out)


def solution(mesh):
    in_specs = (
        P(("expert", "dp"), None),
        P("dp", "expert", None),
        P(("expert", "dp")),
        P(("expert", "dp")),
        P("dp", "expert"),
        P("dp", "expert"),
    )
    out_specs = (P(("expert", "dp"), None), P("dp", "expert"), P("dp", "expert"))
    return jax.shard_map(shards, mesh=mesh, in_specs=in_specs, out_specs=out_specs, check_vma=False)
```

```python
import jax
import jax.numpy as jnp
from jax import lax
from jax.sharding import PartitionSpec as P

FF = 5120
SHARDS = 16


gelu_coef = 0.7978845608028654
cubic_coef = 0.044715
step_rate = 0.5


def gelu_value(inputs):
    return (
        0.5
        * inputs
        * (1.0 + jnp.tanh(gelu_coef * (inputs + cubic_coef * inputs * inputs * inputs)))
    )


def gelu_slope(inputs):
    tangent = jnp.tanh(gelu_coef * (inputs + cubic_coef * inputs * inputs * inputs))
    return 0.5 * (1.0 + tangent) + 0.5 * inputs * (1.0 - tangent * tangent) * gelu_coef * (
        1.0 + 3.0 * cubic_coef * inputs * inputs
    )


def contract_rows(left, right):
    return lax.dot_general(
        left, right, (((0,), (0,)), ((), ())), preferred_element_type=jnp.float32
    )


def contract_cols(left, right):
    return lax.dot_general(
        left, right, (((1,), (1,)), ((), ())), preferred_element_type=jnp.float32
    )


def summed_grads(attn_partials, gate):
    if lax.axis_size("dp") == 1:
        out_grad = attn_partials[0].astype(jnp.float32)
    else:
        out_grad = lax.psum_scatter(
            attn_partials[0], "dp", scatter_dimension=0, tiled=True
        ).astype(jnp.float32)
    return (gate[:, None] * out_grad).astype(jnp.bfloat16)


def whole_weights(shard):
    if lax.axis_size("dp") == 1:
        return shard.astype(jnp.bfloat16)
    return lax.all_gather(shard.astype(jnp.bfloat16), "dp", axis=0, tiled=True)


def stepped(weights, grads):
    if lax.axis_size("dp") > 1:
        grads = lax.psum_scatter(
            grads.astype(jnp.bfloat16), "dp", scatter_dimension=0, tiled=True
        ).astype(jnp.float32)
    return weights - step_rate * grads


def swap(rows, mask):
    n_expert = lax.axis_size("expert")
    return lax.ppermute(rows, "expert", [(i, i ^ mask) for i in range(n_expert)])


core_bit, x_bit, y_bit, z_bit = 1, 2, 4, 8


def thirds(columns):
    lanes = columns // 128
    first = (lanes + 2) // 3 * 128
    second = first + (lanes + 1) // 3 * 128
    return (0, first), (first, second), (second, columns)


def gather(own):
    near_x, near_y, near_z = swap(own, x_bit), swap(own, y_bit), swap(own, z_bit)
    xy, yz, zx = swap(near_x, y_bit), swap(near_y, z_bit), swap(near_z, x_bit)
    (a0, a1), (b0, b1), (c0, c1) = thirds(own.shape[1])
    far = jnp.concatenate(
        [swap(xy[:, a0:a1], z_bit), swap(yz[:, b0:b1], x_bit), swap(zx[:, c0:c1], y_bit)], axis=1
    )
    return jnp.concatenate([own, near_x, near_y, near_z, xy, yz, zx, far], axis=0)


def added(left, right):
    return (left.astype(jnp.float32) + right.astype(jnp.float32)).astype(jnp.bfloat16)


def scatter_sum(parts):
    rows = parts.shape[0] // 8
    own, near_x, near_y, near_z, xy, yz, zx, far = [
        parts[k * rows : (k + 1) * rows] for k in range(8)
    ]
    (a0, a1), (b0, b1), (c0, c1) = thirds(parts.shape[1])
    far_a, far_b, far_c = (
        swap(far[:, a0:a1], z_bit),
        swap(far[:, b0:b1], x_bit),
        swap(far[:, c0:c1], y_bit),
    )
    xy = jnp.concatenate([added(xy[:, a0:a1], far_a), xy[:, a1:]], axis=1)
    yz = jnp.concatenate([yz[:, :b0], added(yz[:, b0:b1], far_b), yz[:, b1:]], axis=1)
    zx = jnp.concatenate([zx[:, :c0], added(zx[:, c0:c1], far_c)], axis=1)
    near_x = added(near_x, swap(xy, y_bit))
    near_y = added(near_y, swap(yz, z_bit))
    near_z = added(near_z, swap(zx, x_bit))
    total = own.astype(jnp.float32) + swap(near_x, x_bit).astype(jnp.float32)
    total = total + swap(near_y, y_bit).astype(jnp.float32)
    total = total + swap(near_z, z_bit).astype(jnp.float32)
    return total.astype(jnp.bfloat16)


def shards(tokens, attn_partials, expert_ids, gate, w_in, w_out):
    tok_rows, width = tokens.shape
    n_expert = lax.axis_size("expert")
    experts = n_expert // SHARDS
    capacity = 5 * tok_rows // (8 * experts)
    first = capacity // 8 * 8
    rest = experts * capacity - first
    units = w_in.shape[1]
    scale_in = width ** (-0.5)
    scale_out = FF ** (-0.5)

    def shifted(rows, hops):
        pairs = [(i, (i + SHARDS * hops) % n_expert) for i in range(n_expert)]
        return lax.ppermute(rows, "expert", pairs)

    my_expert = lax.axis_index("expert") // SHARDS
    relative = lax.rem(expert_ids - my_expert + experts, experts)
    expert_range = jnp.arange(experts, dtype=jnp.int32)
    member = (relative[:, None] == expert_range[None, :]).astype(jnp.int32)
    slot_rank = jnp.sum(member * (jnp.cumsum(member, axis=0) - 1), axis=1)
    across = (relative - 1) * capacity + slot_rank
    late = (experts - 1) * capacity + slot_rank - first

    def one_hot(rows, index, chosen):
        index = jnp.where(chosen & (slot_rank < capacity), index, -1)
        return (jnp.arange(rows, dtype=jnp.int32)[:, None] == index[None, :]).astype(jnp.bfloat16)

    picks = [
        one_hot(first, slot_rank, (relative == 0) & (slot_rank < first)),
        one_hot(rest, late, (relative == 0) & (slot_rank >= first)),
    ] + [one_hot(rest, across, relative == s) for s in range(1, experts)]

    gated = summed_grads(attn_partials, gate)
    both = jnp.concatenate([tokens, gated], axis=1)
    packed = [
        jnp.dot(pick, both, preferred_element_type=jnp.float32).astype(jnp.bfloat16)
        for pick in picks
    ]
    early_rows = gather(packed[0])
    late_own = packed[1]
    for s in range(1, experts):
        late_own = late_own + shifted(packed[s + 1], s)
    late_rows = gather(late_own)

    def paired(weights):
        own = whole_weights(weights).T
        return jnp.concatenate([own, swap(own, core_bit)], axis=0)

    weights_in, weights_out = paired(w_in), paired(w_out)

    def worked(rows):
        expert_rows, grad_rows = rows[:, :width], rows[:, width:]
        pre_act = contract_cols(expert_rows, weights_in) * scale_in
        hidden = gelu_value(pre_act).astype(jnp.bfloat16)
        hidden_grad = contract_cols(grad_rows, weights_out) * scale_out
        pre_grad = (hidden_grad * gelu_slope(pre_act)).astype(jnp.bfloat16)
        partial_x = jnp.dot(pre_grad, weights_in, preferred_element_type=jnp.float32) * scale_in
        return expert_rows, grad_rows, hidden, pre_grad, partial_x.astype(jnp.bfloat16)

    early, later = worked(early_rows), worked(late_rows)
    early_sum, late_sum = scatter_sum(early[4]), scatter_sum(later[4])
    returned = [early_sum, late_sum] + [shifted(late_sum, -s) for s in range(1, experts)]
    token_grad = sum(contract_rows(pick, rows) for pick, rows in zip(picks, returned))

    def step(weights, left, right, scale):
        theirs = sum(contract_rows(e[left][:, units:], e[right]) for e in (early, later)) * scale
        theirs = swap(theirs.astype(jnp.bfloat16), core_bit)
        mine = sum(contract_rows(e[left][:, :units], e[right]) for e in (early, later)) * scale
        return stepped(weights, (mine + theirs.astype(jnp.float32)).T)

    new_w_in = step(w_in, 3, 0, scale_in)
    new_w_out = step(w_out, 2, 1, scale_out)
    return (token_grad.astype(jnp.bfloat16), new_w_in, new_w_out)


def solution(mesh):
    in_specs = (
        P(("expert", "dp"), None),
        P("dp", "expert", None),
        P(("expert", "dp")),
        P(("expert", "dp")),
        P("dp", "expert"),
        P("dp", "expert"),
    )
    out_specs = (P(("expert", "dp"), None), P("dp", "expert"), P("dp", "expert"))
    return jax.shard_map(shards, mesh=mesh, in_specs=in_specs, out_specs=out_specs, check_vma=False)
```

```python
import jax
import jax.numpy as jnp
from jax import lax
from jax.sharding import PartitionSpec as P

FF = 5120
SHARDS = 16


gelu_coef = 0.7978845608028654
cubic_coef = 0.044715
step_rate = 0.5


def gelu_value(inputs):
    return (
        0.5
        * inputs
        * (1.0 + jnp.tanh(gelu_coef * (inputs + cubic_coef * inputs * inputs * inputs)))
    )


def gelu_slope(inputs):
    tangent = jnp.tanh(gelu_coef * (inputs + cubic_coef * inputs * inputs * inputs))
    return 0.5 * (1.0 + tangent) + 0.5 * inputs * (1.0 - tangent * tangent) * gelu_coef * (
        1.0 + 3.0 * cubic_coef * inputs * inputs
    )


def contract_rows(left, right):
    return lax.dot_general(
        left, right, (((0,), (0,)), ((), ())), preferred_element_type=jnp.float32
    )


def contract_cols(left, right):
    return lax.dot_general(
        left, right, (((1,), (1,)), ((), ())), preferred_element_type=jnp.float32
    )


def summed_grads(attn_partials, gate):
    if lax.axis_size("dp") == 1:
        out_grad = attn_partials[0].astype(jnp.float32)
    else:
        out_grad = lax.psum_scatter(
            attn_partials[0], "dp", scatter_dimension=0, tiled=True
        ).astype(jnp.float32)
    return (gate[:, None] * out_grad).astype(jnp.bfloat16)


def whole_weights(shard):
    if lax.axis_size("dp") == 1:
        return shard.astype(jnp.bfloat16)
    return lax.all_gather(shard.astype(jnp.bfloat16), "dp", axis=0, tiled=True)


def stepped(weights, grads):
    if lax.axis_size("dp") > 1:
        grads = lax.psum_scatter(
            grads.astype(jnp.bfloat16), "dp", scatter_dimension=0, tiled=True
        ).astype(jnp.float32)
    return weights - step_rate * grads


def swap(rows, mask):
    n_expert = lax.axis_size("expert")
    return lax.ppermute(rows, "expert", [(i, i ^ mask) for i in range(n_expert)])


core_bit = 1


def same_core():
    n_expert = lax.axis_size("expert")
    return [
        [e * SHARDS + k for k in range(c, SHARDS, 2)]
        for e in range(n_expert // SHARDS)
        for c in range(2)
    ]


def exchange(blocks):
    return lax.all_to_all(
        blocks, "expert", split_axis=0, concat_axis=0, tiled=True, axis_index_groups=same_core()
    )


def gather(own):
    rows, columns = own.shape
    blocks = exchange(jnp.broadcast_to(own[None], (SHARDS // 2, rows, columns)))
    return blocks.reshape(SHARDS // 2 * rows, columns)


def scatter_sum(parts):
    blocks = exchange(parts.reshape(SHARDS // 2, -1, parts.shape[1]))
    return jnp.sum(blocks.astype(jnp.float32), axis=0).astype(jnp.bfloat16)


def shards(tokens, attn_partials, expert_ids, gate, w_in, w_out):
    tok_rows, width = tokens.shape
    n_expert = lax.axis_size("expert")
    experts = n_expert // SHARDS
    capacity = 5 * tok_rows // (8 * experts)
    first = capacity // 8 * 8
    rest = experts * capacity - first
    units = w_in.shape[1]
    scale_in = width ** (-0.5)
    scale_out = FF ** (-0.5)

    def shifted(rows, hops):
        pairs = [(i, (i + SHARDS * hops) % n_expert) for i in range(n_expert)]
        return lax.ppermute(rows, "expert", pairs)

    my_expert = lax.axis_index("expert") // SHARDS
    relative = lax.rem(expert_ids - my_expert + experts, experts)
    expert_range = jnp.arange(experts, dtype=jnp.int32)
    member = (relative[:, None] == expert_range[None, :]).astype(jnp.int32)
    slot_rank = jnp.sum(member * (jnp.cumsum(member, axis=0) - 1), axis=1)
    across = (relative - 1) * capacity + slot_rank
    late = (experts - 1) * capacity + slot_rank - first

    def one_hot(rows, index, chosen):
        index = jnp.where(chosen & (slot_rank < capacity), index, -1)
        return (jnp.arange(rows, dtype=jnp.int32)[:, None] == index[None, :]).astype(jnp.bfloat16)

    picks = [
        one_hot(first, slot_rank, (relative == 0) & (slot_rank < first)),
        one_hot(rest, late, (relative == 0) & (slot_rank >= first)),
    ] + [one_hot(rest, across, relative == s) for s in range(1, experts)]

    gated = summed_grads(attn_partials, gate)
    both = jnp.concatenate([tokens, gated], axis=1)
    packed = [
        jnp.dot(pick, both, preferred_element_type=jnp.float32).astype(jnp.bfloat16)
        for pick in picks
    ]
    early_rows = gather(packed[0])
    late_own = packed[1]
    for s in range(1, experts):
        late_own = late_own + shifted(packed[s + 1], s)
    late_rows = gather(late_own)

    def paired(weights):
        own = whole_weights(weights).T
        return jnp.concatenate([own, swap(own, core_bit)], axis=0)

    weights_in, weights_out = paired(w_in), paired(w_out)

    def worked(rows):
        expert_rows, grad_rows = rows[:, :width], rows[:, width:]
        pre_act = contract_cols(expert_rows, weights_in) * scale_in
        hidden = gelu_value(pre_act).astype(jnp.bfloat16)
        hidden_grad = contract_cols(grad_rows, weights_out) * scale_out
        pre_grad = (hidden_grad * gelu_slope(pre_act)).astype(jnp.bfloat16)
        partial_x = jnp.dot(pre_grad, weights_in, preferred_element_type=jnp.float32) * scale_in
        return expert_rows, grad_rows, hidden, pre_grad, partial_x.astype(jnp.bfloat16)

    early, later = worked(early_rows), worked(late_rows)
    early_sum, late_sum = scatter_sum(early[4]), scatter_sum(later[4])
    returned = [early_sum, late_sum] + [shifted(late_sum, -s) for s in range(1, experts)]
    token_grad = sum(contract_rows(pick, rows) for pick, rows in zip(picks, returned))

    def step(weights, left, right, scale):
        theirs = sum(contract_rows(e[left][:, units:], e[right]) for e in (early, later)) * scale
        theirs = swap(theirs.astype(jnp.bfloat16), core_bit)
        mine = sum(contract_rows(e[left][:, :units], e[right]) for e in (early, later)) * scale
        return stepped(weights, (mine + theirs.astype(jnp.float32)).T)

    new_w_in = step(w_in, 3, 0, scale_in)
    new_w_out = step(w_out, 2, 1, scale_out)
    return (token_grad.astype(jnp.bfloat16), new_w_in, new_w_out)


def solution(mesh):
    in_specs = (
        P(("expert", "dp"), None),
        P("dp", "expert", None),
        P(("expert", "dp")),
        P(("expert", "dp")),
        P("dp", "expert"),
        P("dp", "expert"),
    )
    out_specs = (P(("expert", "dp"), None), P("dp", "expert"), P("dp", "expert"))
    return jax.shard_map(shards, mesh=mesh, in_specs=in_specs, out_specs=out_specs, check_vma=False)
```

```python
import jax
import jax.numpy as jnp
from jax import lax
from jax.sharding import PartitionSpec as P

FF = 5120
SHARDS = 16


gelu_coef = 0.7978845608028654
cubic_coef = 0.044715
step_rate = 0.5


def gelu_value(inputs):
    return (
        0.5
        * inputs
        * (1.0 + jnp.tanh(gelu_coef * (inputs + cubic_coef * inputs * inputs * inputs)))
    )


def gelu_slope(inputs):
    tangent = jnp.tanh(gelu_coef * (inputs + cubic_coef * inputs * inputs * inputs))
    return 0.5 * (1.0 + tangent) + 0.5 * inputs * (1.0 - tangent * tangent) * gelu_coef * (
        1.0 + 3.0 * cubic_coef * inputs * inputs
    )


def contract_rows(left, right):
    return lax.dot_general(
        left, right, (((0,), (0,)), ((), ())), preferred_element_type=jnp.float32
    )


def contract_cols(left, right):
    return lax.dot_general(
        left, right, (((1,), (1,)), ((), ())), preferred_element_type=jnp.float32
    )


def summed_grads(attn_partials, gate):
    if lax.axis_size("dp") == 1:
        out_grad = attn_partials[0].astype(jnp.float32)
    else:
        out_grad = lax.psum_scatter(
            attn_partials[0], "dp", scatter_dimension=0, tiled=True
        ).astype(jnp.float32)
    return (gate[:, None] * out_grad).astype(jnp.bfloat16)


def whole_weights(shard):
    if lax.axis_size("dp") == 1:
        return shard.astype(jnp.bfloat16)
    return lax.all_gather(shard.astype(jnp.bfloat16), "dp", axis=0, tiled=True)


def stepped(weights, grads):
    if lax.axis_size("dp") > 1:
        grads = lax.psum_scatter(
            grads.astype(jnp.bfloat16), "dp", scatter_dimension=0, tiled=True
        ).astype(jnp.float32)
    return weights - step_rate * grads


def swap(rows, mask):
    n_expert = lax.axis_size("expert")
    return lax.ppermute(rows, "expert", [(i, i ^ mask) for i in range(n_expert)])


core_bit, x_bit, y_bit, z_bit = 1, 2, 4, 8


def after(values, *others):
    return lax.optimization_barrier((values, others))[0]


def first_hop(own):
    return swap(own, x_bit), swap(own, y_bit), swap(own, z_bit)


def second_hop(near_x, near_y, near_z):
    return (
        swap(near_x, y_bit),
        swap(near_y, z_bit),
        swap(near_z, x_bit),
        swap(near_z, x_bit | y_bit),
    )


def second_hop_back(parts):
    rows = parts.shape[0] // 8
    blocks = [parts[k * rows : (k + 1) * rows] for k in range(8)]
    far = (
        swap(blocks[4], y_bit),
        swap(blocks[5], z_bit),
        swap(blocks[6], x_bit),
        swap(blocks[7], x_bit | y_bit),
    )
    return blocks[:4], far


def total(*terms):
    return sum(term.astype(jnp.float32) for term in terms).astype(jnp.bfloat16)


def first_hop_back(near, far):
    near_x = swap(total(near[1], far[0]), x_bit)
    near_y = swap(total(near[2], far[1]), y_bit)
    near_z = swap(total(near[3], far[2], far[3]), z_bit)
    return total(near[0], near_x, near_y, near_z)


def shards(tokens, attn_partials, expert_ids, gate, w_in, w_out):
    tok_rows, width = tokens.shape
    n_expert = lax.axis_size("expert")
    experts = n_expert // SHARDS
    capacity = 5 * tok_rows // (8 * experts)
    first = capacity // 8 * 8
    rest = experts * capacity - first
    units = w_in.shape[1]
    scale_in = width ** (-0.5)
    scale_out = FF ** (-0.5)

    def shifted(rows, hops):
        pairs = [(i, (i + SHARDS * hops) % n_expert) for i in range(n_expert)]
        return lax.ppermute(rows, "expert", pairs)

    my_expert = lax.axis_index("expert") // SHARDS
    relative = lax.rem(expert_ids - my_expert + experts, experts)
    expert_range = jnp.arange(experts, dtype=jnp.int32)
    member = (relative[:, None] == expert_range[None, :]).astype(jnp.int32)
    slot_rank = jnp.sum(member * (jnp.cumsum(member, axis=0) - 1), axis=1)
    across = (relative - 1) * capacity + slot_rank
    late = (experts - 1) * capacity + slot_rank - first

    def one_hot(rows, index, chosen):
        index = jnp.where(chosen & (slot_rank < capacity), index, -1)
        return (jnp.arange(rows, dtype=jnp.int32)[:, None] == index[None, :]).astype(jnp.bfloat16)

    picks = [
        one_hot(first, slot_rank, (relative == 0) & (slot_rank < first)),
        one_hot(rest, late, (relative == 0) & (slot_rank >= first)),
    ] + [one_hot(rest, across, relative == s) for s in range(1, experts)]

    gated = summed_grads(attn_partials, gate)
    both = jnp.concatenate([tokens, gated], axis=1)
    packed = [
        jnp.dot(pick, both, preferred_element_type=jnp.float32).astype(jnp.bfloat16)
        for pick in picks
    ]

    def paired(weights):
        own = whole_weights(weights).T
        return jnp.concatenate([own, swap(own, core_bit)], axis=0)

    def activated(rows):
        expert_rows, grad_rows = rows[:, :width], rows[:, width:]
        pre_act = contract_cols(expert_rows, weights_in) * scale_in
        hidden = gelu_value(pre_act).astype(jnp.bfloat16)
        hidden_grad = contract_cols(grad_rows, weights_out) * scale_out
        pre_grad = (hidden_grad * gelu_slope(pre_act)).astype(jnp.bfloat16)
        return expert_rows, grad_rows, hidden, pre_grad

    def input_parts(pre_grad):
        parts = jnp.dot(pre_grad, weights_in, preferred_element_type=jnp.float32) * scale_in
        return parts.astype(jnp.bfloat16)

    early_near = first_hop(packed[0])
    weights_in, weights_out = paired(w_in), paired(w_out)
    late_own = packed[1]
    for s in range(1, experts):
        late_own = late_own + shifted(packed[s + 1], s)
    early_far = second_hop(*early_near)
    late_own = after(late_own, early_near)
    late_near = first_hop(late_own)
    early_rows = jnp.concatenate([packed[0], *early_near, *early_far], axis=0)
    early = activated(early_rows)
    late_near = after(late_near, early[3])
    late_far = second_hop(*late_near)
    early_parts = input_parts(early[3])
    late_far = after(late_far, early_parts)
    late_rows = jnp.concatenate([late_own, *late_near, *late_far], axis=0)
    later = activated(late_rows)
    late_parts = input_parts(later[3])
    early_back = second_hop_back(early_parts)
    late_back = second_hop_back(late_parts)
    early_sum = first_hop_back(*early_back)
    late_sum = first_hop_back(*late_back)
    returned = [early_sum, late_sum] + [shifted(late_sum, -s) for s in range(1, experts)]

    def step(weights, left, right, scale):
        theirs = sum(contract_rows(e[left][:, units:], e[right]) for e in (early, later)) * scale
        theirs = swap(theirs.astype(jnp.bfloat16), core_bit)
        mine = sum(contract_rows(e[left][:, :units], e[right]) for e in (early, later)) * scale
        return stepped(weights, (mine + theirs.astype(jnp.float32)).T)

    new_w_in = step(w_in, 3, 0, scale_in)
    new_w_out = step(w_out, 2, 1, scale_out)
    token_grad = sum(contract_rows(pick, rows) for pick, rows in zip(picks, returned))
    return (token_grad.astype(jnp.bfloat16), new_w_in, new_w_out)


def solution(mesh):
    in_specs = (
        P(("expert", "dp"), None),
        P("dp", "expert", None),
        P(("expert", "dp")),
        P(("expert", "dp")),
        P("dp", "expert"),
        P("dp", "expert"),
    )
    out_specs = (P(("expert", "dp"), None), P("dp", "expert"), P("dp", "expert"))
    return jax.shard_map(shards, mesh=mesh, in_specs=in_specs, out_specs=out_specs, check_vma=False)
```

```python
import jax
import jax.numpy as jnp
from jax import lax
from jax.experimental import pallas as pl
from jax.experimental.pallas import tpu as pltpu
from jax.sharding import PartitionSpec as P

FF = 5120
SHARDS = 16


gelu_coef = 0.7978845608028654
cubic_coef = 0.044715
step_rate = 0.5


def gelu_value(inputs):
    return (
        0.5
        * inputs
        * (1.0 + jnp.tanh(gelu_coef * (inputs + cubic_coef * inputs * inputs * inputs)))
    )


def gelu_slope(inputs):
    tangent = jnp.tanh(gelu_coef * (inputs + cubic_coef * inputs * inputs * inputs))
    return 0.5 * (1.0 + tangent) + 0.5 * inputs * (1.0 - tangent * tangent) * gelu_coef * (
        1.0 + 3.0 * cubic_coef * inputs * inputs
    )


def contract_rows(left, right):
    return lax.dot_general(
        left, right, (((0,), (0,)), ((), ())), preferred_element_type=jnp.float32
    )


def contract_cols(left, right):
    return lax.dot_general(
        left, right, (((1,), (1,)), ((), ())), preferred_element_type=jnp.float32
    )


def summed_grads(attn_partials):
    if lax.axis_size("dp") == 1:
        return attn_partials[0]
    return lax.psum_scatter(attn_partials[0], "dp", scatter_dimension=0, tiled=True)


def pack_kernel(blocks, capacity, experts, n_in, *refs):
    ids_ref, gate_ref, tokens_ref, grads_ref = refs[:4]
    outs = refs[n_in:]
    n, width = tokens_ref.shape
    mine = (lax.axis_index("expert") // SHARDS).astype(jnp.float32)
    ids = ids_ref[...].astype(jnp.float32)
    relative = ids - mine
    relative = jnp.where(relative < 0.0, relative + experts, relative)
    down = lax.broadcasted_iota(jnp.int32, (n, n), 0)
    across = lax.broadcasted_iota(jnp.int32, (n, n), 1)
    ids_down = jnp.sum(jnp.where(down == across, ids, 0.0), axis=1, keepdims=True)
    gate_down = jnp.sum(jnp.where(down == across, gate_ref[...], 0.0), axis=1, keepdims=True)
    rivals = jnp.where((ids_down == ids) & (down < across), 1.0, 0.0)
    rank = jnp.sum(rivals, axis=0, keepdims=True)
    gated = (gate_down * grads_ref[...].astype(jnp.float32)).astype(jnp.bfloat16)
    for k, (expert, begin, end, row) in enumerate(blocks):
        rows_ref, pick_ref = outs[2 * k], outs[2 * k + 1]
        chosen = (relative == expert) & (rank >= begin) & (rank < end)
        slot = jnp.where(chosen, rank - begin + row, -1.0).astype(jnp.int32)
        slots = lax.broadcasted_iota(jnp.int32, pick_ref.shape, 0)
        pick = jnp.where(slots == slot, 1.0, 0.0).astype(jnp.bfloat16)
        pick_ref[...] = pick
        for half, source in enumerate((tokens_ref[...], gated)):
            rows_ref[:, half * width : (half + 1) * width] = jnp.dot(
                pick, source, preferred_element_type=jnp.float32
            ).astype(jnp.bfloat16)


def pack(blocks, rows, capacity, experts, ids, gate, tokens, grads, *awaited):
    n, width = tokens.shape
    shapes = []
    for count in rows:
        shapes.append(jax.ShapeDtypeStruct((count, 2 * width), jnp.bfloat16))
        shapes.append(jax.ShapeDtypeStruct((count, n), jnp.bfloat16))
    whole = pl.BlockSpec(memory_space=pltpu.VMEM)
    outs = pl.pallas_call(
        lambda *refs: pack_kernel(blocks, capacity, experts, 4 + len(awaited), *refs),
        out_shape=shapes,
        in_specs=[whole] * 4 + [pl.BlockSpec(memory_space=pl.ANY)] * len(awaited),
        out_specs=[whole] * len(shapes),
    )(ids.reshape(1, n), gate.reshape(1, n), tokens, grads, *awaited)
    return outs[::2], outs[1::2]


def whole_weights(shard):
    if lax.axis_size("dp") == 1:
        return shard.astype(jnp.bfloat16)
    return lax.all_gather(shard.astype(jnp.bfloat16), "dp", axis=0, tiled=True)


def stepped(weights, grads):
    if lax.axis_size("dp") > 1:
        grads = lax.psum_scatter(
            grads.astype(jnp.bfloat16), "dp", scatter_dimension=0, tiled=True
        ).astype(jnp.float32)
    return weights - step_rate * grads


def swap(rows, mask):
    n_expert = lax.axis_size("expert")
    return lax.ppermute(rows, "expert", [(i, i ^ mask) for i in range(n_expert)])


core_bit, x_bit, y_bit, z_bit = 1, 2, 4, 8
direct_masks = (2, 4, 8, 6, 12, 10, 14)


def after(values, *others):
    return lax.optimization_barrier((values, others))[0]


def first_hop(own):
    return swap(own, x_bit), swap(own, y_bit), swap(own, z_bit)


def second_hop(near_x, near_y, near_z):
    return (
        swap(near_x, y_bit),
        swap(near_y, z_bit),
        swap(near_z, x_bit),
        swap(near_z, x_bit | y_bit),
    )


def second_hop_back(parts):
    rows = parts.shape[0] // 8
    blocks = [parts[k * rows : (k + 1) * rows] for k in range(8)]
    far = (
        swap(blocks[4], y_bit),
        swap(blocks[5], z_bit),
        swap(blocks[6], x_bit),
        swap(blocks[7], x_bit | y_bit),
    )
    return blocks[:4], far


def total(*terms):
    return sum(term.astype(jnp.float32) for term in terms).astype(jnp.bfloat16)


def first_hop_back(near, far):
    near_x = swap(total(near[1], far[0]), x_bit)
    near_y = swap(total(near[2], far[1]), y_bit)
    near_z = swap(total(near[3], far[2], far[3]), z_bit)
    return total(near[0], near_x, near_y, near_z)


def shards(tokens, attn_partials, expert_ids, gate, w_in, w_out):
    tok_rows, width = tokens.shape
    n_expert = lax.axis_size("expert")
    experts = n_expert // SHARDS
    capacity = 5 * tok_rows // (8 * experts)
    first = capacity // 8 * 8
    rest = experts * capacity - first
    units = w_in.shape[1]
    scale_in = width ** (-0.5)
    scale_out = FF ** (-0.5)

    def shifted(rows, hops):
        pairs = [(i, (i + SHARDS * hops) % n_expert) for i in range(n_expert)]
        return lax.ppermute(rows, "expert", pairs)

    offset = (experts - 1) * capacity - first
    own_blocks = [(0, 0, first, 0), (0, first, capacity, offset + first)]
    cross_blocks = [(s, 0, capacity, (s - 1) * capacity) for s in range(1, experts)]
    grads = summed_grads(attn_partials)
    sent, sent_picks = pack(
        cross_blocks, [rest] * len(cross_blocks), capacity, experts, expert_ids, gate, tokens, grads
    )
    (early_own, late_own), own_picks = pack(
        own_blocks, [first, rest], capacity, experts, expert_ids, gate, tokens, grads, *sent
    )

    def paired(weights):
        own = whole_weights(weights).T
        return jnp.concatenate([own, swap(own, core_bit)], axis=0)

    def activated(rows):
        expert_rows, grad_rows = rows[:, :width], rows[:, width:]
        pre_act = contract_cols(expert_rows, weights_in) * scale_in
        hidden = gelu_value(pre_act).astype(jnp.bfloat16)
        hidden_grad = contract_cols(grad_rows, weights_out) * scale_out
        pre_grad = (hidden_grad * gelu_slope(pre_act)).astype(jnp.bfloat16)
        return expert_rows, grad_rows, hidden, pre_grad

    def input_parts(pre_grad):
        parts = jnp.dot(pre_grad, weights_in, preferred_element_type=jnp.float32) * scale_in
        return parts.astype(jnp.bfloat16)

    for s in range(1, experts):
        late_own = late_own + shifted(sent[s - 1], s)
    early_blocks = [early_own] + [swap(early_own, mask) for mask in direct_masks]
    weights_in, weights_out = paired(w_in), paired(w_out)
    late_near = first_hop(late_own)
    early_rows = after(jnp.concatenate(early_blocks, axis=0), late_own)
    early = activated(early_rows)
    late_near = after(late_near, early[3])
    late_far = second_hop(*late_near)
    early_parts = input_parts(early[3])
    late_far = after(late_far, early_parts)
    late_rows = jnp.concatenate([late_own, *late_near, *late_far], axis=0)
    later = activated(late_rows)
    late_parts = input_parts(later[3])
    early_back = [early_parts[:first]] + [
        swap(early_parts[k * first : (k + 1) * first], mask)
        for k, mask in enumerate(direct_masks, 1)
    ]
    late_back = second_hop_back(late_parts)
    early_sum = total(*early_back)
    late_sum = after(first_hop_back(*late_back), early_sum)
    returned = [early_sum, late_sum] + [shifted(late_sum, -s) for s in range(1, experts)]

    def step(weights, left, right, scale):
        theirs = sum(contract_rows(e[left][:, units:], e[right]) for e in (early, later)) * scale
        theirs = swap(theirs.astype(jnp.bfloat16), core_bit)
        mine = sum(contract_rows(e[left][:, :units], e[right]) for e in (early, later)) * scale
        return stepped(weights, (mine + theirs.astype(jnp.float32)).T)

    new_w_in = step(w_in, 3, 0, scale_in)
    new_w_out = step(w_out, 2, 1, scale_out)
    returned = after(returned, new_w_in, new_w_out)
    picks = [*own_picks, *sent_picks]
    token_grad = sum(contract_rows(pick, rows) for pick, rows in zip(picks, returned))
    return (token_grad.astype(jnp.bfloat16), new_w_in, new_w_out)


def solution(mesh):
    in_specs = (
        P(("expert", "dp"), None),
        P("dp", "expert", None),
        P(("expert", "dp")),
        P(("expert", "dp")),
        P("dp", "expert"),
        P("dp", "expert"),
    )
    out_specs = (P(("expert", "dp"), None), P("dp", "expert"), P("dp", "expert"))
    return jax.shard_map(shards, mesh=mesh, in_specs=in_specs, out_specs=out_specs, check_vma=False)
```

```python
import jax
import jax.numpy as jnp
from jax import lax
from jax.experimental import pallas as pl
from jax.experimental.pallas import tpu as pltpu
from jax.sharding import PartitionSpec as P

FF = 5120
SHARDS = 16


gelu_coef = 0.7978845608028654
cubic_coef = 0.044715
step_rate = 0.5


def gelu_value(inputs):
    return (
        0.5
        * inputs
        * (1.0 + jnp.tanh(gelu_coef * (inputs + cubic_coef * inputs * inputs * inputs)))
    )


def gelu_slope(inputs):
    tangent = jnp.tanh(gelu_coef * (inputs + cubic_coef * inputs * inputs * inputs))
    return 0.5 * (1.0 + tangent) + 0.5 * inputs * (1.0 - tangent * tangent) * gelu_coef * (
        1.0 + 3.0 * cubic_coef * inputs * inputs
    )


def contract_rows(left, right):
    return lax.dot_general(
        left, right, (((0,), (0,)), ((), ())), preferred_element_type=jnp.float32
    )


def contract_cols(left, right):
    return lax.dot_general(
        left, right, (((1,), (1,)), ((), ())), preferred_element_type=jnp.float32
    )


def summed_grads(attn_partials):
    if lax.axis_size("dp") == 1:
        return attn_partials[0]
    return lax.psum_scatter(attn_partials[0], "dp", scatter_dimension=0, tiled=True)


def pack_kernel(blocks, experts, *refs):
    ids_ref, gate_ref, tokens_ref, grads_ref, *outs = refs
    n, width = tokens_ref.shape
    mine = (lax.axis_index("expert") // SHARDS).astype(jnp.float32)
    ids = ids_ref[...].astype(jnp.float32)
    relative = ids - mine
    relative = jnp.where(relative < 0.0, relative + experts, relative)
    down = lax.broadcasted_iota(jnp.int32, (n, n), 0)
    across = lax.broadcasted_iota(jnp.int32, (n, n), 1)
    ids_down = jnp.sum(jnp.where(down == across, ids, 0.0), axis=1, keepdims=True)
    gate_down = jnp.sum(jnp.where(down == across, gate_ref[...], 0.0), axis=1, keepdims=True)
    rivals = jnp.where((ids_down == ids) & (down < across), 1.0, 0.0)
    rank = jnp.sum(rivals, axis=0, keepdims=True)
    gated = (gate_down * grads_ref[...].astype(jnp.float32)).astype(jnp.bfloat16)
    for k, (expert, begin, end, row) in enumerate(blocks):
        rows_ref, pick_ref = outs[2 * k], outs[2 * k + 1]
        chosen = (relative == expert) & (rank >= begin) & (rank < end)
        slot = jnp.where(chosen, rank - begin + row, -1.0).astype(jnp.int32)
        slots = lax.broadcasted_iota(jnp.int32, pick_ref.shape, 0)
        pick = jnp.where(slots == slot, 1.0, 0.0).astype(jnp.bfloat16)
        pick_ref[...] = pick
        for half, source in enumerate((tokens_ref[...], gated)):
            rows_ref[:, half * width : (half + 1) * width] = jnp.dot(
                pick, source, preferred_element_type=jnp.float32
            ).astype(jnp.bfloat16)


def pack(blocks, rows, experts, ids, gate, tokens, grads):
    n, width = tokens.shape
    shapes = []
    for count in rows:
        shapes.append(jax.ShapeDtypeStruct((count, 2 * width), jnp.bfloat16))
        shapes.append(jax.ShapeDtypeStruct((count, n), jnp.bfloat16))
    whole = pl.BlockSpec(memory_space=pltpu.VMEM)
    outs = pl.pallas_call(
        lambda *refs: pack_kernel(blocks, experts, *refs),
        out_shape=shapes,
        in_specs=[whole] * 4,
        out_specs=[whole] * len(shapes),
    )(ids.reshape(1, n), gate.reshape(1, n), tokens, grads)
    return outs[::2], outs[1::2]


def whole_weights(shard):
    if lax.axis_size("dp") == 1:
        return shard.astype(jnp.bfloat16)
    return lax.all_gather(shard.astype(jnp.bfloat16), "dp", axis=0, tiled=True)


def stepped(weights, grads):
    if lax.axis_size("dp") > 1:
        grads = lax.psum_scatter(
            grads.astype(jnp.bfloat16), "dp", scatter_dimension=0, tiled=True
        ).astype(jnp.float32)
    return weights - step_rate * grads


def swap(rows, mask):
    n_expert = lax.axis_size("expert")
    return lax.ppermute(rows, "expert", [(i, i ^ mask) for i in range(n_expert)])


core_bit, x_bit, y_bit, z_bit = 1, 2, 4, 8
far_mask = x_bit | y_bit | z_bit


def after(values, *others):
    return lax.optimization_barrier((values, others))[0]


def first_hop(own):
    return swap(own, x_bit), swap(own, y_bit), swap(own, z_bit)


second_masks = (y_bit, z_bit, x_bit, x_bit | y_bit)


def total(*terms):
    return sum(term.astype(jnp.float32) for term in terms).astype(jnp.bfloat16)


def split_rows(array, rows):
    return [array[k : k + rows] for k in range(0, array.shape[0], rows)]


def near_sums(near, far):
    return (
        total(near[1], far[0]),
        total(near[2], far[1]),
        total(near[3], far[2], far[3]),
    )


def shards(tokens, attn_partials, expert_ids, gate, w_in, w_out):
    tok_rows, width = tokens.shape
    n_expert = lax.axis_size("expert")
    experts = n_expert // SHARDS
    capacity = 5 * tok_rows // (8 * experts)
    first = capacity // 8 * 8
    rest = experts * capacity - first
    units = w_in.shape[1]
    scale_in = width ** (-0.5)
    scale_out = FF ** (-0.5)

    def shifted(rows, hops):
        pairs = [(i, (i + SHARDS * hops) % n_expert) for i in range(n_expert)]
        return lax.ppermute(rows, "expert", pairs)

    offset = (experts - 1) * capacity - first
    own_blocks = [(0, 0, first, 0), (0, first, capacity, offset + first)]
    cross_blocks = [(s, 0, capacity, (s - 1) * capacity) for s in range(1, experts)]
    grads = summed_grads(attn_partials)
    (early_own, late_own, *sent), picks = pack(
        own_blocks + cross_blocks,
        [first] + [rest] * experts,
        experts,
        expert_ids,
        gate,
        tokens,
        grads,
    )

    def activated(rows):
        expert_rows, grad_rows = rows[:, :width], rows[:, width:]
        pre_act = contract_cols(expert_rows, weights_in) * scale_in
        hidden = gelu_value(pre_act).astype(jnp.bfloat16)
        hidden_grad = contract_cols(grad_rows, weights_out) * scale_out
        pre_grad = (hidden_grad * gelu_slope(pre_act)).astype(jnp.bfloat16)
        return expert_rows, grad_rows, hidden, pre_grad

    def input_parts(pre_grad):
        parts = jnp.dot(pre_grad, weights_in, preferred_element_type=jnp.float32) * scale_in
        return parts.astype(jnp.bfloat16)

    for s in range(1, experts):
        late_own = late_own + shifted(sent[s - 1], s)
    early_near = first_hop(early_own)
    early_far = swap(early_own, far_mask)
    early_near, early_far = after((early_near, early_far), late_own)
    arrived = [
        swap(jnp.concatenate([rows, late_own], axis=0), mask)
        for rows, mask in zip(
            (early_near[2], early_near[0], early_near[1]), (x_bit, y_bit, z_bit)
        )
    ]
    early_zx, early_xy, early_yz = [rows[:first] for rows in arrived]
    late_near = [rows[first:] for rows in arrived]
    early_rows = [early_own, *early_near, early_xy, early_yz, early_zx, early_far]

    own_weights = jnp.concatenate([whole_weights(w_in).T, whole_weights(w_out).T], axis=0)
    their_weights = swap(after(own_weights, late_own), core_bit)
    weights_in, weights_out = [
        jnp.concatenate([own_weights[part], their_weights[part]], axis=0)
        for part in (slice(0, units), slice(units, 2 * units))
    ]
    near_x, near_y, near_z = late_near
    late_far = [
        swap(rows, mask) for rows, mask in zip((near_x, near_y, near_z, near_z), second_masks)
    ]
    early = activated(jnp.concatenate(early_rows, axis=0))
    early_parts = input_parts(early[3])
    late_far = after(late_far, early_parts)
    later = activated(jnp.concatenate([late_own, *late_near, *late_far], axis=0))
    late_parts = input_parts(later[3])
    parts = [
        jnp.concatenate(pair, axis=0)
        for pair in zip(split_rows(early_parts, first), split_rows(late_parts, rest))
    ]
    back_far = [swap(rows, mask) for rows, mask in zip(parts[4:], second_masks)]
    back_near = [
        swap(rows, mask)
        for rows, mask in zip(near_sums(parts, back_far), (x_bit, y_bit, z_bit))
    ]
    sums = total(parts[0], *back_near)
    early_sum, late_sum = sums[:first], sums[first:]
    crossed = [shifted(late_sum, -s) for s in range(1, experts)]

    def gradient(left, right, part, scale):
        return sum(contract_rows(e[left][:, part], e[right]) for e in (early, later)) * scale

    mine, theirs = slice(0, units), slice(units, 2 * units)
    shared = jnp.concatenate(
        [
            gradient(3, 0, theirs, scale_in).astype(jnp.bfloat16),
            gradient(2, 1, theirs, scale_out).astype(jnp.bfloat16),
        ],
        axis=0,
    )
    shared = swap(shared, core_bit).astype(jnp.float32)
    new_w_in = stepped(w_in, (gradient(3, 0, mine, scale_in) + shared[mine]).T)
    new_w_out = stepped(w_out, (gradient(2, 1, mine, scale_out) + shared[theirs]).T)
    crossed = after(crossed, new_w_in, new_w_out)
    returned = [early_sum, late_sum, *crossed]
    token_grad = sum(contract_rows(pick, rows) for pick, rows in zip(picks, returned))
    return (token_grad.astype(jnp.bfloat16), new_w_in, new_w_out)


def solution(mesh):
    in_specs = (
        P(("expert", "dp"), None),
        P("dp", "expert", None),
        P(("expert", "dp")),
        P(("expert", "dp")),
        P("dp", "expert"),
        P("dp", "expert"),
    )
    out_specs = (P(("expert", "dp"), None), P("dp", "expert"), P("dp", "expert"))
    return jax.shard_map(shards, mesh=mesh, in_specs=in_specs, out_specs=out_specs, check_vma=False)
```

```python
import jax
import jax.numpy as jnp
from jax import lax
from jax.experimental import pallas as pl
from jax.experimental.pallas import tpu as pltpu
from jax.sharding import PartitionSpec as P

FF = 5120
SHARDS = 16


gelu_coef = 0.7978845608028654
cubic_coef = 0.044715
step_rate = 0.5


def gelu_value(inputs):
    return (
        0.5
        * inputs
        * (1.0 + jnp.tanh(gelu_coef * (inputs + cubic_coef * inputs * inputs * inputs)))
    )


def gelu_slope(inputs):
    tangent = jnp.tanh(gelu_coef * (inputs + cubic_coef * inputs * inputs * inputs))
    return 0.5 * (1.0 + tangent) + 0.5 * inputs * (1.0 - tangent * tangent) * gelu_coef * (
        1.0 + 3.0 * cubic_coef * inputs * inputs
    )


def contract_rows(left, right):
    return lax.dot_general(
        left, right, (((0,), (0,)), ((), ())), preferred_element_type=jnp.float32
    )


def contract_cols(left, right):
    return lax.dot_general(
        left, right, (((1,), (1,)), ((), ())), preferred_element_type=jnp.float32
    )


def summed_grads(attn_partials):
    if lax.axis_size("dp") == 1:
        return attn_partials[0]
    return lax.psum_scatter(attn_partials[0], "dp", scatter_dimension=0, tiled=True)


def pack_kernel(blocks, copies, experts, *refs):
    ids_ref, gate_ref, tokens_ref, grads_ref, *outs = refs
    n, width = tokens_ref.shape
    mine = (lax.axis_index("expert") // SHARDS).astype(jnp.float32)
    ids = ids_ref[...].astype(jnp.float32)
    relative = ids - mine
    relative = jnp.where(relative < 0.0, relative + experts, relative)
    down = lax.broadcasted_iota(jnp.int32, (n, n), 0)
    across = lax.broadcasted_iota(jnp.int32, (n, n), 1)
    ids_down = jnp.sum(jnp.where(down == across, ids, 0.0), axis=1, keepdims=True)
    gate_down = jnp.sum(jnp.where(down == across, gate_ref[...], 0.0), axis=1, keepdims=True)
    rivals = jnp.where((ids_down == ids) & (down < across), 1.0, 0.0)
    rank = jnp.sum(rivals, axis=0, keepdims=True)
    gated = (gate_down * grads_ref[...].astype(jnp.float32)).astype(jnp.bfloat16)
    for k, (expert, begin, end, row) in enumerate(blocks):
        rows_ref, pick_ref = outs[copies + 2 * k], outs[copies + 2 * k + 1]
        chosen = (relative == expert) & (rank >= begin) & (rank < end)
        slot = jnp.where(chosen, rank - begin + row, -1.0).astype(jnp.int32)
        slots = lax.broadcasted_iota(jnp.int32, pick_ref.shape, 0)
        pick = jnp.where(slots == slot, 1.0, 0.0).astype(jnp.bfloat16)
        pick_ref[...] = pick
        for half, source in enumerate((tokens_ref[...], gated)):
            rows_ref[:, half * width : (half + 1) * width] = jnp.dot(
                pick, source, preferred_element_type=jnp.float32
            ).astype(jnp.bfloat16)
    for copy_ref in outs[:copies]:
        copy_ref[...] = outs[copies][...]


def pack(blocks, rows, copies, experts, ids, gate, tokens, grads):
    n, width = tokens.shape
    shapes = [jax.ShapeDtypeStruct((rows[0], 2 * width), jnp.bfloat16)] * copies
    for count in rows:
        shapes.append(jax.ShapeDtypeStruct((count, 2 * width), jnp.bfloat16))
        shapes.append(jax.ShapeDtypeStruct((count, n), jnp.bfloat16))
    whole = pl.BlockSpec(memory_space=pltpu.VMEM)
    outs = pl.pallas_call(
        lambda *refs: pack_kernel(blocks, copies, experts, *refs),
        out_shape=shapes,
        in_specs=[whole] * 4,
        out_specs=[whole] * len(shapes),
    )(ids.reshape(1, n), gate.reshape(1, n), tokens, grads)
    return outs[:copies], outs[copies::2], outs[copies + 1 :: 2]


def whole_weights(shard):
    if lax.axis_size("dp") == 1:
        return shard.astype(jnp.bfloat16)
    return lax.all_gather(shard.astype(jnp.bfloat16), "dp", axis=0, tiled=True)


def stepped(weights, grads):
    if lax.axis_size("dp") > 1:
        grads = lax.psum_scatter(
            grads.astype(jnp.bfloat16), "dp", scatter_dimension=0, tiled=True
        ).astype(jnp.float32)
    return weights - step_rate * grads


def swap(rows, mask):
    n_expert = lax.axis_size("expert")
    return lax.ppermute(rows, "expert", [(i, i ^ mask) for i in range(n_expert)])


core_bit, x_bit, y_bit, z_bit = 1, 2, 4, 8
early_masks = (x_bit, y_bit, z_bit, x_bit | y_bit | z_bit)


def after(values, *others):
    return lax.optimization_barrier((others, values))[1]


def swaps(blocks, masks):
    chained = []
    for block in blocks:
        chained.append(after(block, chained[-1]) if chained else block)
    return [swap(block, mask) for block, mask in zip(chained, masks)]


second_masks = (y_bit, z_bit, x_bit, x_bit | y_bit)


def total(*terms):
    return sum(term.astype(jnp.float32) for term in terms).astype(jnp.bfloat16)


def split_rows(array, rows):
    return [array[k : k + rows] for k in range(0, array.shape[0], rows)]


def near_sums(near, far):
    return (
        total(near[1], far[0]),
        total(near[2], far[1]),
        total(near[3], far[2], far[3]),
    )


def shards(tokens, attn_partials, expert_ids, gate, w_in, w_out):
    tok_rows, width = tokens.shape
    n_expert = lax.axis_size("expert")
    experts = n_expert // SHARDS
    capacity = 5 * tok_rows // (8 * experts)
    first = capacity // 8 * 8
    rest = experts * capacity - first
    units = w_in.shape[1]
    scale_in = width ** (-0.5)
    scale_out = FF ** (-0.5)

    def shifted(rows, hops):
        pairs = [(i, (i + SHARDS * hops) % n_expert) for i in range(n_expert)]
        return lax.ppermute(rows, "expert", pairs)

    offset = (experts - 1) * capacity - first
    own_blocks = [(0, 0, first, 0), (0, first, capacity, offset + first)]
    cross_blocks = [(s, 0, capacity, (s - 1) * capacity) for s in range(1, experts)]
    grads = summed_grads(attn_partials)
    early_copies, (early_own, late_own, *sent), picks = pack(
        own_blocks + cross_blocks,
        [first] + [rest] * experts,
        len(early_masks),
        experts,
        expert_ids,
        gate,
        tokens,
        grads,
    )

    def activated(rows):
        expert_rows, grad_rows = rows[:, :width], rows[:, width:]
        pre_act = contract_cols(expert_rows, weights_in) * scale_in
        hidden = gelu_value(pre_act).astype(jnp.bfloat16)
        hidden_grad = contract_cols(grad_rows, weights_out) * scale_out
        pre_grad = (hidden_grad * gelu_slope(pre_act)).astype(jnp.bfloat16)
        return expert_rows, grad_rows, hidden, pre_grad

    def input_parts(pre_grad):
        parts = jnp.dot(pre_grad, weights_in, preferred_element_type=jnp.float32) * scale_in
        return parts.astype(jnp.bfloat16)

    for s in range(1, experts):
        late_own = late_own + shifted(sent[s - 1], s)
    *early_near, early_far = after(
        [swap(rows, mask) for rows, mask in zip(early_copies, early_masks)], late_own
    )
    arrived = swaps(
        [
            jnp.concatenate([rows, late_own], axis=0)
            for rows in (early_near[2], early_near[0], early_near[1])
        ],
        (x_bit, y_bit, z_bit),
    )
    early_zx, early_xy, early_yz = [rows[:first] for rows in arrived]
    late_near = [rows[first:] for rows in arrived]
    early_rows = [early_own, *early_near, early_xy, early_yz, early_zx, early_far]

    own_weights = jnp.concatenate([whole_weights(w_in).T, whole_weights(w_out).T], axis=0)
    their_weights = swap(after(own_weights, late_own), core_bit)
    weights_in, weights_out = [
        jnp.concatenate([own_weights[part], their_weights[part]], axis=0)
        for part in (slice(0, units), slice(units, 2 * units))
    ]
    near_x, near_y, near_z = late_near
    late_far = [
        swap(rows, mask) for rows, mask in zip((near_x, near_y, near_z, near_z), second_masks)
    ]
    early = activated(jnp.concatenate(early_rows, axis=0))
    early_parts = input_parts(early[3])
    mine, theirs = slice(0, units), slice(units, 2 * units)

    def gradients(chunk):
        return [
            contract_rows(chunk[left][:, part], chunk[right])
            for left, right in ((3, 0), (2, 1))
            for part in (mine, theirs)
        ]

    early_gradients = gradients(early)
    late_far = after(late_far, early_parts, early_gradients)
    later = activated(jnp.concatenate([late_own, *late_near, *late_far], axis=0))
    late_parts = input_parts(later[3])
    parts = [
        jnp.concatenate(pair, axis=0)
        for pair in zip(split_rows(early_parts, first), split_rows(late_parts, rest))
    ]
    back_far = swaps(parts[4:], second_masks)
    in_mine, in_theirs, out_mine, out_theirs = [
        sum(pair) * scale
        for pair, scale in zip(
            zip(early_gradients, gradients(later)),
            (scale_in, scale_in, scale_out, scale_out),
        )
    ]
    in_shared = swap(in_theirs.astype(jnp.bfloat16), core_bit).astype(jnp.float32)
    out_shared = swap(out_theirs.astype(jnp.bfloat16), core_bit).astype(jnp.float32)
    new_w_in = stepped(w_in, (in_mine + in_shared).T)
    new_w_out = stepped(w_out, (out_mine + out_shared).T)
    back_near = swaps(near_sums(parts, back_far), (x_bit, y_bit, z_bit))
    back_near = after(back_near, new_w_in)
    sums = total(parts[0], *back_near)
    early_sum, late_sum = sums[:first], sums[first:]
    crossed = [shifted(late_sum, -s) for s in range(1, experts)]

    crossed = after(crossed, new_w_in, new_w_out)
    returned = [early_sum, late_sum, *crossed]
    token_grad = sum(contract_rows(pick, rows) for pick, rows in zip(picks, returned))
    return (token_grad.astype(jnp.bfloat16), new_w_in, new_w_out)


def solution(mesh):
    in_specs = (
        P(("expert", "dp"), None),
        P("dp", "expert", None),
        P(("expert", "dp")),
        P(("expert", "dp")),
        P("dp", "expert"),
        P("dp", "expert"),
    )
    out_specs = (P(("expert", "dp"), None), P("dp", "expert"), P("dp", "expert"))
    return jax.shard_map(shards, mesh=mesh, in_specs=in_specs, out_specs=out_specs, check_vma=False)
```

```python
import jax
import jax.numpy as jnp
from jax import lax
from jax.experimental import pallas as pl
from jax.experimental.pallas import tpu as pltpu
from jax.sharding import PartitionSpec as P

FF = 5120
SHARDS = 16


gelu_coef = 0.7978845608028654
cubic_coef = 0.044715
step_rate = 0.5


def gelu_value(inputs):
    return (
        0.5
        * inputs
        * (1.0 + jnp.tanh(gelu_coef * (inputs + cubic_coef * inputs * inputs * inputs)))
    )


def gelu_slope(inputs):
    tangent = jnp.tanh(gelu_coef * (inputs + cubic_coef * inputs * inputs * inputs))
    return 0.5 * (1.0 + tangent) + 0.5 * inputs * (1.0 - tangent * tangent) * gelu_coef * (
        1.0 + 3.0 * cubic_coef * inputs * inputs
    )


def contract_rows(left, right):
    return lax.dot_general(
        left, right, (((0,), (0,)), ((), ())), preferred_element_type=jnp.float32
    )


def contract_cols(left, right):
    return lax.dot_general(
        left, right, (((1,), (1,)), ((), ())), preferred_element_type=jnp.float32
    )


def summed_grads(attn_partials):
    if lax.axis_size("dp") == 1:
        return attn_partials[0]
    return lax.psum_scatter(attn_partials[0], "dp", scatter_dimension=0, tiled=True)


def pack_kernel(blocks, experts, *refs):
    ids_ref, gate_ref, tokens_ref, grads_ref, *outs = refs
    n, width = tokens_ref.shape
    mine = (lax.axis_index("expert") // SHARDS).astype(jnp.float32)
    ids = ids_ref[...].astype(jnp.float32)
    relative = ids - mine
    relative = jnp.where(relative < 0.0, relative + experts, relative)
    down = lax.broadcasted_iota(jnp.int32, (n, n), 0)
    across = lax.broadcasted_iota(jnp.int32, (n, n), 1)
    ids_down = jnp.sum(jnp.where(down == across, ids, 0.0), axis=1, keepdims=True)
    gate_down = jnp.sum(jnp.where(down == across, gate_ref[...], 0.0), axis=1, keepdims=True)
    rivals = jnp.where((ids_down == ids) & (down < across), 1.0, 0.0)
    rank = jnp.sum(rivals, axis=0, keepdims=True)
    gated = (gate_down * grads_ref[...].astype(jnp.float32)).astype(jnp.bfloat16)
    for k, (expert, begin, end, row) in enumerate(blocks):
        rows_ref, pick_ref = outs[2 * k], outs[2 * k + 1]
        chosen = (relative == expert) & (rank >= begin) & (rank < end)
        slot = jnp.where(chosen, rank - begin + row, -1.0).astype(jnp.int32)
        slots = lax.broadcasted_iota(jnp.int32, pick_ref.shape, 0)
        pick = jnp.where(slots == slot, 1.0, 0.0).astype(jnp.bfloat16)
        pick_ref[...] = pick
        for half, source in enumerate((tokens_ref[...], gated)):
            rows_ref[:, half * width : (half + 1) * width] = jnp.dot(
                pick, source, preferred_element_type=jnp.float32
            ).astype(jnp.bfloat16)


def pack(blocks, rows, experts, ids, gate, tokens, grads):
    n, width = tokens.shape
    shapes = []
    for count in rows:
        shapes.append(jax.ShapeDtypeStruct((count, 2 * width), jnp.bfloat16))
        shapes.append(jax.ShapeDtypeStruct((count, n), jnp.bfloat16))
    whole = pl.BlockSpec(memory_space=pltpu.VMEM)
    outs = pl.pallas_call(
        lambda *refs: pack_kernel(blocks, experts, *refs),
        out_shape=shapes,
        in_specs=[whole] * 4,
        out_specs=[whole] * len(shapes),
    )(ids.reshape(1, n), gate.reshape(1, n), tokens, grads)
    return outs[::2], outs[1::2]


def copies_kernel(rows_ref, *refs):
    for copy_ref in refs[-len(early_masks) :]:
        copy_ref[...] = rows_ref[...]


def early_copies(rows, *awaited):
    whole = pl.BlockSpec(memory_space=pltpu.VMEM)
    return pl.pallas_call(
        copies_kernel,
        out_shape=[jax.ShapeDtypeStruct(rows.shape, rows.dtype)] * len(early_masks),
        in_specs=[whole] + [pl.BlockSpec(memory_space=pl.ANY)] * len(awaited),
        out_specs=[whole] * len(early_masks),
    )(rows, *awaited)


def whole_weights(shard):
    if lax.axis_size("dp") == 1:
        return shard.astype(jnp.bfloat16)
    return lax.all_gather(shard.astype(jnp.bfloat16), "dp", axis=0, tiled=True)


def stepped(weights, grads):
    if lax.axis_size("dp") > 1:
        grads = lax.psum_scatter(
            grads.astype(jnp.bfloat16), "dp", scatter_dimension=0, tiled=True
        ).astype(jnp.float32)
    return weights - step_rate * grads


def swap(rows, mask):
    n_expert = lax.axis_size("expert")
    return lax.ppermute(rows, "expert", [(i, i ^ mask) for i in range(n_expert)])


core_bit, x_bit, y_bit, z_bit = 1, 2, 4, 8
early_masks = (x_bit, y_bit, z_bit, x_bit | y_bit)


def after(values, *others):
    return lax.optimization_barrier((others, values))[1]


def swaps(blocks, masks):
    chained = []
    for block in blocks:
        chained.append(after(block, chained[-1]) if chained else block)
    return [swap(block, mask) for block, mask in zip(chained, masks)]


def total(*terms):
    return sum(term.astype(jnp.float32) for term in terms).astype(jnp.bfloat16)


def split_rows(array, rows):
    return [array[k : k + rows] for k in range(0, array.shape[0], rows)]


def shards(tokens, attn_partials, expert_ids, gate, w_in, w_out):
    tok_rows, width = tokens.shape
    n_expert = lax.axis_size("expert")
    experts = n_expert // SHARDS
    capacity = 5 * tok_rows // (8 * experts)
    first = capacity // 8 * 8
    rest = experts * capacity - first
    units = w_in.shape[1]
    scale_in = width ** (-0.5)
    scale_out = FF ** (-0.5)

    def shifted(rows, hops):
        pairs = [(i, (i + SHARDS * hops) % n_expert) for i in range(n_expert)]
        return lax.ppermute(rows, "expert", pairs)

    offset = (experts - 1) * capacity - first
    own_blocks = [(0, 0, first, 0), (0, first, capacity, offset + first)]
    cross_blocks = [(s, 0, capacity, (s - 1) * capacity) for s in range(1, experts)]
    grads = summed_grads(attn_partials)
    (early_own, late_own, *sent), picks = pack(
        own_blocks + cross_blocks,
        [first] + [rest] * experts,
        experts,
        expert_ids,
        gate,
        tokens,
        grads,
    )

    def activated(rows):
        expert_rows, grad_rows = rows[:, :width], rows[:, width:]
        pre_act = contract_cols(expert_rows, weights_in) * scale_in
        hidden = gelu_value(pre_act).astype(jnp.bfloat16)
        hidden_grad = contract_cols(grad_rows, weights_out) * scale_out
        pre_grad = (hidden_grad * gelu_slope(pre_act)).astype(jnp.bfloat16)
        return expert_rows, grad_rows, hidden, pre_grad

    def input_parts(pre_grad):
        parts = jnp.dot(pre_grad, weights_in, preferred_element_type=jnp.float32) * scale_in
        return parts.astype(jnp.bfloat16)

    for s in range(1, experts):
        late_own = late_own + shifted(sent[s - 1], s)
    early_x, early_y, early_z, early_xy = after(
        [swap(rows, mask) for rows, mask in zip(early_copies(early_own, *sent), early_masks)], late_own
    )
    late_x, late_y, late_z = swaps(
        [
            jnp.concatenate([late_own, early_z], axis=0),
            jnp.concatenate([late_own, early_z], axis=0),
            late_own,
        ],
        (x_bit, y_bit, z_bit),
    )
    early_zx, early_yz = late_x[rest:], late_y[rest:]
    late_x, late_y = late_x[:rest], late_y[:rest]
    early_rows = [early_own, early_x, early_y, early_z, early_xy, early_yz, early_zx]

    own_weights = jnp.concatenate([whole_weights(w_in).T, whole_weights(w_out).T], axis=0)
    their_weights = swap(after(own_weights, late_own), core_bit)
    weights_in, weights_out = [
        jnp.concatenate([own_weights[part], their_weights[part]], axis=0)
        for part in (slice(0, units), slice(units, 2 * units))
    ]
    late_far, late_zx, late_yz, late_xy = swaps(
        [late_z, late_z, jnp.concatenate([late_y, early_xy], axis=0), late_x],
        (x_bit | y_bit, x_bit, z_bit, y_bit),
    )
    early = activated(jnp.concatenate(early_rows, axis=0))
    early_parts = input_parts(early[3])
    mine, theirs = slice(0, units), slice(units, 2 * units)

    def gradients(chunk):
        return [
            contract_rows(chunk[left][:, part], chunk[right])
            for left, right in ((3, 0), (2, 1))
            for part in (mine, theirs)
        ]

    early_gradients = gradients(early)
    late_rows = [late_own, late_x, late_y, late_z, late_xy, late_yz[:rest], late_zx, late_far]
    late_rows = after([*late_rows, late_yz[rest:]], early_parts, early_gradients)
    later = activated(jnp.concatenate(late_rows, axis=0))
    late_parts = input_parts(later[3])
    late_parts, last_parts = late_parts[: 8 * rest], late_parts[8 * rest :]
    parts = [
        jnp.concatenate(pair, axis=0)
        for pair in zip([*split_rows(early_parts, first), last_parts], split_rows(late_parts, rest))
    ]
    own, sum_x, sum_y, sum_z, sum_xy, sum_yz, sum_zx, sum_far = parts
    far, zx, xy, yz = swaps(
        [sum_far, sum_zx, sum_xy, sum_yz], (x_bit | y_bit, x_bit, y_bit, z_bit)
    )
    in_mine, in_theirs, out_mine, out_theirs = [
        sum(pair) * scale
        for pair, scale in zip(
            zip(early_gradients, gradients(later)),
            (scale_in, scale_in, scale_out, scale_out),
        )
    ]
    in_shared = swap(in_theirs.astype(jnp.bfloat16), core_bit).astype(jnp.float32)
    out_shared = swap(out_theirs.astype(jnp.bfloat16), core_bit).astype(jnp.float32)
    new_w_in = stepped(w_in, (in_mine + in_shared).T)
    new_w_out = stepped(w_out, (out_mine + out_shared).T)
    near = swaps(
        [total(sum_z, zx, far), total(sum_x, xy), total(sum_y, yz)], (z_bit, x_bit, y_bit)
    )
    sums = total(own, *near)
    early_sum, late_sum = sums[:first], sums[first:]
    crossed = [shifted(late_sum, -s) for s in range(1, experts)]

    crossed = after(crossed, new_w_in, new_w_out)
    returned = [early_sum, late_sum, *crossed]
    token_grad = sum(contract_rows(pick, rows) for pick, rows in zip(picks, returned))
    return (token_grad.astype(jnp.bfloat16), new_w_in, new_w_out)


def solution(mesh):
    in_specs = (
        P(("expert", "dp"), None),
        P("dp", "expert", None),
        P(("expert", "dp")),
        P(("expert", "dp")),
        P("dp", "expert"),
        P("dp", "expert"),
    )
    out_specs = (P(("expert", "dp"), None), P("dp", "expert"), P("dp", "expert"))
    return jax.shard_map(shards, mesh=mesh, in_specs=in_specs, out_specs=out_specs, check_vma=False)
```

```python
import jax
import jax.numpy as jnp
from jax import lax
from jax.experimental import pallas as pl
from jax.experimental.pallas import tpu as pltpu
from jax.sharding import PartitionSpec as P

FF = 5120
SHARDS = 16


gelu_coef = 0.7978845608028654
cubic_coef = 0.044715
step_rate = 0.5


def gelu_value(inputs):
    return (
        0.5
        * inputs
        * (1.0 + jnp.tanh(gelu_coef * (inputs + cubic_coef * inputs * inputs * inputs)))
    )


def gelu_slope(inputs):
    tangent = jnp.tanh(gelu_coef * (inputs + cubic_coef * inputs * inputs * inputs))
    return 0.5 * (1.0 + tangent) + 0.5 * inputs * (1.0 - tangent * tangent) * gelu_coef * (
        1.0 + 3.0 * cubic_coef * inputs * inputs
    )


def contract_rows(left, right):
    return lax.dot_general(
        left, right, (((0,), (0,)), ((), ())), preferred_element_type=jnp.float32
    )


def contract_cols(left, right):
    return lax.dot_general(
        left, right, (((1,), (1,)), ((), ())), preferred_element_type=jnp.float32
    )


def summed_grads(attn_partials):
    if lax.axis_size("dp") == 1:
        return attn_partials[0]
    return lax.psum_scatter(attn_partials[0], "dp", scatter_dimension=0, tiled=True)


def pick_rows(rows_ref, pick, tokens, gated):
    width = tokens.shape[1]
    for half, source in enumerate((tokens, gated)):
        rows_ref[:, half * width : (half + 1) * width] = jnp.dot(
            pick, source, preferred_element_type=jnp.float32
        ).astype(jnp.bfloat16)


def cross_kernel(blocks, experts, ids_ref, gate_ref, tokens_ref, grads_ref, gated_ref, *outs):
    picks, sent = outs[: len(blocks)], outs[len(blocks) :]
    n = tokens_ref.shape[0]
    mine = (lax.axis_index("expert") // SHARDS).astype(jnp.float32)
    ids = ids_ref[...].astype(jnp.float32)
    relative = ids - mine
    relative = jnp.where(relative < 0.0, relative + experts, relative)
    down = lax.broadcasted_iota(jnp.int32, (n, n), 0)
    across = lax.broadcasted_iota(jnp.int32, (n, n), 1)
    ids_down = jnp.sum(jnp.where(down == across, ids, 0.0), axis=1, keepdims=True)
    gate_down = jnp.sum(jnp.where(down == across, gate_ref[...], 0.0), axis=1, keepdims=True)
    rivals = jnp.where((ids_down == ids) & (down < across), 1.0, 0.0)
    rank = jnp.sum(rivals, axis=0, keepdims=True)
    gated = (gate_down * grads_ref[...].astype(jnp.float32)).astype(jnp.bfloat16)
    gated_ref[...] = gated
    for k, (expert, begin, end, row) in enumerate(blocks):
        chosen = (relative == expert) & (rank >= begin) & (rank < end)
        slot = jnp.where(chosen, rank - begin + row, -1.0).astype(jnp.int32)
        slots = lax.broadcasted_iota(jnp.int32, picks[k].shape, 0)
        pick = jnp.where(slots == slot, 1.0, 0.0).astype(jnp.bfloat16)
        picks[k][...] = pick
        if k >= len(blocks) - len(sent):
            pick_rows(sent[k - len(blocks) + len(sent)], pick, tokens_ref[...], gated)


def pack_cross(blocks, rows, experts, ids, gate, tokens, grads):
    n, width = tokens.shape
    whole = pl.BlockSpec(memory_space=pltpu.VMEM)
    gated, *outs = pl.pallas_call(
        lambda *refs: cross_kernel(blocks, experts, *refs),
        out_shape=[jax.ShapeDtypeStruct((n, width), jnp.bfloat16)]
        + [jax.ShapeDtypeStruct((count, n), jnp.bfloat16) for count in rows]
        + [jax.ShapeDtypeStruct((count, 2 * width), jnp.bfloat16) for count in rows[2:]],
        in_specs=[whole] * 4,
        out_specs=[whole] * (2 * len(rows) - 1),
    )(ids.reshape(1, n), gate.reshape(1, n), tokens, grads)
    return gated, outs[: len(rows)], outs[len(rows) :]


def own_kernel(early_pick_ref, late_pick_ref, tokens_ref, gated_ref, *refs):
    late_ref, early_ref, *copies = refs[-len(early_masks) - 2 :]
    pick_rows(early_ref, early_pick_ref[...], tokens_ref[...], gated_ref[...])
    for copy_ref in copies:
        copy_ref[...] = early_ref[...]
    pick_rows(late_ref, late_pick_ref[...], tokens_ref[...], gated_ref[...])


def pack_own(early_pick, late_pick, tokens, gated, *sent):
    whole = pl.BlockSpec(memory_space=pltpu.VMEM)
    width = tokens.shape[1]
    early, late = [
        jax.ShapeDtypeStruct((pick.shape[0], 2 * width), jnp.bfloat16)
        for pick in (early_pick, late_pick)
    ]
    shapes = [late] + [early] * (len(early_masks) + 1)
    return pl.pallas_call(
        own_kernel,
        out_shape=shapes,
        in_specs=[whole] * 4 + [pl.BlockSpec(memory_space=pl.ANY)] * len(sent),
        out_specs=[whole] * len(shapes),
    )(early_pick, late_pick, tokens, gated, *sent)


def whole_weights(shard):
    if lax.axis_size("dp") == 1:
        return shard.astype(jnp.bfloat16)
    return lax.all_gather(shard.astype(jnp.bfloat16), "dp", axis=0, tiled=True)


def stepped(weights, grads):
    if lax.axis_size("dp") > 1:
        grads = lax.psum_scatter(
            grads.astype(jnp.bfloat16), "dp", scatter_dimension=0, tiled=True
        ).astype(jnp.float32)
    return weights - step_rate * grads


def swap(rows, mask):
    n_expert = lax.axis_size("expert")
    return lax.ppermute(rows, "expert", [(i, i ^ mask) for i in range(n_expert)])


core_bit, x_bit, y_bit, z_bit = 1, 2, 4, 8
early_masks = (x_bit, y_bit, z_bit, x_bit | y_bit)


def after(values, *others):
    return lax.optimization_barrier((others, values))[1]


def swaps(blocks, masks):
    chained = []
    for block in blocks:
        chained.append(after(block, chained[-1]) if chained else block)
    return [swap(block, mask) for block, mask in zip(chained, masks)]


def total(*terms):
    return sum(term.astype(jnp.float32) for term in terms).astype(jnp.bfloat16)


def split_rows(array, rows):
    return [array[k : k + rows] for k in range(0, array.shape[0], rows)]


def shards(tokens, attn_partials, expert_ids, gate, w_in, w_out):
    tok_rows, width = tokens.shape
    n_expert = lax.axis_size("expert")
    experts = n_expert // SHARDS
    capacity = 5 * tok_rows // (8 * experts)
    first = capacity // 8 * 8
    rest = experts * capacity - first
    units = w_in.shape[1]
    scale_in = width ** (-0.5)
    scale_out = FF ** (-0.5)

    def shifted(rows, hops):
        pairs = [(i, (i + SHARDS * hops) % n_expert) for i in range(n_expert)]
        return lax.ppermute(rows, "expert", pairs)

    offset = (experts - 1) * capacity - first
    own_blocks = [(0, 0, first, 0), (0, first, capacity, offset + first)]
    cross_blocks = [(s, 0, capacity, (s - 1) * capacity) for s in range(1, experts)]
    grads = summed_grads(attn_partials)
    gated, picks, sent = pack_cross(
        own_blocks + cross_blocks,
        [first] + [rest] * experts,
        experts,
        expert_ids,
        gate,
        tokens,
        grads,
    )
    late_own, early_own, *early_copies = pack_own(picks[0], picks[1], tokens, gated, *sent)

    def activated(rows):
        expert_rows, grad_rows = rows[:, :width], rows[:, width:]
        pre_act = contract_cols(expert_rows, weights_in) * scale_in
        hidden = gelu_value(pre_act).astype(jnp.bfloat16)
        hidden_grad = contract_cols(grad_rows, weights_out) * scale_out
        pre_grad = (hidden_grad * gelu_slope(pre_act)).astype(jnp.bfloat16)
        return [expert_rows, grad_rows, hidden, pre_grad]

    def input_parts(pre_grad):
        parts = jnp.dot(pre_grad, weights_in, preferred_element_type=jnp.float32) * scale_in
        return parts.astype(jnp.bfloat16)

    for s in range(1, experts):
        late_own = late_own + shifted(sent[s - 1], s)
    early_x, early_y, early_z, early_xy = after(
        [swap(rows, mask) for rows, mask in zip(early_copies, early_masks)], late_own
    )
    late_x, late_y, late_z = swaps(
        [
            jnp.concatenate([late_own, early_z], axis=0),
            jnp.concatenate([late_own, early_z], axis=0),
            jnp.concatenate([late_own, early_xy], axis=0),
        ],
        (x_bit, y_bit, z_bit),
    )
    early_zx, early_yz, early_far = late_x[rest:], late_y[rest:], late_z[rest:]
    late_x, late_y, late_z = late_x[:rest], late_y[:rest], late_z[:rest]
    early_rows = [early_own, early_x, early_y, early_z, early_xy, early_yz, early_zx, early_far]

    own_weights = jnp.concatenate([whole_weights(w_in).T, whole_weights(w_out).T], axis=0)
    their_weights = swap(after(own_weights, late_own), core_bit)
    weights_in, weights_out = [
        jnp.concatenate([own_weights[part], their_weights[part]], axis=0)
        for part in (slice(0, units), slice(units, 2 * units))
    ]
    late_far, late_zx, late_yz, late_xy = swaps(
        [late_z, late_z, late_y, late_x],
        (x_bit | y_bit, x_bit, z_bit, y_bit),
    )
    early = activated(jnp.concatenate(early_rows, axis=0))
    early_parts = input_parts(early[3])
    mine, theirs = slice(0, units), slice(units, 2 * units)

    def gradients(chunk):
        return [
            contract_rows(chunk[left][:, part], chunk[right])
            for left, right in ((3, 0), (2, 1))
            for part in (mine, theirs)
        ]

    early_gradients = gradients(early)
    late_far = after([late_xy, late_yz, late_zx, late_far], early_parts, early_gradients)
    late_rows = [late_own, late_x, late_y, late_z, *late_far]
    later = activated(jnp.concatenate(late_rows, axis=0))
    late_parts = input_parts(later[3])
    parts = [
        jnp.concatenate(pair, axis=0)
        for pair in zip(split_rows(early_parts, first), split_rows(late_parts, rest))
    ]
    own, sum_x, sum_y, sum_z, sum_xy, sum_yz, sum_zx, sum_far = parts
    far, zx, xy, yz = swaps(
        [sum_far, sum_zx, sum_xy, sum_yz], (x_bit | y_bit, x_bit, y_bit, z_bit)
    )
    in_mine, in_theirs, out_mine, out_theirs = [
        sum(pair) * scale
        for pair, scale in zip(
            zip(early_gradients, gradients(later[:2] + after(later[2:], zx))),
            (scale_in, scale_in, scale_out, scale_out),
        )
    ]
    in_shared = swap(in_theirs.astype(jnp.bfloat16), core_bit).astype(jnp.float32)
    out_shared = swap(out_theirs.astype(jnp.bfloat16), core_bit).astype(jnp.float32)
    new_w_in = stepped(w_in, (in_mine + in_shared).T)
    new_w_out = stepped(w_out, (out_mine + out_shared).T)
    near = swaps(
        [total(sum_z, zx, far), total(sum_x, xy), total(sum_y, yz)], (z_bit, x_bit, y_bit)
    )
    sums = total(own, *near)
    early_sum, late_sum = sums[:first], sums[first:]
    crossed = [shifted(late_sum, -s) for s in range(1, experts)]

    crossed = after(crossed, new_w_in, new_w_out)
    returned = [early_sum, late_sum, *crossed]
    token_grad = sum(contract_rows(pick, rows) for pick, rows in zip(picks, returned))
    return (token_grad.astype(jnp.bfloat16), new_w_in, new_w_out)


def solution(mesh):
    in_specs = (
        P(("expert", "dp"), None),
        P("dp", "expert", None),
        P(("expert", "dp")),
        P(("expert", "dp")),
        P("dp", "expert"),
        P("dp", "expert"),
    )
    out_specs = (P(("expert", "dp"), None), P("dp", "expert"), P("dp", "expert"))
    return jax.shard_map(shards, mesh=mesh, in_specs=in_specs, out_specs=out_specs, check_vma=False)
```

```python
import jax
import jax.numpy as jnp
from jax import lax
from jax.experimental import pallas as pl
from jax.experimental.pallas import tpu as pltpu
from jax.sharding import PartitionSpec as P

FF = 5120
SHARDS = 16


gelu_coef = 0.7978845608028654
cubic_coef = 0.044715
step_rate = 0.5


def gelu_value(inputs):
    return (
        0.5
        * inputs
        * (1.0 + jnp.tanh(gelu_coef * (inputs + cubic_coef * inputs * inputs * inputs)))
    )


def gelu_slope(inputs):
    tangent = jnp.tanh(gelu_coef * (inputs + cubic_coef * inputs * inputs * inputs))
    return 0.5 * (1.0 + tangent) + 0.5 * inputs * (1.0 - tangent * tangent) * gelu_coef * (
        1.0 + 3.0 * cubic_coef * inputs * inputs
    )


def contract_rows(left, right):
    return lax.dot_general(
        left, right, (((0,), (0,)), ((), ())), preferred_element_type=jnp.float32
    )


def contract_cols(left, right):
    return lax.dot_general(
        left, right, (((1,), (1,)), ((), ())), preferred_element_type=jnp.float32
    )


def summed_grads(attn_partials):
    if lax.axis_size("dp") == 1:
        return attn_partials[0]
    return lax.psum_scatter(attn_partials[0], "dp", scatter_dimension=0, tiled=True)


def pick_rows(rows_ref, pick, tokens, gated):
    width = tokens.shape[1]
    for half, source in enumerate((tokens, gated)):
        rows_ref[:, half * width : (half + 1) * width] = jnp.dot(
            pick, source, preferred_element_type=jnp.float32
        ).astype(jnp.bfloat16)


def cross_kernel(blocks, experts, ids_ref, gate_ref, tokens_ref, grads_ref, gated_ref, *outs):
    picks, sent = outs[: len(blocks)], outs[len(blocks) :]
    n = tokens_ref.shape[0]
    mine = (lax.axis_index("expert") // SHARDS).astype(jnp.float32)
    ids = ids_ref[...].astype(jnp.float32)
    relative = ids - mine
    relative = jnp.where(relative < 0.0, relative + experts, relative)
    down = lax.broadcasted_iota(jnp.int32, (n, n), 0)
    across = lax.broadcasted_iota(jnp.int32, (n, n), 1)
    ids_down = jnp.sum(jnp.where(down == across, ids, 0.0), axis=1, keepdims=True)
    gate_down = jnp.sum(jnp.where(down == across, gate_ref[...], 0.0), axis=1, keepdims=True)
    rivals = jnp.where((ids_down == ids) & (down < across), 1.0, 0.0)
    rank = jnp.sum(rivals, axis=0, keepdims=True)
    gated = (gate_down * grads_ref[...].astype(jnp.float32)).astype(jnp.bfloat16)
    gated_ref[...] = gated
    for k, (expert, begin, end, row) in enumerate(blocks):
        chosen = (relative == expert) & (rank >= begin) & (rank < end)
        slot = jnp.where(chosen, rank - begin + row, -1.0).astype(jnp.int32)
        slots = lax.broadcasted_iota(jnp.int32, picks[k].shape, 0)
        pick = jnp.where(slots == slot, 1.0, 0.0).astype(jnp.bfloat16)
        picks[k][...] = pick
        if k >= len(blocks) - len(sent):
            pick_rows(sent[k - len(blocks) + len(sent)], pick, tokens_ref[...], gated)


def pack_cross(blocks, rows, experts, ids, gate, tokens, grads):
    n, width = tokens.shape
    whole = pl.BlockSpec(memory_space=pltpu.VMEM)
    gated, *outs = pl.pallas_call(
        lambda *refs: cross_kernel(blocks, experts, *refs),
        out_shape=[jax.ShapeDtypeStruct((n, width), jnp.bfloat16)]
        + [jax.ShapeDtypeStruct((count, n), jnp.bfloat16) for count in rows]
        + [jax.ShapeDtypeStruct((count, 2 * width), jnp.bfloat16) for count in rows[2:]],
        in_specs=[whole] * 4,
        out_specs=[whole] * (2 * len(rows) - 1),
    )(ids.reshape(1, n), gate.reshape(1, n), tokens, grads)
    return gated, outs[: len(rows)], outs[len(rows) :]


def own_kernel(early_pick_ref, late_pick_ref, tokens_ref, gated_ref, *refs):
    late_ref, early_ref, *copies = refs[-len(early_masks) - 2 :]
    pick_rows(early_ref, early_pick_ref[...], tokens_ref[...], gated_ref[...])
    for copy_ref in copies:
        copy_ref[...] = early_ref[...]
    pick_rows(late_ref, late_pick_ref[...], tokens_ref[...], gated_ref[...])


def pack_own(early_pick, late_pick, tokens, gated, *sent):
    whole = pl.BlockSpec(memory_space=pltpu.VMEM)
    width = tokens.shape[1]
    early, late = [
        jax.ShapeDtypeStruct((pick.shape[0], 2 * width), jnp.bfloat16)
        for pick in (early_pick, late_pick)
    ]
    shapes = [late] + [early] * (len(early_masks) + 1)
    return pl.pallas_call(
        own_kernel,
        out_shape=shapes,
        in_specs=[whole] * 4 + [pl.BlockSpec(memory_space=pl.ANY)] * len(sent),
        out_specs=[whole] * len(shapes),
    )(early_pick, late_pick, tokens, gated, *sent)


def whole_weights(shard):
    if lax.axis_size("dp") == 1:
        return shard.astype(jnp.bfloat16)
    return lax.all_gather(shard.astype(jnp.bfloat16), "dp", axis=0, tiled=True)


def stepped(weights, grads):
    if lax.axis_size("dp") > 1:
        grads = lax.psum_scatter(
            grads.astype(jnp.bfloat16), "dp", scatter_dimension=0, tiled=True
        ).astype(jnp.float32)
    return weights - step_rate * grads


def swap(rows, mask):
    n_expert = lax.axis_size("expert")
    return lax.ppermute(rows, "expert", [(i, i ^ mask) for i in range(n_expert)])


core_bit, x_bit, y_bit, z_bit = 1, 2, 4, 8
early_masks = (x_bit, y_bit, z_bit, x_bit | y_bit)
back_masks = (14, 12, 10, 6, 2, 4, 8)


def after(values, *others):
    return lax.optimization_barrier((others, values))[1]


def swaps(blocks, masks):
    chained = []
    for block in blocks:
        chained.append(after(block, chained[-1]) if chained else block)
    return [swap(block, mask) for block, mask in zip(chained, masks)]


def total(*terms):
    return sum(term.astype(jnp.float32) for term in terms).astype(jnp.bfloat16)


def split_rows(array, rows):
    return [array[k : k + rows] for k in range(0, array.shape[0], rows)]


def shards(tokens, attn_partials, expert_ids, gate, w_in, w_out):
    tok_rows, width = tokens.shape
    n_expert = lax.axis_size("expert")
    experts = n_expert // SHARDS
    capacity = 5 * tok_rows // (8 * experts)
    first = capacity // 8 * 8
    rest = experts * capacity - first
    units = w_in.shape[1]
    scale_in = width ** (-0.5)
    scale_out = FF ** (-0.5)

    def shifted(rows, hops):
        pairs = [(i, (i + SHARDS * hops) % n_expert) for i in range(n_expert)]
        return lax.ppermute(rows, "expert", pairs)

    offset = (experts - 1) * capacity - first
    own_blocks = [(0, 0, first, 0), (0, first, capacity, offset + first)]
    cross_blocks = [(s, 0, capacity, (s - 1) * capacity) for s in range(1, experts)]
    grads = summed_grads(attn_partials)
    gated, picks, sent = pack_cross(
        own_blocks + cross_blocks,
        [first] + [rest] * experts,
        experts,
        expert_ids,
        gate,
        tokens,
        grads,
    )
    late_own, early_own, *early_copies = pack_own(picks[0], picks[1], tokens, gated, *sent)

    def activated(rows):
        expert_rows, grad_rows = rows[:, :width], rows[:, width:]
        pre_act = contract_cols(expert_rows, weights_in) * scale_in
        hidden = gelu_value(pre_act).astype(jnp.bfloat16)
        hidden_grad = contract_cols(grad_rows, weights_out) * scale_out
        pre_grad = (hidden_grad * gelu_slope(pre_act)).astype(jnp.bfloat16)
        return [expert_rows, grad_rows, hidden, pre_grad]

    def input_parts(pre_grad):
        parts = jnp.dot(pre_grad, weights_in, preferred_element_type=jnp.float32) * scale_in
        return parts.astype(jnp.bfloat16)

    for s in range(1, experts):
        late_own = late_own + shifted(sent[s - 1], s)
    early_x, early_y, early_z, early_xy = after(
        [swap(rows, mask) for rows, mask in zip(early_copies, early_masks)], late_own
    )
    late_x, late_y, late_z = swaps(
        [
            jnp.concatenate([late_own, early_z], axis=0),
            jnp.concatenate([late_own, early_z], axis=0),
            jnp.concatenate([late_own, early_xy], axis=0),
        ],
        (x_bit, y_bit, z_bit),
    )
    early_zx, early_yz, early_far = late_x[rest:], late_y[rest:], late_z[rest:]
    late_x, late_y, late_z = late_x[:rest], late_y[:rest], late_z[:rest]
    early_rows = [early_own, early_x, early_y, early_z, early_xy, early_yz, early_zx, early_far]

    own_weights = jnp.concatenate([whole_weights(w_in).T, whole_weights(w_out).T], axis=0)
    their_weights = swap(after(own_weights, late_own), core_bit)
    weights_in, weights_out = [
        jnp.concatenate([own_weights[part], their_weights[part]], axis=0)
        for part in (slice(0, units), slice(units, 2 * units))
    ]
    late_far, late_zx, late_yz, late_xy = swaps(
        [late_z, late_z, late_y, late_x],
        (x_bit | y_bit, x_bit, z_bit, y_bit),
    )
    early = activated(jnp.concatenate(early_rows, axis=0))
    early_parts = input_parts(early[3])
    mine, theirs = slice(0, units), slice(units, 2 * units)

    def gradients(chunk):
        return [
            contract_rows(chunk[left][:, part], chunk[right])
            for left, right in ((3, 0), (2, 1))
            for part in (mine, theirs)
        ]

    early_gradients = gradients(early)
    late_far = after([late_xy, late_yz, late_zx, late_far], early_parts, early_gradients)
    late_rows = [late_own, late_x, late_y, late_z, *late_far]
    later = activated(jnp.concatenate(late_rows, axis=0))
    late_parts = input_parts(later[3])
    early_parts, late_parts = split_rows(early_parts, first), split_rows(late_parts, rest)
    back = swaps(
        [
            late_parts[7],
            late_parts[5],
            late_parts[6],
            jnp.concatenate([late_parts[4], early_parts[7]], axis=0),
            jnp.concatenate([late_parts[1], early_parts[6]], axis=0),
            jnp.concatenate([late_parts[2], early_parts[4]], axis=0),
            jnp.concatenate([late_parts[3], early_parts[5]], axis=0),
        ],
        back_masks,
    )
    far, zx, xy, yz = [rows[rest:] for rows in back[3:]]
    late_sum = total(late_parts[0], *[rows[:rest] for rows in back])
    crossed = [shifted(late_sum, -s) for s in range(1, experts)]
    in_mine, in_theirs, out_mine, out_theirs = [
        sum(pair) * scale
        for pair, scale in zip(
            zip(early_gradients, gradients(later[:2] + after(later[2:], back[0]))),
            (scale_in, scale_in, scale_out, scale_out),
        )
    ]
    in_shared = swap(in_theirs.astype(jnp.bfloat16), core_bit).astype(jnp.float32)
    out_shared = swap(out_theirs.astype(jnp.bfloat16), core_bit).astype(jnp.float32)
    new_w_in = stepped(w_in, (in_mine + in_shared).T)
    new_w_out = stepped(w_out, (out_mine + out_shared).T)
    near = [
        total(early_parts[3], zx, far),
        total(early_parts[1], xy),
        total(early_parts[2], yz),
    ]
    near = swaps(after(near, late_sum), (z_bit, x_bit, y_bit))
    early_sum = total(early_parts[0], *near)
    crossed = after(crossed, new_w_in, new_w_out)
    returned = [early_sum, late_sum, *crossed]
    token_grad = sum(contract_rows(pick, rows) for pick, rows in zip(picks, returned))
    return (token_grad.astype(jnp.bfloat16), new_w_in, new_w_out)


def solution(mesh):
    in_specs = (
        P(("expert", "dp"), None),
        P("dp", "expert", None),
        P(("expert", "dp")),
        P(("expert", "dp")),
        P("dp", "expert"),
        P("dp", "expert"),
    )
    out_specs = (P(("expert", "dp"), None), P("dp", "expert"), P("dp", "expert"))
    return jax.shard_map(shards, mesh=mesh, in_specs=in_specs, out_specs=out_specs, check_vma=False)
```

```python
import jax
import jax.numpy as jnp
from jax import lax
from jax.experimental import pallas as pl
from jax.experimental.pallas import tpu as pltpu
from jax.sharding import PartitionSpec as P

FF = 5120
SHARDS = 16


gelu_coef = 0.7978845608028654
cubic_coef = 0.044715
step_rate = 0.5


def gelu_value(inputs):
    return (
        0.5
        * inputs
        * (1.0 + jnp.tanh(gelu_coef * (inputs + cubic_coef * inputs * inputs * inputs)))
    )


def gelu_slope(inputs):
    tangent = jnp.tanh(gelu_coef * (inputs + cubic_coef * inputs * inputs * inputs))
    return 0.5 * (1.0 + tangent) + 0.5 * inputs * (1.0 - tangent * tangent) * gelu_coef * (
        1.0 + 3.0 * cubic_coef * inputs * inputs
    )


def contract_rows(left, right):
    return lax.dot_general(
        left, right, (((0,), (0,)), ((), ())), preferred_element_type=jnp.float32
    )


def contract_cols(left, right):
    return lax.dot_general(
        left, right, (((1,), (1,)), ((), ())), preferred_element_type=jnp.float32
    )


def summed_grads(attn_partials):
    if lax.axis_size("dp") == 1:
        return attn_partials[0]
    return lax.psum_scatter(attn_partials[0], "dp", scatter_dimension=0, tiled=True)


def picked(pick, source):
    return jnp.dot(pick, source, preferred_element_type=jnp.float32)


def pack_kernel(blocks, experts, ids_ref, gate_ref, tokens_ref, grads_ref, *outs):
    n, width = tokens_ref.shape
    mine = (lax.axis_index("expert") // SHARDS).astype(jnp.float32)
    ids = ids_ref[...].astype(jnp.float32)
    relative = ids - mine
    relative = jnp.where(relative < 0.0, relative + experts, relative)
    down = lax.broadcasted_iota(jnp.int32, (n, n), 0)
    across = lax.broadcasted_iota(jnp.int32, (n, n), 1)
    ids_down = jnp.sum(jnp.where(down == across, ids, 0.0), axis=1, keepdims=True)
    gate_down = jnp.sum(jnp.where(down == across, gate_ref[...], 0.0), axis=1, keepdims=True)
    rivals = jnp.where((ids_down == ids) & (down < across), 1.0, 0.0)
    rank = jnp.sum(rivals, axis=0, keepdims=True)
    tokens = tokens_ref[...]
    gated = (gate_down * grads_ref[...].astype(jnp.float32)).astype(jnp.bfloat16)
    rows, picks = outs[: len(blocks)], outs[len(blocks) : 3 * len(blocks) - 2]
    copies = outs[3 * len(blocks) - 2 :]

    def one_hot(shape, block, shift):
        expert, begin, end, row = block
        chosen = (relative == expert) & (rank >= begin) & (rank < end)
        slot = jnp.where(chosen, rank - begin + row + shift, -1.0).astype(jnp.int32)
        slots = lax.broadcasted_iota(jnp.int32, shape, 0)
        return jnp.where(slots == slot, 1.0, 0.0).astype(jnp.bfloat16)

    for k, block in enumerate(blocks[2:]):
        upper_ref, lower_ref = picks[2 * k + 2], picks[2 * k + 3]
        upper = one_hot(upper_ref.shape, block, 0)
        lower = one_hot(lower_ref.shape, block, block[2])
        upper_ref[...], lower_ref[...] = upper, lower
        both = picked(upper, tokens) + picked(lower, gated)
        rows[k + 2][...] = both.astype(jnp.bfloat16)
    for k, block in enumerate(blocks[:2]):
        pick = one_hot(picks[k].shape, block, 0)
        picks[k][...] = pick
        rows[k][:, :width] = picked(pick, tokens).astype(jnp.bfloat16)
        rows[k][:, width:] = picked(pick, gated).astype(jnp.bfloat16)
    for copy_ref in copies:
        copy_ref[...] = rows[0][...]


def pack(blocks, first, rest, capacity, experts, ids, gate, tokens, grads):
    n, width = tokens.shape
    whole = pl.BlockSpec(memory_space=pltpu.VMEM)
    crossing = len(blocks) - 2

    def shape(rows, columns):
        return jax.ShapeDtypeStruct((rows, columns), jnp.bfloat16)

    shapes = [shape(first, 2 * width), shape(rest, 2 * width)]
    shapes += [shape(2 * capacity, width)] * crossing
    shapes += [shape(first, n), shape(rest, n)] + [shape(2 * capacity, n)] * (2 * crossing)
    shapes += [shape(first, 2 * width)] * len(early_masks)
    outs = pl.pallas_call(
        lambda *refs: pack_kernel(blocks, experts, *refs),
        out_shape=shapes,
        in_specs=[whole] * 4,
        out_specs=[whole] * len(shapes),
    )(ids.reshape(1, n), gate.reshape(1, n), tokens, grads)
    rows, picks = outs[: len(blocks)], outs[len(blocks) : 3 * len(blocks) - 2]
    return rows, picks, outs[3 * len(blocks) - 2 :]


def handed_on(copies, sent):
    anywhere = pl.BlockSpec(memory_space=pl.ANY)
    return pl.pallas_call(
        lambda *refs: None,
        out_shape=[jax.ShapeDtypeStruct(rows.shape, rows.dtype) for rows in copies],
        in_specs=[anywhere] * (len(copies) + len(sent)),
        out_specs=[anywhere] * len(copies),
        input_output_aliases={k: k for k in range(len(copies))},
    )(*copies, *sent)


def unpack_kernel(own_ref, *refs):
    *refs, out_ref = refs
    crossings = len(refs) // 3
    picks, rows = refs[: 2 * crossings], refs[2 * crossings :]
    half = out_ref.shape[1] // 2
    for side in range(2):
        columns = slice(side * half, (side + 1) * half)
        both = own_ref[:, columns].astype(jnp.float32)
        for pick_ref, rows_ref in zip(picks[side::2], rows):
            both = both + contract_rows(pick_ref[...], rows_ref[...])
        out_ref[:, columns] = both.astype(jnp.bfloat16)


def unpacked(own_grad, picks, crossed):
    return pl.pallas_call(
        unpack_kernel, out_shape=jax.ShapeDtypeStruct(own_grad.shape, own_grad.dtype)
    )(own_grad, *picks, *crossed)


def whole_weights(shard):
    if lax.axis_size("dp") == 1:
        return shard.astype(jnp.bfloat16)
    return lax.all_gather(shard.astype(jnp.bfloat16), "dp", axis=0, tiled=True)


def stepped(weights, grads):
    if lax.axis_size("dp") > 1:
        grads = lax.psum_scatter(
            grads.astype(jnp.bfloat16), "dp", scatter_dimension=0, tiled=True
        ).astype(jnp.float32)
    return weights - step_rate * grads


def swap(rows, mask):
    n_expert = lax.axis_size("expert")
    return lax.ppermute(rows, "expert", [(i, i ^ mask) for i in range(n_expert)])


core_bit, x_bit, y_bit, z_bit = 1, 2, 4, 8
early_masks = (x_bit, y_bit, z_bit, x_bit | y_bit)


def after(values, *others):
    return lax.optimization_barrier((others, values))[1]


def swaps(blocks, masks):
    chained = []
    for block in blocks:
        chained.append(after(block, chained[-1]) if chained else block)
    return [swap(block, mask) for block, mask in zip(chained, masks)]


def total(*terms):
    return sum(term.astype(jnp.float32) for term in terms).astype(jnp.bfloat16)


def split_rows(array, rows):
    return [array[k : k + rows] for k in range(0, array.shape[0], rows)]


def shards(tokens, attn_partials, expert_ids, gate, w_in, w_out):
    tok_rows, width = tokens.shape
    n_expert = lax.axis_size("expert")
    experts = n_expert // SHARDS
    capacity = 5 * tok_rows // (8 * experts)
    first = capacity // 8 * 8
    rest = experts * capacity - first
    units = w_in.shape[1]
    scale_in = width ** (-0.5)
    scale_out = FF ** (-0.5)

    def shifted(rows, hops):
        pairs = [(i, (i + SHARDS * hops) % n_expert) for i in range(n_expert)]
        return lax.ppermute(rows, "expert", pairs)

    offset = (experts - 1) * capacity - first
    own_blocks = [(0, 0, first, 0), (0, first, capacity, offset + first)]
    cross_blocks = [(s, 0, capacity, 0) for s in range(1, experts)]
    grads = summed_grads(attn_partials)
    (early_own, late_own, *sent), picks, copies = pack(
        own_blocks + cross_blocks, first, rest, capacity, experts, expert_ids, gate, tokens, grads
    )
    early_copies = handed_on(copies, sent)

    def activated(rows):
        expert_rows, grad_rows = rows[:, :width], rows[:, width:]
        pre_act = contract_cols(expert_rows, weights_in) * scale_in
        hidden = gelu_value(pre_act).astype(jnp.bfloat16)
        hidden_grad = contract_cols(grad_rows, weights_out) * scale_out
        pre_grad = (hidden_grad * gelu_slope(pre_act)).astype(jnp.bfloat16)
        return [expert_rows, grad_rows, hidden, pre_grad]

    def input_parts(pre_grad):
        parts = jnp.dot(pre_grad, weights_in, preferred_element_type=jnp.float32) * scale_in
        return parts.astype(jnp.bfloat16)

    for s in range(1, experts):
        side_by_side = jnp.concatenate(split_rows(shifted(sent[s - 1], s), capacity), axis=1)
        late_own = late_own + jnp.pad(
            side_by_side, (((s - 1) * capacity, rest - s * capacity), (0, 0))
        )
    early_x, early_y, early_z, early_xy = after(
        [swap(rows, mask) for rows, mask in zip(early_copies, early_masks)], late_own
    )
    late_x, late_y, late_z = swaps(
        [
            jnp.concatenate([late_own, early_z], axis=0),
            jnp.concatenate([late_own, early_z], axis=0),
            jnp.concatenate([late_own, early_xy], axis=0),
        ],
        (x_bit, y_bit, z_bit),
    )
    early_zx, early_yz, early_far = late_x[rest:], late_y[rest:], late_z[rest:]
    late_x, late_y, late_z = late_x[:rest], late_y[:rest], late_z[:rest]
    early_rows = [early_own, early_x, early_y, early_z, early_xy, early_yz, early_zx, early_far]

    own_weights = jnp.concatenate([whole_weights(w_in).T, whole_weights(w_out).T], axis=0)
    their_weights = swap(after(own_weights, late_own), core_bit)
    weights_in, weights_out = [
        jnp.concatenate([own_weights[part], their_weights[part]], axis=0)
        for part in (slice(0, units), slice(units, 2 * units))
    ]
    late_far, late_zx, late_yz, late_xy = swaps(
        [late_z, late_z, late_y, late_x],
        (x_bit | y_bit, x_bit, z_bit, y_bit),
    )
    early = activated(jnp.concatenate(early_rows, axis=0))
    early_parts = input_parts(early[3])
    mine, theirs = slice(0, units), slice(units, 2 * units)

    def gradients(chunk):
        return [
            contract_rows(chunk[left][:, part], chunk[right])
            for left, right in ((3, 0), (2, 1))
            for part in (mine, theirs)
        ]

    early_gradients = gradients(early)
    late_far = after([late_xy, late_yz, late_zx, late_far], early_parts, early_gradients)
    late_rows = [late_own, late_x, late_y, late_z, *late_far]
    later = activated(jnp.concatenate(late_rows, axis=0))
    late_parts = input_parts(later[3])
    parts = [
        jnp.concatenate(pair, axis=0)
        for pair in zip(split_rows(early_parts, first), split_rows(late_parts, rest))
    ]
    own, sum_x, sum_y, sum_z, sum_xy, sum_yz, sum_zx, sum_far = parts
    far, zx, xy, yz = swaps(
        [sum_far, sum_zx, sum_xy, sum_yz], (x_bit | y_bit, x_bit, y_bit, z_bit)
    )
    in_mine, in_theirs, out_mine, out_theirs = [
        sum(pair) * scale
        for pair, scale in zip(
            zip(early_gradients, gradients(later[:2] + after(later[2:], zx))),
            (scale_in, scale_in, scale_out, scale_out),
        )
    ]
    in_shared = swap(in_theirs.astype(jnp.bfloat16), core_bit).astype(jnp.float32)
    out_shared = swap(out_theirs.astype(jnp.bfloat16), core_bit).astype(jnp.float32)
    new_w_in = stepped(w_in, (in_mine + in_shared).T)
    new_w_out = stepped(w_out, (out_mine + out_shared).T)
    near = swaps(
        [total(sum_z, zx, far), total(sum_x, xy), total(sum_y, yz)], (z_bit, x_bit, y_bit)
    )
    sums = total(own, *near)
    early_sum, late_sum = sums[:first], sums[first:]
    half = width // 2
    crossed = []
    for s in range(1, experts):
        rows = late_sum[(s - 1) * capacity : s * capacity]
        crossed.append(
            shifted(jnp.concatenate([rows[:, :half], rows[:, half:]], axis=0), -s)
        )
    crossed = after(crossed, new_w_in, new_w_out)
    own_grad = contract_rows(picks[0], early_sum) + contract_rows(picks[1], late_sum)
    token_grad = unpacked(own_grad.astype(jnp.bfloat16), picks[2:], crossed)
    return (token_grad, new_w_in, new_w_out)


def solution(mesh):
    in_specs = (
        P(("expert", "dp"), None),
        P("dp", "expert", None),
        P(("expert", "dp")),
        P(("expert", "dp")),
        P("dp", "expert"),
        P("dp", "expert"),
    )
    out_specs = (P(("expert", "dp"), None), P("dp", "expert"), P("dp", "expert"))
    return jax.shard_map(shards, mesh=mesh, in_specs=in_specs, out_specs=out_specs, check_vma=False)
```

```python
import jax
import jax.numpy as jnp
from jax import lax
from jax.experimental import pallas as pl
from jax.experimental.pallas import tpu as pltpu
from jax.sharding import PartitionSpec as P

FF = 5120
SHARDS = 16


gelu_coef = 0.7978845608028654
cubic_coef = 0.044715
step_rate = 0.5


def gelu_value(inputs):
    return (
        0.5
        * inputs
        * (1.0 + jnp.tanh(gelu_coef * (inputs + cubic_coef * inputs * inputs * inputs)))
    )


def gelu_slope(inputs):
    tangent = jnp.tanh(gelu_coef * (inputs + cubic_coef * inputs * inputs * inputs))
    return 0.5 * (1.0 + tangent) + 0.5 * inputs * (1.0 - tangent * tangent) * gelu_coef * (
        1.0 + 3.0 * cubic_coef * inputs * inputs
    )


def contract_rows(left, right):
    return lax.dot_general(
        left, right, (((0,), (0,)), ((), ())), preferred_element_type=jnp.float32
    )


def contract_cols(left, right):
    return lax.dot_general(
        left, right, (((1,), (1,)), ((), ())), preferred_element_type=jnp.float32
    )


def summed_grads(attn_partials):
    if lax.axis_size("dp") == 1:
        return attn_partials[0]
    return lax.psum_scatter(attn_partials[0], "dp", scatter_dimension=0, tiled=True)


def picked(pick, source):
    return jnp.dot(pick, source, preferred_element_type=jnp.float32)


def pack_kernel(blocks, experts, ids_ref, gate_ref, tokens_ref, grads_ref, *outs):
    n, width = tokens_ref.shape
    mine = (lax.axis_index("expert") // SHARDS).astype(jnp.float32)
    ids = ids_ref[...].astype(jnp.float32)
    relative = ids - mine
    relative = jnp.where(relative < 0.0, relative + experts, relative)
    down = lax.broadcasted_iota(jnp.int32, (n, n), 0)
    across = lax.broadcasted_iota(jnp.int32, (n, n), 1)
    ids_down = jnp.sum(jnp.where(down == across, ids, 0.0), axis=1, keepdims=True)
    gate_down = jnp.sum(jnp.where(down == across, gate_ref[...], 0.0), axis=1, keepdims=True)
    rivals = jnp.where((ids_down == ids) & (down < across), 1.0, 0.0)
    rank = jnp.sum(rivals, axis=0, keepdims=True)
    tokens = tokens_ref[...]
    gated = (gate_down * grads_ref[...].astype(jnp.float32)).astype(jnp.bfloat16)
    rows, picks = outs[: len(blocks)], outs[len(blocks) : 3 * len(blocks) - 2]
    copies = outs[3 * len(blocks) - 2 :]

    def one_hot(shape, block, shift):
        expert, begin, end, row = block
        chosen = (relative == expert) & (rank >= begin) & (rank < end)
        slot = jnp.where(chosen, rank - begin + row + shift, -1.0).astype(jnp.int32)
        slots = lax.broadcasted_iota(jnp.int32, shape, 0)
        return jnp.where(slots == slot, 1.0, 0.0).astype(jnp.bfloat16)

    for k, block in enumerate(blocks[2:]):
        upper_ref, lower_ref = picks[2 * k + 2], picks[2 * k + 3]
        upper = one_hot(upper_ref.shape, block, 0)
        lower = one_hot(lower_ref.shape, block, block[2])
        upper_ref[...], lower_ref[...] = upper, lower
        both = picked(upper, tokens) + picked(lower, gated)
        rows[k + 2][...] = both.astype(jnp.bfloat16)
    for k, block in enumerate(blocks[:2]):
        pick = one_hot(picks[k].shape, block, 0)
        picks[k][...] = pick
        rows[k][:, :width] = picked(pick, tokens).astype(jnp.bfloat16)
        rows[k][:, width:] = picked(pick, gated).astype(jnp.bfloat16)
    for copy_ref in copies:
        copy_ref[...] = rows[0][...]


def pack(blocks, first, rest, capacity, experts, ids, gate, tokens, grads):
    n, width = tokens.shape
    whole = pl.BlockSpec(memory_space=pltpu.VMEM)
    crossing = len(blocks) - 2

    def shape(rows, columns):
        return jax.ShapeDtypeStruct((rows, columns), jnp.bfloat16)

    shapes = [shape(first, 2 * width), shape(rest, 2 * width)]
    shapes += [shape(2 * capacity, width)] * crossing
    shapes += [shape(first, n), shape(rest, n)] + [shape(2 * capacity, n)] * (2 * crossing)
    shapes += [shape(first, 2 * width)] * len(early_masks)
    outs = pl.pallas_call(
        lambda *refs: pack_kernel(blocks, experts, *refs),
        out_shape=shapes,
        in_specs=[whole] * 4,
        out_specs=[whole] * len(shapes),
    )(ids.reshape(1, n), gate.reshape(1, n), tokens, grads)
    rows, picks = outs[: len(blocks)], outs[len(blocks) : 3 * len(blocks) - 2]
    return rows, picks, outs[3 * len(blocks) - 2 :]


def handed_on(copies, sent):
    anywhere = pl.BlockSpec(memory_space=pl.ANY)
    return pl.pallas_call(
        lambda *refs: None,
        out_shape=[jax.ShapeDtypeStruct(rows.shape, rows.dtype) for rows in copies],
        in_specs=[anywhere] * (len(copies) + len(sent)),
        out_specs=[anywhere] * len(copies),
        input_output_aliases={k: k for k in range(len(copies))},
    )(*copies, *sent)


def whole_weights(shard):
    if lax.axis_size("dp") == 1:
        return shard.astype(jnp.bfloat16)
    return lax.all_gather(shard.astype(jnp.bfloat16), "dp", axis=0, tiled=True)


def stepped(weights, grads):
    if lax.axis_size("dp") > 1:
        grads = lax.psum_scatter(
            grads.astype(jnp.bfloat16), "dp", scatter_dimension=0, tiled=True
        ).astype(jnp.float32)
    return weights - step_rate * grads


def swap(rows, mask):
    n_expert = lax.axis_size("expert")
    return lax.ppermute(rows, "expert", [(i, i ^ mask) for i in range(n_expert)])


core_bit, x_bit, y_bit, z_bit = 1, 2, 4, 8
early_masks = (x_bit, y_bit, z_bit, x_bit | y_bit)


def after(values, *others):
    return lax.optimization_barrier((others, values))[1]


def chain(blocks):
    chained = []
    for block in blocks:
        chained.append(after(block, chained[-1]) if chained else block)
    return chained


def swaps(blocks, masks):
    return [swap(block, mask) for block, mask in zip(chain(blocks), masks)]


def total(*terms):
    return sum(term.astype(jnp.float32) for term in terms).astype(jnp.bfloat16)


def split_rows(array, rows):
    return [array[k : k + rows] for k in range(0, array.shape[0], rows)]


def shards(tokens, attn_partials, expert_ids, gate, w_in, w_out):
    tok_rows, width = tokens.shape
    n_expert = lax.axis_size("expert")
    experts = n_expert // SHARDS
    capacity = 5 * tok_rows // (8 * experts)
    first = capacity // 8 * 8
    rest = experts * capacity - first
    units = w_in.shape[1]
    scale_in = width ** (-0.5)
    scale_out = FF ** (-0.5)

    def shifted(rows, hops):
        pairs = [(i, (i + SHARDS * hops) % n_expert) for i in range(n_expert)]
        return lax.ppermute(rows, "expert", pairs)

    offset = (experts - 1) * capacity - first
    own_blocks = [(0, 0, first, 0), (0, first, capacity, offset + first)]
    cross_blocks = [(s, 0, capacity, 0) for s in range(1, experts)]
    grads = summed_grads(attn_partials)
    (early_own, late_own, *sent), picks, copies = pack(
        own_blocks + cross_blocks, first, rest, capacity, experts, expert_ids, gate, tokens, grads
    )
    early_copies = handed_on(copies, sent)

    def activated(rows):
        expert_rows, grad_rows = rows[:, :width], rows[:, width:]
        pre_act = contract_cols(expert_rows, weights_in) * scale_in
        hidden = gelu_value(pre_act).astype(jnp.bfloat16)
        hidden_grad = contract_cols(grad_rows, weights_out) * scale_out
        pre_grad = (hidden_grad * gelu_slope(pre_act)).astype(jnp.bfloat16)
        return [expert_rows, grad_rows, hidden, pre_grad]

    def input_parts(pre_grad):
        parts = jnp.dot(pre_grad, weights_in, preferred_element_type=jnp.float32) * scale_in
        return parts.astype(jnp.bfloat16)

    for s in range(1, experts):
        side_by_side = jnp.concatenate(split_rows(shifted(sent[s - 1], s), capacity), axis=1)
        late_own = late_own + jnp.pad(
            side_by_side, (((s - 1) * capacity, rest - s * capacity), (0, 0))
        )
    early_x, early_y, early_z, early_xy = after(
        [swap(rows, mask) for rows, mask in zip(early_copies, early_masks)], late_own
    )
    late_x, late_y, late_z = swaps(
        [
            jnp.concatenate([late_own, early_z], axis=0),
            jnp.concatenate([late_own, early_z], axis=0),
            jnp.concatenate([late_own, early_xy], axis=0),
        ],
        (x_bit, y_bit, z_bit),
    )
    early_zx, early_yz, early_far = late_x[rest:], late_y[rest:], late_z[rest:]
    late_x, late_y, late_z = late_x[:rest], late_y[:rest], late_z[:rest]
    early_rows = [early_own, early_x, early_y, early_z, early_xy, early_yz, early_zx, early_far]

    own_weights = jnp.concatenate([whole_weights(w_in).T, whole_weights(w_out).T], axis=0)
    their_weights = swap(after(own_weights, late_own), core_bit)
    weights_in, weights_out = [
        jnp.concatenate([own_weights[part], their_weights[part]], axis=0)
        for part in (slice(0, units), slice(units, 2 * units))
    ]
    late_far, late_zx, late_yz, late_xy = swaps(
        [late_z, late_z, late_y, late_x],
        (x_bit | y_bit, x_bit, z_bit, y_bit),
    )
    early = activated(jnp.concatenate(early_rows, axis=0))
    early_parts = input_parts(early[3])
    late_far = after([late_xy, late_yz, late_zx, late_far], early_parts)
    late_rows = [late_own, late_x, late_y, late_z, *late_far]
    later = activated(jnp.concatenate(late_rows, axis=0))
    late_parts = input_parts(later[3])
    parts = [
        jnp.concatenate(pair, axis=0)
        for pair in zip(split_rows(early_parts, first), split_rows(late_parts, rest))
    ]
    own, sum_x, sum_y, sum_z, sum_xy, sum_yz, sum_zx, sum_far = parts
    back = chain([sum_far, sum_zx, sum_xy, sum_yz])
    far, zx, xy, yz = [
        swap(rows, mask) for rows, mask in zip(back, (x_bit | y_bit, x_bit, y_bit, z_bit))
    ]

    def gradients(part, awaited):
        chunks = [chunk[:2] + after(chunk[2:], awaited) for chunk in (early, later)]
        return [
            sum(contract_rows(chunk[left][:, part], chunk[right]) for chunk in chunks) * scale
            for left, right, scale in ((3, 0, scale_in), (2, 1, scale_out))
        ]

    in_mine, out_mine = gradients(slice(0, units), back[-1])
    zx = after(zx, in_mine, out_mine)
    in_theirs, out_theirs = gradients(slice(units, 2 * units), zx)
    in_shared = swap(in_theirs.astype(jnp.bfloat16), core_bit).astype(jnp.float32)
    out_shared = swap(out_theirs.astype(jnp.bfloat16), core_bit).astype(jnp.float32)
    new_w_in = stepped(w_in, (in_mine + in_shared).T)
    new_w_out = stepped(w_out, (out_mine + out_shared).T)
    near = swaps(
        [total(sum_z, zx, far), total(sum_x, xy), total(sum_y, yz)], (z_bit, x_bit, y_bit)
    )
    sums = total(own, *near)
    early_sum, late_sum = sums[:first], sums[first:]
    half = width // 2
    returned = [early_sum, late_sum]
    for s in range(1, experts):
        rows = late_sum[(s - 1) * capacity : s * capacity]
        rows = jnp.concatenate([rows[:, :half], rows[:, half:]], axis=0)
        rows = after(shifted(rows, -s), new_w_in, new_w_out)
        returned.append(jnp.concatenate(split_rows(rows, capacity), axis=1))
    picks = [*picks[:2], *[pick[:capacity] for pick in picks[2::2]]]
    token_grad = sum(contract_rows(pick, rows) for pick, rows in zip(picks, returned))
    return (token_grad.astype(jnp.bfloat16), new_w_in, new_w_out)


def solution(mesh):
    in_specs = (
        P(("expert", "dp"), None),
        P("dp", "expert", None),
        P(("expert", "dp")),
        P(("expert", "dp")),
        P("dp", "expert"),
        P("dp", "expert"),
    )
    out_specs = (P(("expert", "dp"), None), P("dp", "expert"), P("dp", "expert"))
    return jax.shard_map(shards, mesh=mesh, in_specs=in_specs, out_specs=out_specs, check_vma=False)
```

```python
import jax
import jax.numpy as jnp
from jax import lax
from jax.experimental import pallas as pl
from jax.experimental.pallas import tpu as pltpu
from jax.sharding import PartitionSpec as P

FF = 5120
SHARDS = 16


gelu_coef = 0.7978845608028654
cubic_coef = 0.044715
step_rate = 0.5


def gelu_value(inputs):
    return (
        0.5
        * inputs
        * (1.0 + jnp.tanh(gelu_coef * (inputs + cubic_coef * inputs * inputs * inputs)))
    )


def gelu_slope(inputs):
    tangent = jnp.tanh(gelu_coef * (inputs + cubic_coef * inputs * inputs * inputs))
    return 0.5 * (1.0 + tangent) + 0.5 * inputs * (1.0 - tangent * tangent) * gelu_coef * (
        1.0 + 3.0 * cubic_coef * inputs * inputs
    )


def contract_rows(left, right):
    return lax.dot_general(
        left, right, (((0,), (0,)), ((), ())), preferred_element_type=jnp.float32
    )


def contract_cols(left, right):
    return lax.dot_general(
        left, right, (((1,), (1,)), ((), ())), preferred_element_type=jnp.float32
    )


def summed_grads(attn_partials):
    if lax.axis_size("dp") == 1:
        return attn_partials[0]
    return lax.psum_scatter(attn_partials[0], "dp", scatter_dimension=0, tiled=True)


def picked(pick, source):
    return jnp.dot(pick, source, preferred_element_type=jnp.float32)


def pack_kernel(blocks, experts, ids_ref, gate_ref, tokens_ref, grads_ref, *outs):
    n, width = tokens_ref.shape
    mine = (lax.axis_index("expert") // SHARDS).astype(jnp.float32)
    ids = ids_ref[...].astype(jnp.float32)
    relative = ids - mine
    relative = jnp.where(relative < 0.0, relative + experts, relative)
    down = lax.broadcasted_iota(jnp.int32, (n, n), 0)
    across = lax.broadcasted_iota(jnp.int32, (n, n), 1)
    ids_down = jnp.sum(jnp.where(down == across, ids, 0.0), axis=1, keepdims=True)
    gate_down = jnp.sum(jnp.where(down == across, gate_ref[...], 0.0), axis=1, keepdims=True)
    rivals = jnp.where((ids_down == ids) & (down < across), 1.0, 0.0)
    rank = jnp.sum(rivals, axis=0, keepdims=True)
    tokens = tokens_ref[...]
    gated = (gate_down * grads_ref[...].astype(jnp.float32)).astype(jnp.bfloat16)
    rows, picks = outs[: len(blocks)], outs[len(blocks) : 2 * len(blocks)]
    copies = outs[2 * len(blocks) :]

    def one_hot(shape, block, shift):
        expert, begin, end, row = block
        chosen = (relative == expert) & (rank >= begin) & (rank < end)
        slot = jnp.where(chosen, rank - begin + row + shift, -1.0).astype(jnp.int32)
        slots = lax.broadcasted_iota(jnp.int32, shape, 0)
        return jnp.where(slots == slot, 1.0, 0.0)

    uppers, lowers = [], []
    for k, block in enumerate(blocks):
        shape = picks[k].shape
        uppers.append(one_hot(shape, block, 0))
        lowers.append(uppers[k] if k < 2 else one_hot(shape, block, block[2]))
        picks[k][...] = uppers[k].astype(jnp.bfloat16)
    upper, lower = [jnp.concatenate(p, axis=0).astype(jnp.bfloat16) for p in (uppers, lowers)]
    from_tokens, from_gated = picked(upper, tokens), picked(lower, gated)
    start = 0
    for k, rows_ref in enumerate(rows):
        part = slice(start, start + rows_ref.shape[0])
        start = part.stop
        if k < 2:
            rows_ref[:, :width] = from_tokens[part].astype(jnp.bfloat16)
            rows_ref[:, width:] = from_gated[part].astype(jnp.bfloat16)
        else:
            rows_ref[...] = (from_tokens[part] + from_gated[part]).astype(jnp.bfloat16)
    for copy_ref in copies:
        copy_ref[...] = rows[0][...]


def pack(blocks, first, rest, capacity, experts, ids, gate, tokens, grads):
    n, width = tokens.shape
    whole = pl.BlockSpec(memory_space=pltpu.VMEM)
    crossing = len(blocks) - 2

    def shape(rows, columns):
        return jax.ShapeDtypeStruct((rows, columns), jnp.bfloat16)

    shapes = [shape(first, 2 * width), shape(rest, 2 * width)]
    shapes += [shape(2 * capacity, width)] * crossing
    shapes += [shape(first, n), shape(rest, n)] + [shape(2 * capacity, n)] * crossing
    shapes += [shape(first, 2 * width)] * len(early_masks)
    outs = pl.pallas_call(
        lambda *refs: pack_kernel(blocks, experts, *refs),
        out_shape=shapes,
        in_specs=[whole] * 4,
        out_specs=[whole] * len(shapes),
    )(ids.reshape(1, n), gate.reshape(1, n), tokens, grads)
    return outs[: len(blocks)], outs[len(blocks) : 2 * len(blocks)], outs[2 * len(blocks) :]


def handed_on(copies, sent):
    anywhere = pl.BlockSpec(memory_space=pl.ANY)
    return pl.pallas_call(
        lambda *refs: None,
        out_shape=[jax.ShapeDtypeStruct(rows.shape, rows.dtype) for rows in copies],
        in_specs=[anywhere] * (len(copies) + len(sent)),
        out_specs=[anywhere] * len(copies),
        input_output_aliases={k: k for k in range(len(copies))},
    )(*copies, *sent)


def whole_weights(shard):
    if lax.axis_size("dp") == 1:
        return shard.astype(jnp.bfloat16)
    return lax.all_gather(shard.astype(jnp.bfloat16), "dp", axis=0, tiled=True)


def step_kernel(*refs):
    count = len(refs) // 3
    bases, shares, outs = refs[:count], refs[count : 2 * count], refs[2 * count :]
    rows = outs[0].shape[0]
    part = pl.ds(pl.multiple_of(pl.program_id(0) * rows, rows), rows)
    for base_ref, share_ref, out_ref in zip(bases, shares, outs):
        out_ref[...] = base_ref[part, :] - step_rate * share_ref[part, :].astype(jnp.float32)


def stepped(bases, shares):
    units, width = bases[0].shape
    rows = 64 if units % 64 == 0 else units
    whole = pl.BlockSpec(memory_space=pltpu.VMEM)
    return pl.pallas_call(
        step_kernel,
        grid=(units // rows,),
        out_shape=[jax.ShapeDtypeStruct(base.shape, base.dtype) for base in bases],
        in_specs=[whole] * (2 * len(bases)),
        out_specs=[pl.BlockSpec((rows, width), lambda i: (i, 0))] * len(bases),
        compiler_params=pltpu.CompilerParams(vmem_limit_bytes=32 * 1024 * 1024),
        cost_estimate=pl.CostEstimate(
            flops=4 * units * width, bytes_accessed=8 * units * width, transcendentals=0
        ),
    )(*bases, *shares)


def stepped_over_dp(weights, grads):
    grads = lax.psum_scatter(
        grads.astype(jnp.bfloat16), "dp", scatter_dimension=0, tiled=True
    ).astype(jnp.float32)
    return weights - step_rate * grads


def swap(rows, mask):
    n_expert = lax.axis_size("expert")
    return lax.ppermute(rows, "expert", [(i, i ^ mask) for i in range(n_expert)])


core_bit, x_bit, y_bit, z_bit = 1, 2, 4, 8
early_masks = (x_bit | y_bit, z_bit, x_bit, y_bit)


def after(values, *others):
    return lax.optimization_barrier((others, values))[1]


def chain(blocks):
    chained = []
    for block in blocks:
        chained.append(after(block, chained[-1]) if chained else block)
    return chained


def swaps(blocks, masks):
    return [swap(block, mask) for block, mask in zip(chain(blocks), masks)]


def total(*terms):
    return sum(term.astype(jnp.float32) for term in terms).astype(jnp.bfloat16)


def split_rows(array, rows):
    return [array[k : k + rows] for k in range(0, array.shape[0], rows)]


def shards(tokens, attn_partials, expert_ids, gate, w_in, w_out):
    tok_rows, width = tokens.shape
    n_expert = lax.axis_size("expert")
    experts = n_expert // SHARDS
    capacity = 5 * tok_rows // (8 * experts)
    first = capacity // 8 * 8
    rest = experts * capacity - first
    units = w_in.shape[1]
    scale_in = width ** (-0.5)
    scale_out = FF ** (-0.5)

    def shifted(rows, hops):
        pairs = [(i, (i + SHARDS * hops) % n_expert) for i in range(n_expert)]
        return lax.ppermute(rows, "expert", pairs)

    offset = (experts - 1) * capacity - first
    own_blocks = [(0, 0, first, 0), (0, first, capacity, offset + first)]
    cross_blocks = [(s, 0, capacity, 0) for s in range(1, experts)]
    grads = summed_grads(attn_partials)
    (early_own, late_own, *sent), picks, copies = pack(
        own_blocks + cross_blocks, first, rest, capacity, experts, expert_ids, gate, tokens, grads
    )
    early_copies = handed_on(copies, sent)

    def activated(rows):
        expert_rows, grad_rows = rows[:, :width], rows[:, width:]
        pre_act = contract_cols(expert_rows, weights_in) * scale_in
        hidden = gelu_value(pre_act).astype(jnp.bfloat16)
        hidden_grad = contract_cols(grad_rows, weights_out) * scale_out
        pre_grad = (hidden_grad * gelu_slope(pre_act)).astype(jnp.bfloat16)
        return [expert_rows, grad_rows, hidden, pre_grad]

    def input_parts(pre_grad):
        parts = jnp.dot(pre_grad, weights_in, preferred_element_type=jnp.float32) * scale_in
        return parts.astype(jnp.bfloat16)

    for s in range(1, experts):
        side_by_side = jnp.concatenate(split_rows(shifted(sent[s - 1], s), capacity), axis=1)
        late_own = late_own + jnp.pad(
            side_by_side, (((s - 1) * capacity, rest - s * capacity), (0, 0))
        )
    early_xy, early_z, early_x, early_y = after(
        [swap(rows, mask) for rows, mask in zip(early_copies, early_masks)], late_own
    )
    late_x, late_y, late_z = swaps(
        [
            jnp.concatenate([late_own, early_z], axis=0),
            jnp.concatenate([late_own, early_z], axis=0),
            jnp.concatenate([late_own, early_xy], axis=0),
        ],
        (x_bit, y_bit, z_bit),
    )
    early_zx, early_yz, early_far = late_x[rest:], late_y[rest:], late_z[rest:]
    late_x, late_y, late_z = late_x[:rest], late_y[:rest], late_z[:rest]
    early_rows = [early_own, early_x, early_y, early_z, early_xy, early_yz, early_zx, early_far]

    own_weights = jnp.concatenate([whole_weights(w_in).T, whole_weights(w_out).T], axis=0)
    their_weights = swap(after(own_weights, late_own), core_bit)
    weights_in, weights_out = [
        jnp.concatenate([own_weights[part], their_weights[part]], axis=0)
        for part in (slice(0, units), slice(units, 2 * units))
    ]
    late_far, late_zx, late_yz, late_xy = swaps(
        [late_z, late_z, late_y, late_x],
        (x_bit | y_bit, x_bit, z_bit, y_bit),
    )
    early = activated(jnp.concatenate(early_rows, axis=0))
    early_parts = input_parts(early[3])
    late_far = after([late_xy, late_yz, late_zx, late_far], early_parts)
    late_rows = [late_own, late_x, late_y, late_z, *late_far]
    later = activated(jnp.concatenate(late_rows, axis=0))
    late_parts = input_parts(later[3])
    parts = [
        jnp.concatenate(pair, axis=0)
        for pair in zip(split_rows(early_parts, first), split_rows(late_parts, rest))
    ]
    own, sum_x, sum_y, sum_z, sum_xy, sum_yz, sum_zx, sum_far = parts
    back = chain([sum_far, sum_zx, sum_xy, sum_yz])
    far, zx, xy, yz = [
        swap(rows, mask) for rows, mask in zip(back, (x_bit | y_bit, x_bit, y_bit, z_bit))
    ]

    def gradients(part, awaited):
        chunks = [chunk[:2] + after(chunk[2:], awaited) for chunk in (early, later)]
        return [
            sum(contract_rows(chunk[left][:, part], chunk[right]) for chunk in chunks) * scale
            for left, right, scale in ((3, 0, scale_in), (2, 1, scale_out))
        ]

    mine = gradients(slice(0, units), back[-1])
    split_width = lax.axis_size("dp") > 1
    if not split_width:
        mine = [weights.T - step_rate * grads for weights, grads in zip((w_in, w_out), mine)]
    zx = after(zx, mine)
    theirs = gradients(slice(units, 2 * units), zx)
    shares = [swap(grads.astype(jnp.bfloat16), core_bit) for grads in theirs]
    if split_width:
        new_weights = [
            stepped_over_dp(weights, (grads + share.astype(jnp.float32)).T)
            for weights, grads, share in zip((w_in, w_out), mine, shares)
        ]
    else:
        new_weights = [weights.T for weights in stepped(mine, shares)]
    near = swaps(
        [total(sum_z, zx, far), total(sum_x, xy), total(sum_y, yz)], (z_bit, x_bit, y_bit)
    )
    sums = total(own, *near)
    early_sum, late_sum = sums[:first], sums[first:]
    half = width // 2
    returned = [early_sum, late_sum]
    for s in range(1, experts):
        rows = late_sum[(s - 1) * capacity : s * capacity]
        rows = jnp.concatenate([rows[:, :half], rows[:, half:]], axis=0)
        rows = after(shifted(rows, -s), new_weights)
        returned.append(jnp.concatenate(split_rows(rows, capacity), axis=1))
    picks = [*picks[:2], *[pick[:capacity] for pick in picks[2:]]]
    token_grad = sum(contract_rows(pick, rows) for pick, rows in zip(picks, returned))
    return (token_grad.astype(jnp.bfloat16), *new_weights)


def solution(mesh):
    in_specs = (
        P(("expert", "dp"), None),
        P("dp", "expert", None),
        P(("expert", "dp")),
        P(("expert", "dp")),
        P("dp", "expert"),
        P("dp", "expert"),
    )
    out_specs = (P(("expert", "dp"), None), P("dp", "expert"), P("dp", "expert"))
    return jax.shard_map(shards, mesh=mesh, in_specs=in_specs, out_specs=out_specs, check_vma=False)
```

```python
import jax
import jax.numpy as jnp
from jax import lax
from jax.experimental import pallas as pl
from jax.experimental.pallas import tpu as pltpu
from jax.sharding import PartitionSpec as P

FF = 5120
SHARDS = 16


gelu_coef = 0.7978845608028654
cubic_coef = 0.044715
step_rate = 0.5


def gelu_value(inputs):
    return (
        0.5
        * inputs
        * (1.0 + jnp.tanh(gelu_coef * (inputs + cubic_coef * inputs * inputs * inputs)))
    )


def gelu_slope(inputs):
    tangent = jnp.tanh(gelu_coef * (inputs + cubic_coef * inputs * inputs * inputs))
    return 0.5 * (1.0 + tangent) + 0.5 * inputs * (1.0 - tangent * tangent) * gelu_coef * (
        1.0 + 3.0 * cubic_coef * inputs * inputs
    )


def contract_rows(left, right):
    return lax.dot_general(
        left, right, (((0,), (0,)), ((), ())), preferred_element_type=jnp.float32
    )


def contract_cols(left, right):
    return lax.dot_general(
        left, right, (((1,), (1,)), ((), ())), preferred_element_type=jnp.float32
    )


def summed_grads(attn_partials):
    if lax.axis_size("dp") == 1:
        return attn_partials[0]
    return lax.psum_scatter(attn_partials[0], "dp", scatter_dimension=0, tiled=True)


def picked(pick, source):
    return jnp.dot(pick, source, preferred_element_type=jnp.float32)


def pack_kernel(blocks, experts, ids_ref, gate_ref, tokens_ref, grads_ref, *outs):
    n, width = tokens_ref.shape
    mine = (lax.axis_index("expert") // SHARDS).astype(jnp.float32)
    ids = ids_ref[...].astype(jnp.float32)
    relative = ids - mine
    relative = jnp.where(relative < 0.0, relative + experts, relative)
    down = lax.broadcasted_iota(jnp.int32, (n, n), 0)
    across = lax.broadcasted_iota(jnp.int32, (n, n), 1)
    ids_down = jnp.sum(jnp.where(down == across, ids, 0.0), axis=1, keepdims=True)
    gate_down = jnp.sum(jnp.where(down == across, gate_ref[...], 0.0), axis=1, keepdims=True)
    rivals = jnp.where((ids_down == ids) & (down < across), 1.0, 0.0)
    rank = jnp.sum(rivals, axis=0, keepdims=True)
    tokens = tokens_ref[...]
    gated = (gate_down * grads_ref[...].astype(jnp.float32)).astype(jnp.bfloat16)
    rows, picks = outs[: len(blocks)], outs[len(blocks) : 2 * len(blocks)]
    copies = outs[2 * len(blocks) :]

    def one_hot(shape, block, shift):
        expert, begin, end, row = block
        chosen = (relative == expert) & (rank >= begin) & (rank < end)
        slot = jnp.where(chosen, rank - begin + row + shift, -1.0).astype(jnp.int32)
        slots = lax.broadcasted_iota(jnp.int32, shape, 0)
        return jnp.where(slots == slot, 1.0, 0.0)

    uppers, lowers = [], []
    for k, block in enumerate(blocks):
        shape = picks[k].shape
        uppers.append(one_hot(shape, block, 0))
        lowers.append(uppers[k] if k < 2 else one_hot(shape, block, block[2]))
        picks[k][...] = uppers[k].astype(jnp.bfloat16)
    upper, lower = [jnp.concatenate(p, axis=0).astype(jnp.bfloat16) for p in (uppers, lowers)]
    from_tokens, from_gated = picked(upper, tokens), picked(lower, gated)
    start = 0
    for k, rows_ref in enumerate(rows):
        part = slice(start, start + rows_ref.shape[0])
        start = part.stop
        if k < 2:
            rows_ref[:, :width] = from_tokens[part].astype(jnp.bfloat16)
            rows_ref[:, width:] = from_gated[part].astype(jnp.bfloat16)
        else:
            rows_ref[...] = (from_tokens[part] + from_gated[part]).astype(jnp.bfloat16)
    for copy_ref in copies:
        copy_ref[...] = rows[0][...]


def pack(blocks, first, rest, capacity, experts, ids, gate, tokens, grads):
    n, width = tokens.shape
    whole = pl.BlockSpec(memory_space=pltpu.VMEM)
    crossing = len(blocks) - 2

    def shape(rows, columns):
        return jax.ShapeDtypeStruct((rows, columns), jnp.bfloat16)

    shapes = [shape(first, 2 * width), shape(rest, 2 * width)]
    shapes += [shape(2 * capacity, width)] * crossing
    shapes += [shape(first, n), shape(rest, n)] + [shape(2 * capacity, n)] * crossing
    shapes += [shape(first, 2 * width)] * len(early_masks)
    outs = pl.pallas_call(
        lambda *refs: pack_kernel(blocks, experts, *refs),
        out_shape=shapes,
        in_specs=[whole] * 4,
        out_specs=[whole] * len(shapes),
    )(ids.reshape(1, n), gate.reshape(1, n), tokens, grads)
    return outs[: len(blocks)], outs[len(blocks) : 2 * len(blocks)], outs[2 * len(blocks) :]


def handed_on(copies, sent):
    anywhere = pl.BlockSpec(memory_space=pl.ANY)
    return pl.pallas_call(
        lambda *refs: None,
        out_shape=[jax.ShapeDtypeStruct(rows.shape, rows.dtype) for rows in copies],
        in_specs=[anywhere] * (len(copies) + len(sent)),
        out_specs=[anywhere] * len(copies),
        input_output_aliases={k: k for k in range(len(copies))},
    )(*copies, *sent)


def whole_weights(shard):
    if lax.axis_size("dp") == 1:
        return shard.astype(jnp.bfloat16)
    return lax.all_gather(shard.astype(jnp.bfloat16), "dp", axis=0, tiled=True)


def step_kernel(base_ref, share_ref, out_ref):
    rows = out_ref.shape[0]
    part = pl.ds(pl.multiple_of(pl.program_id(0) * rows, rows), rows)
    out_ref[...] = base_ref[part, :] - step_rate * share_ref[part, :].astype(jnp.float32)


def stepped(base, share):
    units, width = base.shape
    rows = 64 if units % 64 == 0 else units
    whole = pl.BlockSpec(memory_space=pltpu.VMEM)
    return pl.pallas_call(
        step_kernel,
        grid=(units // rows,),
        out_shape=jax.ShapeDtypeStruct(base.shape, base.dtype),
        in_specs=[whole] * 2,
        out_specs=pl.BlockSpec((rows, width), lambda i: (i, 0)),
        compiler_params=pltpu.CompilerParams(vmem_limit_bytes=32 * 1024 * 1024),
        cost_estimate=pl.CostEstimate(
            flops=2 * units * width, bytes_accessed=4 * units * width, transcendentals=0
        ),
    )(base, share)


def stepped_over_dp(weights, grads):
    grads = lax.psum_scatter(
        grads.astype(jnp.bfloat16), "dp", scatter_dimension=0, tiled=True
    ).astype(jnp.float32)
    return weights - step_rate * grads


def swap(rows, mask):
    n_expert = lax.axis_size("expert")
    return lax.ppermute(rows, "expert", [(i, i ^ mask) for i in range(n_expert)])


core_bit, x_bit, y_bit, z_bit = 1, 2, 4, 8
early_masks = (x_bit | y_bit, z_bit, x_bit, y_bit)


def after(values, *others):
    return lax.optimization_barrier((others, values))[1]


def chain(blocks):
    chained = []
    for block in blocks:
        chained.append(after(block, chained[-1]) if chained else block)
    return chained


def swaps(blocks, masks):
    return [swap(block, mask) for block, mask in zip(chain(blocks), masks)]


def total(*terms):
    return sum(term.astype(jnp.float32) for term in terms).astype(jnp.bfloat16)


def split_rows(array, rows):
    return [array[k : k + rows] for k in range(0, array.shape[0], rows)]


def shards(tokens, attn_partials, expert_ids, gate, w_in, w_out):
    tok_rows, width = tokens.shape
    n_expert = lax.axis_size("expert")
    experts = n_expert // SHARDS
    capacity = 5 * tok_rows // (8 * experts)
    first = capacity // 8 * 8
    rest = experts * capacity - first
    units = w_in.shape[1]
    scale_in = width ** (-0.5)
    scale_out = FF ** (-0.5)

    def shifted(rows, hops):
        pairs = [(i, (i + SHARDS * hops) % n_expert) for i in range(n_expert)]
        return lax.ppermute(rows, "expert", pairs)

    offset = (experts - 1) * capacity - first
    own_blocks = [(0, 0, first, 0), (0, first, capacity, offset + first)]
    cross_blocks = [(s, 0, capacity, 0) for s in range(1, experts)]
    grads = summed_grads(attn_partials)
    (early_own, late_own, *sent), picks, copies = pack(
        own_blocks + cross_blocks, first, rest, capacity, experts, expert_ids, gate, tokens, grads
    )
    early_copies = handed_on(copies, sent)

    def activated(rows):
        expert_rows, grad_rows = rows[:, :width], rows[:, width:]
        pre_act = contract_cols(expert_rows, weights_in) * scale_in
        hidden = gelu_value(pre_act).astype(jnp.bfloat16)
        hidden_grad = contract_cols(grad_rows, weights_out) * scale_out
        pre_grad = (hidden_grad * gelu_slope(pre_act)).astype(jnp.bfloat16)
        return [expert_rows, grad_rows, hidden, pre_grad]

    def input_parts(pre_grad):
        parts = jnp.dot(pre_grad, weights_in, preferred_element_type=jnp.float32) * scale_in
        return parts.astype(jnp.bfloat16)

    for s in range(1, experts):
        side_by_side = jnp.concatenate(split_rows(shifted(sent[s - 1], s), capacity), axis=1)
        late_own = late_own + jnp.pad(
            side_by_side, (((s - 1) * capacity, rest - s * capacity), (0, 0))
        )
    early_xy, early_z, early_x, early_y = after(
        [swap(rows, mask) for rows, mask in zip(early_copies, early_masks)], late_own
    )
    late_x, late_y, late_z = swaps(
        [
            jnp.concatenate([late_own, early_z], axis=0),
            jnp.concatenate([late_own, early_z], axis=0),
            late_own,
        ],
        (x_bit, y_bit, z_bit),
    )
    early_zx, early_yz = late_x[rest:], late_y[rest:]
    late_x, late_y = late_x[:rest], late_y[:rest]
    early_rows = [early_own, early_x, early_y, early_z, early_xy, early_yz, early_zx]

    own_weights = jnp.concatenate([whole_weights(w_in).T, whole_weights(w_out).T], axis=0)
    their_weights = swap(after(own_weights, late_own), core_bit)
    weights_in, weights_out = [
        jnp.concatenate([own_weights[part], their_weights[part]], axis=0)
        for part in (slice(0, units), slice(units, 2 * units))
    ]
    late_xy, late_yz, late_far, late_zx = swaps(
        [late_x, jnp.concatenate([late_y, early_xy], axis=0), late_z, late_z],
        (y_bit, z_bit, x_bit | y_bit, x_bit),
    )
    early = activated(jnp.concatenate(early_rows, axis=0))
    early_parts = input_parts(early[3])
    late_xy, late_yz, late_zx, late_far = after(
        [late_xy, late_yz, late_zx, late_far], early_parts
    )
    late_yz, early_far = late_yz[:rest], late_yz[rest:]
    late_rows = [late_own, late_x, late_y, late_z, late_xy, late_yz, late_zx, late_far, early_far]
    later = activated(jnp.concatenate(late_rows, axis=0))
    late_parts = input_parts(later[3])
    parts = [
        jnp.concatenate(pair, axis=0)
        for pair in zip(
            [*split_rows(early_parts, first), late_parts[8 * rest :]],
            split_rows(late_parts[: 8 * rest], rest),
        )
    ]
    own, sum_x, sum_y, sum_z, sum_xy, sum_yz, sum_zx, sum_far = parts
    back = chain([sum_far, sum_yz, sum_zx, sum_xy])
    far, yz, zx, xy = [
        swap(rows, mask) for rows, mask in zip(back, (x_bit | y_bit, z_bit, x_bit, y_bit))
    ]

    def gradients(part, awaited):
        chunks = [chunk[:2] + after(chunk[2:], awaited) for chunk in (early, later)]
        return [
            sum(contract_rows(chunk[left][:, part], chunk[right]) for chunk in chunks) * scale
            for left, right, scale in ((3, 0, scale_in), (2, 1, scale_out))
        ]

    mine = gradients(slice(0, units), back[-1])
    split_width = lax.axis_size("dp") > 1
    if not split_width:
        mine = [weights.T - step_rate * grads for weights, grads in zip((w_in, w_out), mine)]
    zx = after(zx, mine)
    theirs = gradients(slice(units, 2 * units), zx)
    shares = [swap(grads.astype(jnp.bfloat16), core_bit) for grads in theirs]
    if split_width:
        new_weights = [
            stepped_over_dp(weights, (grads + share.astype(jnp.float32)).T)
            for weights, grads, share in zip((w_in, w_out), mine, shares)
        ]
    else:
        new_weights = [stepped(base, share).T for base, share in zip(mine, shares)]
    near = swaps(
        [total(sum_y, yz), total(sum_z, zx, far), total(sum_x, xy)], (y_bit, z_bit, x_bit)
    )
    sums = total(own, *near)
    early_sum, late_sum = sums[:first], sums[first:]
    half = width // 2
    returned = [early_sum, late_sum]
    for s in range(1, experts):
        rows = late_sum[(s - 1) * capacity : s * capacity]
        rows = jnp.concatenate([rows[:, :half], rows[:, half:]], axis=0)
        rows = after(shifted(rows, -s), new_weights)
        returned.append(jnp.concatenate(split_rows(rows, capacity), axis=1))
    picks = [*picks[:2], *[pick[:capacity] for pick in picks[2:]]]
    token_grad = sum(contract_rows(pick, rows) for pick, rows in zip(picks, returned))
    return (token_grad.astype(jnp.bfloat16), *new_weights)


def solution(mesh):
    in_specs = (
        P(("expert", "dp"), None),
        P("dp", "expert", None),
        P(("expert", "dp")),
        P(("expert", "dp")),
        P("dp", "expert"),
        P("dp", "expert"),
    )
    out_specs = (P(("expert", "dp"), None), P("dp", "expert"), P("dp", "expert"))
    return jax.shard_map(shards, mesh=mesh, in_specs=in_specs, out_specs=out_specs, check_vma=False)
```

```python
import jax
import jax.numpy as jnp
from jax import lax
from jax.experimental import pallas as pl
from jax.experimental.pallas import tpu as pltpu
from jax.sharding import PartitionSpec as P

FF = 5120
SHARDS = 16


gelu_coef = 0.7978845608028654
cubic_coef = 0.044715
step_rate = 0.5


def gelu_value(inputs):
    return (
        0.5
        * inputs
        * (1.0 + jnp.tanh(gelu_coef * (inputs + cubic_coef * inputs * inputs * inputs)))
    )


def gelu_slope(inputs):
    tangent = jnp.tanh(gelu_coef * (inputs + cubic_coef * inputs * inputs * inputs))
    return 0.5 * (1.0 + tangent) + 0.5 * inputs * (1.0 - tangent * tangent) * gelu_coef * (
        1.0 + 3.0 * cubic_coef * inputs * inputs
    )


def contract_rows(left, right):
    return lax.dot_general(
        left, right, (((0,), (0,)), ((), ())), preferred_element_type=jnp.float32
    )


def contract_cols(left, right):
    return lax.dot_general(
        left, right, (((1,), (1,)), ((), ())), preferred_element_type=jnp.float32
    )


def summed_grads(attn_partials):
    if lax.axis_size("dp") == 1:
        return attn_partials[0]
    return lax.psum_scatter(attn_partials[0], "dp", scatter_dimension=0, tiled=True)


def picked(pick, source):
    return jnp.dot(pick, source, preferred_element_type=jnp.float32)


def pack_kernel(blocks, experts, ids_ref, gate_ref, tokens_ref, grads_ref, *outs):
    n, width = tokens_ref.shape
    mine = (lax.axis_index("expert") // SHARDS).astype(jnp.float32)
    ids = ids_ref[...].astype(jnp.float32)
    relative = ids - mine
    relative = jnp.where(relative < 0.0, relative + experts, relative)
    down = lax.broadcasted_iota(jnp.int32, (n, n), 0)
    across = lax.broadcasted_iota(jnp.int32, (n, n), 1)
    ids_down = jnp.sum(jnp.where(down == across, ids, 0.0), axis=1, keepdims=True)
    gate_down = jnp.sum(jnp.where(down == across, gate_ref[...], 0.0), axis=1, keepdims=True)
    rivals = jnp.where((ids_down == ids) & (down < across), 1.0, 0.0)
    rank = jnp.sum(rivals, axis=0, keepdims=True)
    tokens = tokens_ref[...]
    gated = (gate_down * grads_ref[...].astype(jnp.float32)).astype(jnp.bfloat16)
    rows, picks = outs[: len(blocks)], outs[len(blocks) : 2 * len(blocks)]
    copies = outs[2 * len(blocks) :]

    def one_hot(shape, block, shift):
        expert, begin, end, row = block
        chosen = (relative == expert) & (rank >= begin) & (rank < end)
        slot = jnp.where(chosen, rank - begin + row + shift, -1.0).astype(jnp.int32)
        slots = lax.broadcasted_iota(jnp.int32, shape, 0)
        return jnp.where(slots == slot, 1.0, 0.0)

    uppers, lowers = [], []
    for k, block in enumerate(blocks):
        shape = picks[k].shape
        uppers.append(one_hot(shape, block, 0))
        lowers.append(uppers[k] if k < 2 else one_hot(shape, block, block[2]))
        picks[k][...] = uppers[k].astype(jnp.bfloat16)
    upper, lower = [jnp.concatenate(p, axis=0).astype(jnp.bfloat16) for p in (uppers, lowers)]
    from_tokens, from_gated = picked(upper, tokens), picked(lower, gated)
    start = 0
    for k, rows_ref in enumerate(rows):
        part = slice(start, start + rows_ref.shape[0])
        start = part.stop
        if k < 2:
            rows_ref[:, :width] = from_tokens[part].astype(jnp.bfloat16)
            rows_ref[:, width:] = from_gated[part].astype(jnp.bfloat16)
        else:
            rows_ref[...] = (from_tokens[part] + from_gated[part]).astype(jnp.bfloat16)
    for copy_ref in copies:
        copy_ref[...] = rows[0][...]


def pack(blocks, first, rest, capacity, experts, ids, gate, tokens, grads):
    n, width = tokens.shape
    whole = pl.BlockSpec(memory_space=pltpu.VMEM)
    crossing = len(blocks) - 2

    def shape(rows, columns):
        return jax.ShapeDtypeStruct((rows, columns), jnp.bfloat16)

    shapes = [shape(first, 2 * width), shape(rest, 2 * width)]
    shapes += [shape(2 * capacity, width)] * crossing
    shapes += [shape(first, n), shape(rest, n)] + [shape(2 * capacity, n)] * crossing
    shapes += [shape(first, 2 * width)] * len(early_masks)
    outs = pl.pallas_call(
        lambda *refs: pack_kernel(blocks, experts, *refs),
        out_shape=shapes,
        in_specs=[whole] * 4,
        out_specs=[whole] * len(shapes),
        compiler_params=pltpu.CompilerParams(vmem_limit_bytes=8 * 1024 * 1024),
    )(ids.reshape(1, n), gate.reshape(1, n), tokens, grads)
    return outs[: len(blocks)], outs[len(blocks) : 2 * len(blocks)], outs[2 * len(blocks) :]


def handed_on(copies, sent):
    anywhere = pl.BlockSpec(memory_space=pl.ANY)
    return pl.pallas_call(
        lambda *refs: None,
        out_shape=[jax.ShapeDtypeStruct(rows.shape, rows.dtype) for rows in copies],
        in_specs=[anywhere] * (len(copies) + len(sent)),
        out_specs=[anywhere] * len(copies),
        input_output_aliases={k: k for k in range(len(copies))},
        compiler_params=pltpu.CompilerParams(vmem_limit_bytes=1024 * 1024),
    )(*copies, *sent)


def whole_weights(shard):
    if lax.axis_size("dp") == 1:
        return shard.astype(jnp.bfloat16)
    return lax.all_gather(shard.astype(jnp.bfloat16), "dp", axis=0, tiled=True)


def step_kernel(*refs):
    count = len(refs) // 3
    bases, shares, outs = refs[:count], refs[count : 2 * count], refs[2 * count :]
    rows = outs[0].shape[0]
    part = pl.ds(pl.multiple_of(pl.program_id(0) * rows, rows), rows)
    for base_ref, share_ref, out_ref in zip(bases, shares, outs):
        out_ref[...] = base_ref[part, :] - step_rate * share_ref[part, :].astype(jnp.float32)


def stepped(bases, shares):
    units, width = bases[0].shape
    rows = 64 if units % 64 == 0 else units
    whole = pl.BlockSpec(memory_space=pltpu.VMEM)
    return pl.pallas_call(
        step_kernel,
        grid=(units // rows,),
        out_shape=[jax.ShapeDtypeStruct(base.shape, base.dtype) for base in bases],
        in_specs=[whole] * (2 * len(bases)),
        out_specs=[pl.BlockSpec((rows, width), lambda i: (i, 0))] * len(bases),
        compiler_params=pltpu.CompilerParams(vmem_limit_bytes=14 * 1024 * 1024),
        cost_estimate=pl.CostEstimate(
            flops=4 * units * width, bytes_accessed=8 * units * width, transcendentals=0
        ),
    )(*bases, *shares)


def stepped_over_dp(weights, grads):
    grads = lax.psum_scatter(
        grads.astype(jnp.bfloat16), "dp", scatter_dimension=0, tiled=True
    ).astype(jnp.float32)
    return weights - step_rate * grads


def swap(rows, mask):
    n_expert = lax.axis_size("expert")
    return lax.ppermute(rows, "expert", [(i, i ^ mask) for i in range(n_expert)])


core_bit, x_bit, y_bit, z_bit = 1, 2, 4, 8
early_masks = (x_bit | y_bit, z_bit, x_bit, y_bit)


def after(values, *others):
    return lax.optimization_barrier((others, values))[1]


def chain(blocks):
    chained = []
    for block in blocks:
        chained.append(after(block, chained[-1]) if chained else block)
    return chained


def swaps(blocks, masks):
    return [swap(block, mask) for block, mask in zip(chain(blocks), masks)]


def total(*terms):
    return sum(term.astype(jnp.float32) for term in terms).astype(jnp.bfloat16)


def split_rows(array, rows):
    return [array[k : k + rows] for k in range(0, array.shape[0], rows)]


def shards(tokens, attn_partials, expert_ids, gate, w_in, w_out):
    tok_rows, width = tokens.shape
    n_expert = lax.axis_size("expert")
    experts = n_expert // SHARDS
    capacity = 5 * tok_rows // (8 * experts)
    first = capacity // 8 * 8
    rest = experts * capacity - first
    units = w_in.shape[1]
    scale_in = width ** (-0.5)
    scale_out = FF ** (-0.5)

    def shifted(rows, hops):
        pairs = [(i, (i + SHARDS * hops) % n_expert) for i in range(n_expert)]
        return lax.ppermute(rows, "expert", pairs)

    offset = (experts - 1) * capacity - first
    own_blocks = [(0, 0, first, 0), (0, first, capacity, offset + first)]
    cross_blocks = [(s, 0, capacity, 0) for s in range(1, experts)]
    grads = summed_grads(attn_partials)
    (early_own, late_own, *sent), picks, copies = pack(
        own_blocks + cross_blocks, first, rest, capacity, experts, expert_ids, gate, tokens, grads
    )
    early_copies = handed_on(copies, sent)

    def activated(rows):
        expert_rows, grad_rows = rows[:, :width], rows[:, width:]
        pre_act = contract_cols(expert_rows, weights_in) * scale_in
        hidden = gelu_value(pre_act).astype(jnp.bfloat16)
        hidden_grad = contract_cols(grad_rows, weights_out) * scale_out
        pre_grad = (hidden_grad * gelu_slope(pre_act)).astype(jnp.bfloat16)
        return [expert_rows, grad_rows, hidden, pre_grad]

    def input_parts(pre_grad):
        parts = jnp.dot(pre_grad, weights_in, preferred_element_type=jnp.float32) * scale_in
        return parts.astype(jnp.bfloat16)

    for s in range(1, experts):
        side_by_side = jnp.concatenate(split_rows(shifted(sent[s - 1], s), capacity), axis=1)
        late_own = late_own + jnp.pad(
            side_by_side, (((s - 1) * capacity, rest - s * capacity), (0, 0))
        )
    early_xy, early_z, early_x, early_y = after(
        [swap(rows, mask) for rows, mask in zip(early_copies, early_masks)], late_own
    )
    late_x, late_y, late_z = swaps(
        [
            jnp.concatenate([late_own, early_z], axis=0),
            jnp.concatenate([late_own, early_z], axis=0),
            jnp.concatenate([late_own, early_xy], axis=0),
        ],
        (x_bit, y_bit, z_bit),
    )
    early_zx, early_yz, early_far = late_x[rest:], late_y[rest:], late_z[rest:]
    late_x, late_y, late_z = late_x[:rest], late_y[:rest], late_z[:rest]
    early_rows = [early_own, early_x, early_y, early_z, early_xy, early_yz, early_zx, early_far]

    own_weights = jnp.concatenate([whole_weights(w_in).T, whole_weights(w_out).T], axis=0)
    their_weights = swap(after(own_weights, late_own), core_bit)
    weights_in, weights_out = [
        jnp.concatenate([own_weights[part], their_weights[part]], axis=0)
        for part in (slice(0, units), slice(units, 2 * units))
    ]
    late_far, late_zx, late_yz, late_xy = swaps(
        [late_z, late_z, late_y, late_x],
        (x_bit | y_bit, x_bit, z_bit, y_bit),
    )
    early = activated(jnp.concatenate(early_rows, axis=0))
    early_parts = input_parts(early[3])
    late_far = after([late_xy, late_yz, late_zx, late_far], early_parts)
    late_rows = [late_own, late_x, late_y, late_z, *late_far]
    later = activated(jnp.concatenate(late_rows, axis=0))
    late_parts = input_parts(later[3])
    parts = [
        jnp.concatenate(pair, axis=0)
        for pair in zip(split_rows(early_parts, first), split_rows(late_parts, rest))
    ]
    own, sum_x, sum_y, sum_z, sum_xy, sum_yz, sum_zx, sum_far = parts
    back = chain([sum_far, sum_zx, sum_xy, sum_yz])
    far, zx, xy, yz = [
        swap(rows, mask) for rows, mask in zip(back, (x_bit | y_bit, x_bit, y_bit, z_bit))
    ]

    def gradients(part, awaited):
        chunks = [chunk[:2] + after(chunk[2:], awaited) for chunk in (early, later)]
        return [
            sum(contract_rows(chunk[left][:, part], chunk[right]) for chunk in chunks) * scale
            for left, right, scale in ((3, 0, scale_in), (2, 1, scale_out))
        ]

    mine = gradients(slice(0, units), back[-1])
    split_width = lax.axis_size("dp") > 1
    if not split_width:
        mine = [weights.T - step_rate * grads for weights, grads in zip((w_in, w_out), mine)]
    zx = after(zx, mine)
    theirs = gradients(slice(units, 2 * units), zx)
    shares = [swap(grads.astype(jnp.bfloat16), core_bit) for grads in theirs]
    if split_width:
        new_weights = [
            stepped_over_dp(weights, (grads + share.astype(jnp.float32)).T)
            for weights, grads, share in zip((w_in, w_out), mine, shares)
        ]
    else:
        new_weights = [weights.T for weights in stepped(mine, shares)]
    near = swaps(
        [total(sum_z, zx, far), total(sum_x, xy), total(sum_y, yz)], (z_bit, x_bit, y_bit)
    )
    sums = total(own, *near)
    early_sum, late_sum = sums[:first], sums[first:]
    half = width // 2
    returned = [early_sum, late_sum]
    for s in range(1, experts):
        rows = late_sum[(s - 1) * capacity : s * capacity]
        rows = jnp.concatenate([rows[:, :half], rows[:, half:]], axis=0)
        rows = after(shifted(rows, -s), new_weights)
        returned.append(jnp.concatenate(split_rows(rows, capacity), axis=1))
    picks = [*picks[:2], *[pick[:capacity] for pick in picks[2:]]]
    token_grad = sum(contract_rows(pick, rows) for pick, rows in zip(picks, returned))
    return (token_grad.astype(jnp.bfloat16), *new_weights)


def solution(mesh):
    in_specs = (
        P(("expert", "dp"), None),
        P("dp", "expert", None),
        P(("expert", "dp")),
        P(("expert", "dp")),
        P("dp", "expert"),
        P("dp", "expert"),
    )
    out_specs = (P(("expert", "dp"), None), P("dp", "expert"), P("dp", "expert"))
    return jax.shard_map(shards, mesh=mesh, in_specs=in_specs, out_specs=out_specs, check_vma=False)
```

```python
import jax
import jax.numpy as jnp
from jax import lax
from jax.experimental import pallas as pl
from jax.experimental.pallas import tpu as pltpu
from jax.sharding import PartitionSpec as P

FF = 5120
SHARDS = 16


gelu_coef = 0.7978845608028654
cubic_coef = 0.044715
step_rate = 0.5


def gelu_value(inputs):
    return (
        0.5
        * inputs
        * (1.0 + jnp.tanh(gelu_coef * (inputs + cubic_coef * inputs * inputs * inputs)))
    )


def gelu_slope(inputs):
    tangent = jnp.tanh(gelu_coef * (inputs + cubic_coef * inputs * inputs * inputs))
    return 0.5 * (1.0 + tangent) + 0.5 * inputs * (1.0 - tangent * tangent) * gelu_coef * (
        1.0 + 3.0 * cubic_coef * inputs * inputs
    )


def contract_rows(left, right):
    return lax.dot_general(
        left, right, (((0,), (0,)), ((), ())), preferred_element_type=jnp.float32
    )


def contract_cols(left, right):
    return lax.dot_general(
        left, right, (((1,), (1,)), ((), ())), preferred_element_type=jnp.float32
    )


def summed_grads(attn_partials):
    if lax.axis_size("dp") == 1:
        return attn_partials[0]
    return lax.psum_scatter(attn_partials[0], "dp", scatter_dimension=0, tiled=True)


def picked(pick, source):
    return jnp.dot(pick, source, preferred_element_type=jnp.float32)


def pack_kernel(blocks, experts, *refs):
    sources, (*outs, ids_ref, gate_ref, tokens_ref, grads_ref, sems) = refs[:4], refs[4:]
    fetches = [
        pltpu.make_async_copy(source, target, sems.at[k])
        for k, (source, target) in enumerate(
            zip(sources, (ids_ref, gate_ref, tokens_ref, grads_ref))
        )
    ]
    for fetch in fetches:
        fetch.start()
    for fetch in fetches:
        fetch.wait()
    n, width = tokens_ref.shape
    mine = (lax.axis_index("expert") // SHARDS).astype(jnp.float32)
    ids = ids_ref[...].astype(jnp.float32)
    relative = ids - mine
    relative = jnp.where(relative < 0.0, relative + experts, relative)
    down = lax.broadcasted_iota(jnp.int32, (n, n), 0)
    across = lax.broadcasted_iota(jnp.int32, (n, n), 1)
    ids_down = jnp.sum(jnp.where(down == across, ids, 0.0), axis=1, keepdims=True)
    gate_down = jnp.sum(jnp.where(down == across, gate_ref[...], 0.0), axis=1, keepdims=True)
    rivals = jnp.where((ids_down == ids) & (down < across), 1.0, 0.0)
    rank = jnp.sum(rivals, axis=0, keepdims=True)
    tokens = tokens_ref[...]
    gated = (gate_down * grads_ref[...].astype(jnp.float32)).astype(jnp.bfloat16)
    rows, picks = outs[: len(blocks)], outs[len(blocks) : 2 * len(blocks)]
    copies = outs[2 * len(blocks) :]

    def one_hot(shape, block, shift):
        expert, begin, end, row = block
        chosen = (relative == expert) & (rank >= begin) & (rank < end)
        slot = jnp.where(chosen, rank - begin + row + shift, -1.0).astype(jnp.int32)
        slots = lax.broadcasted_iota(jnp.int32, shape, 0)
        return jnp.where(slots == slot, 1.0, 0.0)

    uppers, lowers = [], []
    for k, block in enumerate(blocks):
        shape = picks[k].shape
        uppers.append(one_hot(shape, block, 0))
        lowers.append(uppers[k] if k < 2 else one_hot(shape, block, block[2]))
        picks[k][...] = uppers[k].astype(jnp.bfloat16)
    upper, lower = [jnp.concatenate(p, axis=0).astype(jnp.bfloat16) for p in (uppers, lowers)]
    from_tokens, from_gated = picked(upper, tokens), picked(lower, gated)
    start = 0
    for k, rows_ref in enumerate(rows):
        part = slice(start, start + rows_ref.shape[0])
        start = part.stop
        if k < 2:
            rows_ref[:, :width] = from_tokens[part].astype(jnp.bfloat16)
            rows_ref[:, width:] = from_gated[part].astype(jnp.bfloat16)
        else:
            rows_ref[...] = (from_tokens[part] + from_gated[part]).astype(jnp.bfloat16)
    for copy_ref in copies:
        copy_ref[...] = rows[0][...]


def pack(blocks, first, rest, capacity, experts, ids, gate, tokens, grads):
    n, width = tokens.shape
    whole = pl.BlockSpec(memory_space=pltpu.VMEM)
    crossing = len(blocks) - 2

    def shape(rows, columns):
        return jax.ShapeDtypeStruct((rows, columns), jnp.bfloat16)

    shapes = [shape(first, 2 * width), shape(rest, 2 * width)]
    shapes += [shape(2 * capacity, width)] * crossing
    shapes += [shape(first, n), shape(rest, n)] + [shape(2 * capacity, n)] * crossing
    shapes += [shape(first, 2 * width)] * len(early_masks)
    outs = pl.pallas_call(
        lambda *refs: pack_kernel(blocks, experts, *refs),
        out_shape=shapes,
        in_specs=[pl.BlockSpec(memory_space=pltpu.HBM)] * 4,
        out_specs=[whole] * len(shapes),
        scratch_shapes=[
            pltpu.VMEM((1, n), jnp.int32),
            pltpu.VMEM((1, n), jnp.float32),
            pltpu.VMEM((n, width), jnp.bfloat16),
            pltpu.VMEM((n, width), jnp.bfloat16),
            pltpu.SemaphoreType.DMA((4,)),
        ],
        compiler_params=pltpu.CompilerParams(vmem_limit_bytes=8 * 1024 * 1024),
    )(ids.reshape(1, n), gate.reshape(1, n), tokens, grads)
    return outs[: len(blocks)], outs[len(blocks) : 2 * len(blocks)], outs[2 * len(blocks) :]


def handed_on(copies, sent):
    anywhere = pl.BlockSpec(memory_space=pl.ANY)
    return pl.pallas_call(
        lambda *refs: None,
        out_shape=[jax.ShapeDtypeStruct(rows.shape, rows.dtype) for rows in copies],
        in_specs=[anywhere] * (len(copies) + len(sent)),
        out_specs=[anywhere] * len(copies),
        input_output_aliases={k: k for k in range(len(copies))},
        compiler_params=pltpu.CompilerParams(vmem_limit_bytes=1024 * 1024),
    )(*copies, *sent)


def whole_weights(shard):
    if lax.axis_size("dp") == 1:
        return shard.astype(jnp.bfloat16)
    return lax.all_gather(shard.astype(jnp.bfloat16), "dp", axis=0, tiled=True)


def step_kernel(rows, *refs):
    *refs, done_ref, sems = refs
    count = len(refs) // 3
    bases, shares, outs = refs[:count], refs[count : 2 * count], refs[2 * count :]
    writes = []
    for start in range(0, outs[0].shape[0], rows):
        part = slice(start, start + rows)
        for k in range(count):
            done_ref[k, part] = bases[k][part] - step_rate * shares[k][part].astype(jnp.float32)
            writes.append(
                pltpu.make_async_copy(done_ref.at[k, part], outs[k].at[part], sems.at[len(writes)])
            )
            writes[-1].start()
    for write in writes:
        write.wait()


def stepped(bases, shares):
    units, width = bases[0].shape
    rows = 64 if units % 64 == 0 else units
    whole = pl.BlockSpec(memory_space=pltpu.VMEM)
    return pl.pallas_call(
        lambda *refs: step_kernel(rows, *refs),
        out_shape=[jax.ShapeDtypeStruct(base.shape, base.dtype) for base in bases],
        in_specs=[whole] * (2 * len(bases)),
        out_specs=[pl.BlockSpec(memory_space=pltpu.HBM)] * len(bases),
        scratch_shapes=[
            pltpu.VMEM((len(bases), units, width), jnp.float32),
            pltpu.SemaphoreType.DMA((len(bases) * (units // rows),)),
        ],
        compiler_params=pltpu.CompilerParams(vmem_limit_bytes=16 * 1024 * 1024),
        cost_estimate=pl.CostEstimate(
            flops=4 * units * width, bytes_accessed=8 * units * width, transcendentals=0
        ),
    )(*bases, *shares)


def stepped_over_dp(weights, grads):
    grads = lax.psum_scatter(
        grads.astype(jnp.bfloat16), "dp", scatter_dimension=0, tiled=True
    ).astype(jnp.float32)
    return weights - step_rate * grads


def swap(rows, mask):
    n_expert = lax.axis_size("expert")
    return lax.ppermute(rows, "expert", [(i, i ^ mask) for i in range(n_expert)])


core_bit, x_bit, y_bit, z_bit = 1, 2, 4, 8
early_masks = (x_bit | y_bit, z_bit, x_bit, y_bit)


def after(values, *others):
    return lax.optimization_barrier((others, values))[1]


def chain(blocks):
    chained = []
    for block in blocks:
        chained.append(after(block, chained[-1]) if chained else block)
    return chained


def swaps(blocks, masks):
    return [swap(block, mask) for block, mask in zip(chain(blocks), masks)]


def total(*terms):
    return sum(term.astype(jnp.float32) for term in terms).astype(jnp.bfloat16)


def split_rows(array, rows):
    return [array[k : k + rows] for k in range(0, array.shape[0], rows)]


def shards(tokens, attn_partials, expert_ids, gate, w_in, w_out):
    tok_rows, width = tokens.shape
    n_expert = lax.axis_size("expert")
    experts = n_expert // SHARDS
    capacity = 5 * tok_rows // (8 * experts)
    first = capacity // 8 * 8
    rest = experts * capacity - first
    units = w_in.shape[1]
    scale_in = width ** (-0.5)
    scale_out = FF ** (-0.5)

    def shifted(rows, hops):
        pairs = [(i, (i + SHARDS * hops) % n_expert) for i in range(n_expert)]
        return lax.ppermute(rows, "expert", pairs)

    offset = (experts - 1) * capacity - first
    own_blocks = [(0, 0, first, 0), (0, first, capacity, offset + first)]
    cross_blocks = [(s, 0, capacity, 0) for s in range(1, experts)]
    grads = summed_grads(attn_partials)
    (early_own, late_own, *sent), picks, copies = pack(
        own_blocks + cross_blocks, first, rest, capacity, experts, expert_ids, gate, tokens, grads
    )
    early_copies = handed_on(copies, sent)

    def activated(rows):
        expert_rows, grad_rows = rows[:, :width], rows[:, width:]
        pre_act = contract_cols(expert_rows, weights_in) * scale_in
        hidden = gelu_value(pre_act).astype(jnp.bfloat16)
        hidden_grad = contract_cols(grad_rows, weights_out) * scale_out
        pre_grad = (hidden_grad * gelu_slope(pre_act)).astype(jnp.bfloat16)
        return [expert_rows, grad_rows, hidden, pre_grad]

    def input_parts(pre_grad):
        parts = jnp.dot(pre_grad, weights_in, preferred_element_type=jnp.float32) * scale_in
        return parts.astype(jnp.bfloat16)

    for s in range(1, experts):
        side_by_side = jnp.concatenate(split_rows(shifted(sent[s - 1], s), capacity), axis=1)
        late_own = late_own + jnp.pad(
            side_by_side, (((s - 1) * capacity, rest - s * capacity), (0, 0))
        )
    early_xy, early_z, early_x, early_y = after(
        [swap(rows, mask) for rows, mask in zip(early_copies, early_masks)], late_own
    )
    late_x, late_y, late_z = swaps(
        [
            jnp.concatenate([late_own, early_z], axis=0),
            jnp.concatenate([late_own, early_z], axis=0),
            jnp.concatenate([late_own, early_xy], axis=0),
        ],
        (x_bit, y_bit, z_bit),
    )
    early_zx, early_yz, early_far = late_x[rest:], late_y[rest:], late_z[rest:]
    late_x, late_y, late_z = late_x[:rest], late_y[:rest], late_z[:rest]
    early_rows = [early_own, early_x, early_y, early_z, early_xy, early_yz, early_zx, early_far]

    own_weights = jnp.concatenate([whole_weights(w_in).T, whole_weights(w_out).T], axis=0)
    their_weights = swap(after(own_weights, late_own), core_bit)
    weights_in, weights_out = [
        jnp.concatenate([own_weights[part], their_weights[part]], axis=0)
        for part in (slice(0, units), slice(units, 2 * units))
    ]
    late_far, late_zx, late_yz, late_xy = swaps(
        [late_z, late_z, late_y, late_x],
        (x_bit | y_bit, x_bit, z_bit, y_bit),
    )
    early = activated(jnp.concatenate(early_rows, axis=0))
    early_parts = input_parts(early[3])
    late_far = after([late_xy, late_yz, late_zx, late_far], early_parts)
    late_rows = [late_own, late_x, late_y, late_z, *late_far]
    later = activated(jnp.concatenate(late_rows, axis=0))
    late_parts = input_parts(later[3])
    parts = [
        jnp.concatenate(pair, axis=0)
        for pair in zip(split_rows(early_parts, first), split_rows(late_parts, rest))
    ]
    own, sum_x, sum_y, sum_z, sum_xy, sum_yz, sum_zx, sum_far = parts
    back = chain([sum_far, sum_zx, sum_xy, sum_yz])
    far, zx, xy, yz = [
        swap(rows, mask) for rows, mask in zip(back, (x_bit | y_bit, x_bit, y_bit, z_bit))
    ]

    def gradients(part, awaited):
        chunks = [chunk[:2] + after(chunk[2:], awaited) for chunk in (early, later)]
        return [
            sum(contract_rows(chunk[left][:, part], chunk[right]) for chunk in chunks) * scale
            for left, right, scale in ((3, 0, scale_in), (2, 1, scale_out))
        ]

    mine = gradients(slice(0, units), back[-1])
    split_width = lax.axis_size("dp") > 1
    if not split_width:
        mine = [weights.T - step_rate * grads for weights, grads in zip((w_in, w_out), mine)]
    zx = after(zx, mine)
    theirs = gradients(slice(units, 2 * units), zx)
    shares = [swap(grads.astype(jnp.bfloat16), core_bit) for grads in theirs]
    if split_width:
        new_weights = [
            stepped_over_dp(weights, (grads + share.astype(jnp.float32)).T)
            for weights, grads, share in zip((w_in, w_out), mine, shares)
        ]
    else:
        new_weights = [weights.T for weights in stepped(mine, shares)]
    near = swaps(
        [total(sum_z, zx, far), total(sum_x, xy), total(sum_y, yz)], (z_bit, x_bit, y_bit)
    )
    sums = total(own, *near)
    early_sum, late_sum = sums[:first], sums[first:]
    half = width // 2
    returned = [early_sum, late_sum]
    for s in range(1, experts):
        rows = late_sum[(s - 1) * capacity : s * capacity]
        rows = jnp.concatenate([rows[:, :half], rows[:, half:]], axis=0)
        rows = after(shifted(rows, -s), new_weights)
        returned.append(jnp.concatenate(split_rows(rows, capacity), axis=1))
    picks = [*picks[:2], *[pick[:capacity] for pick in picks[2:]]]
    token_grad = sum(contract_rows(pick, rows) for pick, rows in zip(picks, returned))
    return (token_grad.astype(jnp.bfloat16), *new_weights)


def solution(mesh):
    in_specs = (
        P(("expert", "dp"), None),
        P("dp", "expert", None),
        P(("expert", "dp")),
        P(("expert", "dp")),
        P("dp", "expert"),
        P("dp", "expert"),
    )
    out_specs = (P(("expert", "dp"), None), P("dp", "expert"), P("dp", "expert"))
    return jax.shard_map(shards, mesh=mesh, in_specs=in_specs, out_specs=out_specs, check_vma=False)
```

```python
import jax
import jax.numpy as jnp
from jax import lax
from jax.experimental import pallas as pl
from jax.experimental.pallas import tpu as pltpu
from jax.sharding import PartitionSpec as P

FF = 5120
SHARDS = 16


gelu_coef = 0.7978845608028654
cubic_coef = 0.044715
step_rate = 0.5


def gelu_value(inputs):
    return (
        0.5
        * inputs
        * (1.0 + jnp.tanh(gelu_coef * (inputs + cubic_coef * inputs * inputs * inputs)))
    )


def gelu_slope(inputs):
    tangent = jnp.tanh(gelu_coef * (inputs + cubic_coef * inputs * inputs * inputs))
    return 0.5 * (1.0 + tangent) + 0.5 * inputs * (1.0 - tangent * tangent) * gelu_coef * (
        1.0 + 3.0 * cubic_coef * inputs * inputs
    )


def contract_rows(left, right):
    return lax.dot_general(
        left, right, (((0,), (0,)), ((), ())), preferred_element_type=jnp.float32
    )


def contract_cols(left, right):
    return lax.dot_general(
        left, right, (((1,), (1,)), ((), ())), preferred_element_type=jnp.float32
    )


def summed_grads(attn_partials):
    if lax.axis_size("dp") == 1:
        return attn_partials[0]
    return lax.psum_scatter(attn_partials[0], "dp", scatter_dimension=0, tiled=True)


def picked(pick, source):
    return jnp.dot(pick, source, preferred_element_type=jnp.float32)


def pack_kernel(blocks, experts, *refs):
    sources, (*outs, ids_ref, gate_ref, tokens_ref, grads_ref, sems) = refs[:4], refs[4:]
    fetches = [
        pltpu.make_async_copy(source, target, sems.at[k])
        for k, (source, target) in enumerate(
            zip(sources, (ids_ref, gate_ref, tokens_ref, grads_ref))
        )
    ]
    for fetch in fetches:
        fetch.start()
    for fetch in fetches:
        fetch.wait()
    n, width = tokens_ref.shape
    mine = (lax.axis_index("expert") // SHARDS).astype(jnp.float32)
    ids = ids_ref[...].astype(jnp.float32)
    relative = ids - mine
    relative = jnp.where(relative < 0.0, relative + experts, relative)
    down = lax.broadcasted_iota(jnp.int32, (n, n), 0)
    across = lax.broadcasted_iota(jnp.int32, (n, n), 1)
    ids_down = jnp.sum(jnp.where(down == across, ids, 0.0), axis=1, keepdims=True)
    gate_down = jnp.sum(jnp.where(down == across, gate_ref[...], 0.0), axis=1, keepdims=True)
    rivals = jnp.where((ids_down == ids) & (down < across), 1.0, 0.0)
    rank = jnp.sum(rivals, axis=0, keepdims=True)
    tokens = tokens_ref[...]
    gated = (gate_down * grads_ref[...].astype(jnp.float32)).astype(jnp.bfloat16)
    rows, picks = outs[: len(blocks)], outs[len(blocks) : 2 * len(blocks)]
    copies = outs[2 * len(blocks) :]

    def one_hot(shape, block, shift):
        expert, begin, end, row = block
        chosen = (relative == expert) & (rank >= begin) & (rank < end)
        slot = jnp.where(chosen, rank - begin + row + shift, -1.0).astype(jnp.int32)
        slots = lax.broadcasted_iota(jnp.int32, shape, 0)
        return jnp.where(slots == slot, 1.0, 0.0)

    uppers, lowers = [], []
    for k, block in enumerate(blocks):
        shape = picks[k].shape
        uppers.append(one_hot(shape, block, 0))
        lowers.append(uppers[k] if k < 2 else one_hot(shape, block, block[2]))
        picks[k][...] = uppers[k].astype(jnp.bfloat16)
    upper, lower = [jnp.concatenate(p, axis=0).astype(jnp.bfloat16) for p in (uppers, lowers)]
    from_tokens, from_gated = picked(upper, tokens), picked(lower, gated)
    start = 0
    for k, rows_ref in enumerate(rows):
        part = slice(start, start + rows_ref.shape[0])
        start = part.stop
        if k < 2:
            rows_ref[:, :width] = from_tokens[part].astype(jnp.bfloat16)
            rows_ref[:, width:] = from_gated[part].astype(jnp.bfloat16)
        else:
            rows_ref[...] = (from_tokens[part] + from_gated[part]).astype(jnp.bfloat16)
    for copy_ref in copies:
        copy_ref[...] = rows[0][...]


def pack(blocks, first, rest, capacity, experts, ids, gate, tokens, grads):
    n, width = tokens.shape
    whole = pl.BlockSpec(memory_space=pltpu.VMEM)
    crossing = len(blocks) - 2

    def shape(rows, columns):
        return jax.ShapeDtypeStruct((rows, columns), jnp.bfloat16)

    shapes = [shape(first, 2 * width), shape(rest, 2 * width)]
    shapes += [shape(2 * capacity, width)] * crossing
    shapes += [shape(first, n), shape(rest, n)] + [shape(2 * capacity, n)] * crossing
    shapes += [shape(first, 2 * width)] * len(early_masks)
    sources = (ids.reshape(1, n), gate.reshape(1, n), tokens, grads)
    outs = pl.pallas_call(
        lambda *refs: pack_kernel(blocks, experts, *refs),
        out_shape=shapes,
        in_specs=[pl.BlockSpec(memory_space=pltpu.HBM)] * 4,
        out_specs=[whole] * len(shapes),
        scratch_shapes=[
            pltpu.VMEM((1, n), jnp.int32),
            pltpu.VMEM((1, n), jnp.float32),
            pltpu.VMEM((n, width), jnp.bfloat16),
            pltpu.VMEM((n, width), jnp.bfloat16),
            pltpu.SemaphoreType.DMA((4,)),
        ],
        compiler_params=pltpu.CompilerParams(vmem_limit_bytes=8 * 1024 * 1024),
    )(*[pltpu.with_memory_space_constraint(source, pltpu.HBM) for source in sources])
    return outs[: len(blocks)], outs[len(blocks) : 2 * len(blocks)], outs[2 * len(blocks) :]


def handed_on(copies, sent):
    anywhere = pl.BlockSpec(memory_space=pl.ANY)
    return pl.pallas_call(
        lambda *refs: None,
        out_shape=[jax.ShapeDtypeStruct(rows.shape, rows.dtype) for rows in copies],
        in_specs=[anywhere] * (len(copies) + len(sent)),
        out_specs=[anywhere] * len(copies),
        input_output_aliases={k: k for k in range(len(copies))},
        compiler_params=pltpu.CompilerParams(vmem_limit_bytes=1024 * 1024),
    )(*copies, *sent)


def whole_weights(shard):
    if lax.axis_size("dp") == 1:
        return shard.astype(jnp.bfloat16)
    return lax.all_gather(shard.astype(jnp.bfloat16), "dp", axis=0, tiled=True)


def step_kernel(rows, *refs):
    *refs, done_ref, sems = refs
    count = len(refs) // 3
    bases, shares, outs = refs[:count], refs[count : 2 * count], refs[2 * count :]
    writes = []
    for start in range(0, outs[0].shape[0], rows):
        part = slice(start, start + rows)
        for k in range(count):
            done_ref[k, part] = bases[k][part] - step_rate * shares[k][part].astype(jnp.float32)
            writes.append(
                pltpu.make_async_copy(done_ref.at[k, part], outs[k].at[part], sems.at[len(writes)])
            )
            writes[-1].start()
    for write in writes:
        write.wait()


def stepped(bases, shares):
    units, width = bases[0].shape
    rows = 64 if units % 64 == 0 else units
    whole = pl.BlockSpec(memory_space=pltpu.VMEM)
    return pl.pallas_call(
        lambda *refs: step_kernel(rows, *refs),
        out_shape=[jax.ShapeDtypeStruct(base.shape, base.dtype) for base in bases],
        in_specs=[whole] * (2 * len(bases)),
        out_specs=[pl.BlockSpec(memory_space=pltpu.HBM)] * len(bases),
        scratch_shapes=[
            pltpu.VMEM((len(bases), units, width), jnp.float32),
            pltpu.SemaphoreType.DMA((len(bases) * (units // rows),)),
        ],
        compiler_params=pltpu.CompilerParams(vmem_limit_bytes=16 * 1024 * 1024),
        cost_estimate=pl.CostEstimate(
            flops=4 * units * width, bytes_accessed=8 * units * width, transcendentals=0
        ),
    )(*bases, *shares)


def stepped_over_dp(weights, grads):
    grads = lax.psum_scatter(
        grads.astype(jnp.bfloat16), "dp", scatter_dimension=0, tiled=True
    ).astype(jnp.float32)
    return weights - step_rate * grads


def swap(rows, mask):
    n_expert = lax.axis_size("expert")
    return lax.ppermute(rows, "expert", [(i, i ^ mask) for i in range(n_expert)])


core_bit, x_bit, y_bit, z_bit = 1, 2, 4, 8
early_masks = (x_bit | y_bit, z_bit, x_bit, y_bit)


def after(values, *others):
    return lax.optimization_barrier((others, values))[1]


def chain(blocks):
    chained = []
    for block in blocks:
        chained.append(after(block, chained[-1]) if chained else block)
    return chained


def swaps(blocks, masks):
    return [swap(block, mask) for block, mask in zip(chain(blocks), masks)]


def total(*terms):
    return sum(term.astype(jnp.float32) for term in terms).astype(jnp.bfloat16)


def split_rows(array, rows):
    return [array[k : k + rows] for k in range(0, array.shape[0], rows)]


def shards(tokens, attn_partials, expert_ids, gate, w_in, w_out):
    tok_rows, width = tokens.shape
    n_expert = lax.axis_size("expert")
    experts = n_expert // SHARDS
    capacity = 5 * tok_rows // (8 * experts)
    first = capacity // 8 * 8
    rest = experts * capacity - first
    units = w_in.shape[1]
    scale_in = width ** (-0.5)
    scale_out = FF ** (-0.5)

    def shifted(rows, hops):
        pairs = [(i, (i + SHARDS * hops) % n_expert) for i in range(n_expert)]
        return lax.ppermute(rows, "expert", pairs)

    offset = (experts - 1) * capacity - first
    own_blocks = [(0, 0, first, 0), (0, first, capacity, offset + first)]
    cross_blocks = [(s, 0, capacity, 0) for s in range(1, experts)]
    grads = summed_grads(attn_partials)
    (early_own, late_own, *sent), picks, copies = pack(
        own_blocks + cross_blocks, first, rest, capacity, experts, expert_ids, gate, tokens, grads
    )
    early_copies = handed_on(copies, sent)

    def activated(rows):
        expert_rows, grad_rows = rows[:, :width], rows[:, width:]
        pre_act = contract_cols(expert_rows, weights_in) * scale_in
        hidden = gelu_value(pre_act).astype(jnp.bfloat16)
        hidden_grad = contract_cols(grad_rows, weights_out) * scale_out
        pre_grad = (hidden_grad * gelu_slope(pre_act)).astype(jnp.bfloat16)
        return [expert_rows, grad_rows, hidden, pre_grad]

    def input_parts(pre_grad):
        parts = jnp.dot(pre_grad, weights_in, preferred_element_type=jnp.float32) * scale_in
        return parts.astype(jnp.bfloat16)

    for s in range(1, experts):
        side_by_side = jnp.concatenate(split_rows(shifted(sent[s - 1], s), capacity), axis=1)
        late_own = late_own + jnp.pad(
            side_by_side, (((s - 1) * capacity, rest - s * capacity), (0, 0))
        )
    early_xy, early_z, early_x, early_y = after(
        [swap(rows, mask) for rows, mask in zip(early_copies, early_masks)], late_own
    )
    late_x, late_y, late_z = swaps(
        [
            jnp.concatenate([late_own, early_z], axis=0),
            jnp.concatenate([late_own, early_z], axis=0),
            jnp.concatenate([late_own, early_xy], axis=0),
        ],
        (x_bit, y_bit, z_bit),
    )
    early_zx, early_yz, early_far = late_x[rest:], late_y[rest:], late_z[rest:]
    late_x, late_y, late_z = late_x[:rest], late_y[:rest], late_z[:rest]
    early_rows = [early_own, early_x, early_y, early_z, early_xy, early_yz, early_zx, early_far]

    own_weights = jnp.concatenate([whole_weights(w_in).T, whole_weights(w_out).T], axis=0)
    their_weights = swap(after(own_weights, late_own), core_bit)
    weights_in, weights_out = [
        jnp.concatenate([own_weights[part], their_weights[part]], axis=0)
        for part in (slice(0, units), slice(units, 2 * units))
    ]
    late_far, late_zx, late_yz, late_xy = swaps(
        [late_z, late_z, late_y, late_x],
        (x_bit | y_bit, x_bit, z_bit, y_bit),
    )
    early = activated(jnp.concatenate(early_rows, axis=0))
    early_parts = input_parts(early[3])
    late_far = after([late_xy, late_yz, late_zx, late_far], early_parts)
    late_rows = [late_own, late_x, late_y, late_z, *late_far]
    later = activated(jnp.concatenate(late_rows, axis=0))
    late_parts = input_parts(later[3])
    parts = [
        jnp.concatenate(pair, axis=0)
        for pair in zip(split_rows(early_parts, first), split_rows(late_parts, rest))
    ]
    own, sum_x, sum_y, sum_z, sum_xy, sum_yz, sum_zx, sum_far = parts
    back = chain([sum_far, sum_zx, sum_xy, sum_yz])
    far, zx, xy, yz = [
        swap(rows, mask) for rows, mask in zip(back, (x_bit | y_bit, x_bit, y_bit, z_bit))
    ]

    def gradients(part, awaited):
        chunks = [chunk[:2] + after(chunk[2:], awaited) for chunk in (early, later)]
        return [
            sum(contract_rows(chunk[left][:, part], chunk[right]) for chunk in chunks) * scale
            for left, right, scale in ((3, 0, scale_in), (2, 1, scale_out))
        ]

    mine = gradients(slice(0, units), back[-1])
    split_width = lax.axis_size("dp") > 1
    if not split_width:
        mine = [weights.T - step_rate * grads for weights, grads in zip((w_in, w_out), mine)]
    zx = after(zx, mine)
    theirs = gradients(slice(units, 2 * units), zx)
    shares = [swap(grads.astype(jnp.bfloat16), core_bit) for grads in theirs]
    if split_width:
        new_weights = [
            stepped_over_dp(weights, (grads + share.astype(jnp.float32)).T)
            for weights, grads, share in zip((w_in, w_out), mine, shares)
        ]
    else:
        new_weights = [weights.T for weights in stepped(mine, shares)]
    near = swaps(
        [total(sum_z, zx, far), total(sum_x, xy), total(sum_y, yz)], (z_bit, x_bit, y_bit)
    )
    sums = total(own, *near)
    early_sum, late_sum = sums[:first], sums[first:]
    half = width // 2
    returned = [early_sum, late_sum]
    for s in range(1, experts):
        rows = late_sum[(s - 1) * capacity : s * capacity]
        rows = jnp.concatenate([rows[:, :half], rows[:, half:]], axis=0)
        rows = after(shifted(rows, -s), new_weights)
        returned.append(jnp.concatenate(split_rows(rows, capacity), axis=1))
    picks = [*picks[:2], *[pick[:capacity] for pick in picks[2:]]]
    token_grad = sum(contract_rows(pick, rows) for pick, rows in zip(picks, returned))
    return (token_grad.astype(jnp.bfloat16), *new_weights)


def solution(mesh):
    in_specs = (
        P(("expert", "dp"), None),
        P("dp", "expert", None),
        P(("expert", "dp")),
        P(("expert", "dp")),
        P("dp", "expert"),
        P("dp", "expert"),
    )
    out_specs = (P(("expert", "dp"), None), P("dp", "expert"), P("dp", "expert"))
    return jax.shard_map(shards, mesh=mesh, in_specs=in_specs, out_specs=out_specs, check_vma=False)
```

```python
import jax
import jax.numpy as jnp
from jax import lax
from jax.experimental import pallas as pl
from jax.experimental.pallas import tpu as pltpu
from jax.sharding import PartitionSpec as P

FF = 5120
SHARDS = 16


gelu_coef = 0.7978845608028654
cubic_coef = 0.044715
step_rate = 0.5


def gelu_value(inputs):
    return (
        0.5
        * inputs
        * (1.0 + jnp.tanh(gelu_coef * (inputs + cubic_coef * inputs * inputs * inputs)))
    )


def gelu_slope(inputs):
    tangent = jnp.tanh(gelu_coef * (inputs + cubic_coef * inputs * inputs * inputs))
    return 0.5 * (1.0 + tangent) + 0.5 * inputs * (1.0 - tangent * tangent) * gelu_coef * (
        1.0 + 3.0 * cubic_coef * inputs * inputs
    )


def contract_rows(left, right):
    return lax.dot_general(
        left, right, (((0,), (0,)), ((), ())), preferred_element_type=jnp.float32
    )


def contract_cols(left, right):
    return lax.dot_general(
        left, right, (((1,), (1,)), ((), ())), preferred_element_type=jnp.float32
    )


def summed_grads(attn_partials):
    if lax.axis_size("dp") == 1:
        return attn_partials[0]
    return lax.psum_scatter(attn_partials[0], "dp", scatter_dimension=0, tiled=True)


def picked(pick, source):
    return jnp.dot(pick, source, preferred_element_type=jnp.float32)


def pack_kernel(blocks, experts, *refs):
    sources, (*outs, ids_ref, gate_ref, tokens_ref, grads_ref, sems) = refs[:4], refs[4:]
    fetches = [
        pltpu.make_async_copy(source, target, sems.at[k])
        for k, (source, target) in enumerate(
            zip(sources, (ids_ref, gate_ref, tokens_ref, grads_ref))
        )
    ]
    for fetch in fetches:
        fetch.start()
    for fetch in fetches[:2]:
        fetch.wait()
    n, width = tokens_ref.shape
    mine = (lax.axis_index("expert") // SHARDS).astype(jnp.float32)
    ids = ids_ref[...].astype(jnp.float32)
    relative = ids - mine
    relative = jnp.where(relative < 0.0, relative + experts, relative)
    down = lax.broadcasted_iota(jnp.int32, (n, n), 0)
    across = lax.broadcasted_iota(jnp.int32, (n, n), 1)
    ids_down = jnp.sum(jnp.where(down == across, ids, 0.0), axis=1, keepdims=True)
    gate_down = jnp.sum(jnp.where(down == across, gate_ref[...], 0.0), axis=1, keepdims=True)
    rivals = jnp.where((ids_down == ids) & (down < across), 1.0, 0.0)
    rank = jnp.sum(rivals, axis=0, keepdims=True)
    rows, picks = outs[: len(blocks)], outs[len(blocks) : 2 * len(blocks)]
    copies = outs[2 * len(blocks) :]

    def one_hot(shape, block, shift):
        expert, begin, end, row = block
        chosen = (relative == expert) & (rank >= begin) & (rank < end)
        slot = jnp.where(chosen, rank - begin + row + shift, -1.0).astype(jnp.int32)
        slots = lax.broadcasted_iota(jnp.int32, shape, 0)
        return jnp.where(slots == slot, 1.0, 0.0)

    uppers, lowers = [], []
    for k, block in enumerate(blocks):
        shape = picks[k].shape
        uppers.append(one_hot(shape, block, 0))
        lowers.append(uppers[k] if k < 2 else one_hot(shape, block, block[2]))
        picks[k][...] = uppers[k].astype(jnp.bfloat16)
    upper, lower = [jnp.concatenate(p, axis=0).astype(jnp.bfloat16) for p in (uppers, lowers)]
    for fetch in fetches[2:]:
        fetch.wait()
    gated = (gate_down * grads_ref[...].astype(jnp.float32)).astype(jnp.bfloat16)
    from_tokens, from_gated = picked(upper, tokens_ref[...]), picked(lower, gated)
    start = 0
    for k, rows_ref in enumerate(rows):
        part = slice(start, start + rows_ref.shape[0])
        start = part.stop
        if k < 2:
            rows_ref[:, :width] = from_tokens[part].astype(jnp.bfloat16)
            rows_ref[:, width:] = from_gated[part].astype(jnp.bfloat16)
        else:
            rows_ref[...] = (from_tokens[part] + from_gated[part]).astype(jnp.bfloat16)
    for copy_ref in copies:
        copy_ref[...] = rows[0][...]


def pack(blocks, first, rest, capacity, experts, ids, gate, tokens, grads):
    n, width = tokens.shape
    whole = pl.BlockSpec(memory_space=pltpu.VMEM)
    crossing = len(blocks) - 2

    def shape(rows, columns):
        return jax.ShapeDtypeStruct((rows, columns), jnp.bfloat16)

    shapes = [shape(first, 2 * width), shape(rest, 2 * width)]
    shapes += [shape(2 * capacity, width)] * crossing
    shapes += [shape(first, n), shape(rest, n)] + [shape(2 * capacity, n)] * crossing
    shapes += [shape(first, 2 * width)] * len(early_masks)
    sources = (ids.reshape(1, n), gate.reshape(1, n), tokens, grads)
    outs = pl.pallas_call(
        lambda *refs: pack_kernel(blocks, experts, *refs),
        out_shape=shapes,
        in_specs=[pl.BlockSpec(memory_space=pltpu.HBM)] * 4,
        out_specs=[whole] * len(shapes),
        scratch_shapes=[
            pltpu.VMEM((1, n), jnp.int32),
            pltpu.VMEM((1, n), jnp.float32),
            pltpu.VMEM((n, width), jnp.bfloat16),
            pltpu.VMEM((n, width), jnp.bfloat16),
            pltpu.SemaphoreType.DMA((4,)),
        ],
        compiler_params=pltpu.CompilerParams(vmem_limit_bytes=8 * 1024 * 1024),
    )(*[pltpu.with_memory_space_constraint(source, pltpu.HBM) for source in sources])
    return outs[: len(blocks)], outs[len(blocks) : 2 * len(blocks)], outs[2 * len(blocks) :]


def handed_on(copies, sent):
    anywhere = pl.BlockSpec(memory_space=pl.ANY)
    return pl.pallas_call(
        lambda *refs: None,
        out_shape=[jax.ShapeDtypeStruct(rows.shape, rows.dtype) for rows in copies],
        in_specs=[anywhere] * (len(copies) + len(sent)),
        out_specs=[anywhere] * len(copies),
        input_output_aliases={k: k for k in range(len(copies))},
        compiler_params=pltpu.CompilerParams(vmem_limit_bytes=1024 * 1024),
    )(*copies, *sent)


def whole_weights(shard):
    if lax.axis_size("dp") == 1:
        return shard.astype(jnp.bfloat16)
    return lax.all_gather(shard.astype(jnp.bfloat16), "dp", axis=0, tiled=True)


def step_kernel(rows, *refs):
    *refs, done_ref, sems = refs
    count = len(refs) // 3
    bases, shares, outs = refs[:count], refs[count : 2 * count], refs[2 * count :]
    writes = []
    for start in range(0, outs[0].shape[0], rows):
        part = slice(start, start + rows)
        for k in range(count):
            done_ref[k, part] = bases[k][part] - step_rate * shares[k][part].astype(jnp.float32)
            writes.append(
                pltpu.make_async_copy(done_ref.at[k, part], outs[k].at[part], sems.at[len(writes)])
            )
            writes[-1].start()
    for write in writes:
        write.wait()


def stepped(bases, shares):
    units, width = bases[0].shape
    rows = 64 if units % 64 == 0 else units
    whole = pl.BlockSpec(memory_space=pltpu.VMEM)
    return pl.pallas_call(
        lambda *refs: step_kernel(rows, *refs),
        out_shape=[jax.ShapeDtypeStruct(base.shape, base.dtype) for base in bases],
        in_specs=[whole] * (2 * len(bases)),
        out_specs=[pl.BlockSpec(memory_space=pltpu.HBM)] * len(bases),
        scratch_shapes=[
            pltpu.VMEM((len(bases), units, width), jnp.float32),
            pltpu.SemaphoreType.DMA((len(bases) * (units // rows),)),
        ],
        compiler_params=pltpu.CompilerParams(vmem_limit_bytes=16 * 1024 * 1024),
        cost_estimate=pl.CostEstimate(
            flops=4 * units * width, bytes_accessed=8 * units * width, transcendentals=0
        ),
    )(*bases, *shares)


def stepped_over_dp(weights, grads):
    grads = lax.psum_scatter(
        grads.astype(jnp.bfloat16), "dp", scatter_dimension=0, tiled=True
    ).astype(jnp.float32)
    return weights - step_rate * grads


def swap(rows, mask):
    n_expert = lax.axis_size("expert")
    return lax.ppermute(rows, "expert", [(i, i ^ mask) for i in range(n_expert)])


core_bit, x_bit, y_bit, z_bit = 1, 2, 4, 8
early_masks = (x_bit | y_bit, z_bit, x_bit, y_bit)


def after(values, *others):
    return lax.optimization_barrier((others, values))[1]


def chain(blocks):
    chained = []
    for block in blocks:
        chained.append(after(block, chained[-1]) if chained else block)
    return chained


def swaps(blocks, masks):
    return [swap(block, mask) for block, mask in zip(chain(blocks), masks)]


def total(*terms):
    return sum(term.astype(jnp.float32) for term in terms).astype(jnp.bfloat16)


def split_rows(array, rows):
    return [array[k : k + rows] for k in range(0, array.shape[0], rows)]


def shards(tokens, attn_partials, expert_ids, gate, w_in, w_out):
    tok_rows, width = tokens.shape
    n_expert = lax.axis_size("expert")
    experts = n_expert // SHARDS
    capacity = 5 * tok_rows // (8 * experts)
    first = capacity // 8 * 8
    rest = experts * capacity - first
    units = w_in.shape[1]
    scale_in = width ** (-0.5)
    scale_out = FF ** (-0.5)

    def shifted(rows, hops):
        pairs = [(i, (i + SHARDS * hops) % n_expert) for i in range(n_expert)]
        return lax.ppermute(rows, "expert", pairs)

    offset = (experts - 1) * capacity - first
    own_blocks = [(0, 0, first, 0), (0, first, capacity, offset + first)]
    cross_blocks = [(s, 0, capacity, 0) for s in range(1, experts)]
    grads = summed_grads(attn_partials)
    (early_own, late_own, *sent), picks, copies = pack(
        own_blocks + cross_blocks, first, rest, capacity, experts, expert_ids, gate, tokens, grads
    )
    early_copies = handed_on(copies, sent)

    def activated(rows):
        expert_rows, grad_rows = rows[:, :width], rows[:, width:]
        pre_act = contract_cols(expert_rows, weights_in) * scale_in
        hidden = gelu_value(pre_act).astype(jnp.bfloat16)
        hidden_grad = contract_cols(grad_rows, weights_out) * scale_out
        pre_grad = (hidden_grad * gelu_slope(pre_act)).astype(jnp.bfloat16)
        return [expert_rows, grad_rows, hidden, pre_grad]

    def input_parts(pre_grad):
        parts = jnp.dot(pre_grad, weights_in, preferred_element_type=jnp.float32) * scale_in
        return parts.astype(jnp.bfloat16)

    for s in range(1, experts):
        side_by_side = jnp.concatenate(split_rows(shifted(sent[s - 1], s), capacity), axis=1)
        late_own = late_own + jnp.pad(
            side_by_side, (((s - 1) * capacity, rest - s * capacity), (0, 0))
        )
    early_xy, early_z, early_x, early_y = after(
        [swap(rows, mask) for rows, mask in zip(early_copies, early_masks)], late_own
    )
    late_x, late_y, late_z = swaps(
        [
            jnp.concatenate([late_own, early_z], axis=0),
            jnp.concatenate([late_own, early_z], axis=0),
            jnp.concatenate([late_own, early_xy], axis=0),
        ],
        (x_bit, y_bit, z_bit),
    )
    early_zx, early_yz, early_far = late_x[rest:], late_y[rest:], late_z[rest:]
    late_x, late_y, late_z = late_x[:rest], late_y[:rest], late_z[:rest]
    early_rows = [early_own, early_x, early_y, early_z, early_xy, early_yz, early_zx, early_far]

    own_weights = jnp.concatenate([whole_weights(w_in).T, whole_weights(w_out).T], axis=0)
    their_weights = swap(after(own_weights, late_own), core_bit)
    weights_in, weights_out = [
        jnp.concatenate([own_weights[part], their_weights[part]], axis=0)
        for part in (slice(0, units), slice(units, 2 * units))
    ]
    late_far, late_zx, late_yz, late_xy = swaps(
        [late_z, late_z, late_y, late_x],
        (x_bit | y_bit, x_bit, z_bit, y_bit),
    )
    early = activated(jnp.concatenate(early_rows, axis=0))
    early_parts = input_parts(early[3])
    late_far = after([late_xy, late_yz, late_zx, late_far], early_parts)
    late_rows = [late_own, late_x, late_y, late_z, *late_far]
    later = activated(jnp.concatenate(late_rows, axis=0))
    late_parts = input_parts(later[3])
    parts = [
        jnp.concatenate(pair, axis=0)
        for pair in zip(split_rows(early_parts, first), split_rows(late_parts, rest))
    ]
    own, sum_x, sum_y, sum_z, sum_xy, sum_yz, sum_zx, sum_far = parts
    back = chain([sum_far, sum_zx, sum_xy, sum_yz])
    far, zx, xy, yz = [
        swap(rows, mask) for rows, mask in zip(back, (x_bit | y_bit, x_bit, y_bit, z_bit))
    ]

    def gradients(part, awaited):
        chunks = [chunk[:2] + after(chunk[2:], awaited) for chunk in (early, later)]
        return [
            sum(contract_rows(chunk[left][:, part], chunk[right]) for chunk in chunks) * scale
            for left, right, scale in ((3, 0, scale_in), (2, 1, scale_out))
        ]

    theirs = gradients(slice(units, 2 * units), back[-1])
    theirs = [grads.astype(jnp.bfloat16) for grads in theirs]
    zx, theirs = lax.optimization_barrier((zx, theirs))
    shares = [swap(grads, core_bit) for grads in theirs]
    mine = gradients(slice(0, units), zx)
    split_width = lax.axis_size("dp") > 1
    if not split_width:
        mine = [weights.T - step_rate * grads for weights, grads in zip((w_in, w_out), mine)]
    if split_width:
        new_weights = [
            stepped_over_dp(weights, (grads + share.astype(jnp.float32)).T)
            for weights, grads, share in zip((w_in, w_out), mine, shares)
        ]
    else:
        new_weights = [weights.T for weights in stepped(mine, shares)]
    near = swaps(
        [total(sum_z, zx, far), total(sum_x, xy), total(sum_y, yz)], (z_bit, x_bit, y_bit)
    )
    sums = total(own, *near)
    early_sum, late_sum = sums[:first], sums[first:]
    half = width // 2
    returned = [early_sum, late_sum]
    for s in range(1, experts):
        rows = late_sum[(s - 1) * capacity : s * capacity]
        rows = jnp.concatenate([rows[:, :half], rows[:, half:]], axis=0)
        rows = after(shifted(rows, -s), new_weights)
        returned.append(jnp.concatenate(split_rows(rows, capacity), axis=1))
    picks = [*picks[:2], *[pick[:capacity] for pick in picks[2:]]]
    token_grad = sum(contract_rows(pick, rows) for pick, rows in zip(picks, returned))
    return (token_grad.astype(jnp.bfloat16), *new_weights)


def solution(mesh):
    in_specs = (
        P(("expert", "dp"), None),
        P("dp", "expert", None),
        P(("expert", "dp")),
        P(("expert", "dp")),
        P("dp", "expert"),
        P("dp", "expert"),
    )
    out_specs = (P(("expert", "dp"), None), P("dp", "expert"), P("dp", "expert"))
    return jax.shard_map(shards, mesh=mesh, in_specs=in_specs, out_specs=out_specs, check_vma=False)
```

```python
import jax
import jax.numpy as jnp
from jax import lax
from jax.experimental import pallas as pl
from jax.experimental.pallas import tpu as pltpu
from jax.sharding import PartitionSpec as P

FF = 5120
SHARDS = 16


gelu_coef = 0.7978845608028654
cubic_coef = 0.044715
step_rate = 0.5


def gelu_value(inputs):
    return (
        0.5
        * inputs
        * (1.0 + jnp.tanh(gelu_coef * (inputs + cubic_coef * inputs * inputs * inputs)))
    )


def gelu_slope(inputs):
    tangent = jnp.tanh(gelu_coef * (inputs + cubic_coef * inputs * inputs * inputs))
    return 0.5 * (1.0 + tangent) + 0.5 * inputs * (1.0 - tangent * tangent) * gelu_coef * (
        1.0 + 3.0 * cubic_coef * inputs * inputs
    )


def contract_rows(left, right):
    return lax.dot_general(
        left, right, (((0,), (0,)), ((), ())), preferred_element_type=jnp.float32
    )


def contract_cols(left, right):
    return lax.dot_general(
        left, right, (((1,), (1,)), ((), ())), preferred_element_type=jnp.float32
    )


def summed_grads(attn_partials):
    if lax.axis_size("dp") == 1:
        return attn_partials[0]
    return lax.psum_scatter(attn_partials[0], "dp", scatter_dimension=0, tiled=True)


def picked(pick, source):
    return jnp.dot(pick, source, preferred_element_type=jnp.float32)


def pack_kernel(blocks, experts, *refs):
    sources, (*outs, ids_ref, gate_ref, tokens_ref, grads_ref, sems) = refs[:4], refs[4:]
    fetches = [
        pltpu.make_async_copy(source, target, sems.at[k])
        for k, (source, target) in enumerate(
            zip(sources, (ids_ref, gate_ref, tokens_ref, grads_ref))
        )
    ]
    for fetch in fetches:
        fetch.start()
    for fetch in fetches[:2]:
        fetch.wait()
    n, width = tokens_ref.shape
    mine = (lax.axis_index("expert") // SHARDS).astype(jnp.float32)
    ids = ids_ref[...].astype(jnp.float32)
    relative = ids - mine
    relative = jnp.where(relative < 0.0, relative + experts, relative)
    down = lax.broadcasted_iota(jnp.int32, (n, n), 0)
    across = lax.broadcasted_iota(jnp.int32, (n, n), 1)
    ids_down = jnp.sum(jnp.where(down == across, ids, 0.0), axis=1, keepdims=True)
    gate_down = jnp.sum(jnp.where(down == across, gate_ref[...], 0.0), axis=1, keepdims=True)
    rivals = jnp.where((ids_down == ids) & (down < across), 1.0, 0.0)
    rank = jnp.sum(rivals, axis=0, keepdims=True)
    rows, picks = outs[: len(blocks)], outs[len(blocks) : 2 * len(blocks)]
    copies = outs[2 * len(blocks) :]

    def one_hot(shape, block, shift):
        expert, begin, end, row = block
        chosen = (relative == expert) & (rank >= begin) & (rank < end)
        slot = jnp.where(chosen, rank - begin + row + shift, -1.0).astype(jnp.int32)
        slots = lax.broadcasted_iota(jnp.int32, shape, 0)
        return jnp.where(slots == slot, 1.0, 0.0)

    uppers, lowers = [], []
    for k, block in enumerate(blocks):
        shape = picks[k].shape
        uppers.append(one_hot(shape, block, 0))
        lowers.append(uppers[k] if k < 2 else one_hot(shape, block, block[2]))
        picks[k][...] = uppers[k].astype(jnp.bfloat16)
    upper, lower = [jnp.concatenate(p, axis=0).astype(jnp.bfloat16) for p in (uppers, lowers)]
    for fetch in fetches[2:]:
        fetch.wait()
    gated = (gate_down * grads_ref[...].astype(jnp.float32)).astype(jnp.bfloat16)
    from_tokens, from_gated = picked(upper, tokens_ref[...]), picked(lower, gated)
    start = 0
    for k, rows_ref in enumerate(rows):
        part = slice(start, start + rows_ref.shape[0])
        start = part.stop
        if k < 2:
            rows_ref[:, :width] = from_tokens[part].astype(jnp.bfloat16)
            rows_ref[:, width:] = from_gated[part].astype(jnp.bfloat16)
        else:
            rows_ref[...] = (from_tokens[part] + from_gated[part]).astype(jnp.bfloat16)
    for copy_ref in copies:
        copy_ref[...] = rows[0][...]


def pack(blocks, first, rest, capacity, experts, ids, gate, tokens, grads):
    n, width = tokens.shape
    whole = pl.BlockSpec(memory_space=pltpu.VMEM)
    crossing = len(blocks) - 2

    def shape(rows, columns):
        return jax.ShapeDtypeStruct((rows, columns), jnp.bfloat16)

    shapes = [shape(first, 2 * width), shape(rest, 2 * width)]
    shapes += [shape(2 * capacity, width)] * crossing
    shapes += [shape(first, n), shape(rest, n)] + [shape(2 * capacity, n)] * crossing
    shapes += [shape(first, 2 * width)] * len(early_masks)
    sources = (ids.reshape(1, n), gate.reshape(1, n), tokens, grads)
    outs = pl.pallas_call(
        lambda *refs: pack_kernel(blocks, experts, *refs),
        out_shape=shapes,
        in_specs=[pl.BlockSpec(memory_space=pltpu.HBM)] * 4,
        out_specs=[whole] * len(shapes),
        scratch_shapes=[
            pltpu.VMEM((1, n), jnp.int32),
            pltpu.VMEM((1, n), jnp.float32),
            pltpu.VMEM((n, width), jnp.bfloat16),
            pltpu.VMEM((n, width), jnp.bfloat16),
            pltpu.SemaphoreType.DMA((4,)),
        ],
        compiler_params=pltpu.CompilerParams(vmem_limit_bytes=8 * 1024 * 1024),
    )(*[pltpu.with_memory_space_constraint(source, pltpu.HBM) for source in sources])
    return outs[: len(blocks)], outs[len(blocks) : 2 * len(blocks)], outs[2 * len(blocks) :]


def handed_on(copies, sent):
    anywhere = pl.BlockSpec(memory_space=pl.ANY)
    return pl.pallas_call(
        lambda *refs: None,
        out_shape=[jax.ShapeDtypeStruct(rows.shape, rows.dtype) for rows in copies],
        in_specs=[anywhere] * (len(copies) + len(sent)),
        out_specs=[anywhere] * len(copies),
        input_output_aliases={k: k for k in range(len(copies))},
        compiler_params=pltpu.CompilerParams(vmem_limit_bytes=1024 * 1024),
    )(*copies, *sent)


def whole_weights(shard):
    if lax.axis_size("dp") == 1:
        return shard.astype(jnp.bfloat16)
    return lax.all_gather(shard.astype(jnp.bfloat16), "dp", axis=0, tiled=True)


def step_kernel(rows, *refs):
    *refs, done_ref, sems = refs
    count = len(refs) // 3
    bases, shares, outs = refs[:count], refs[count : 2 * count], refs[2 * count :]
    writes = []
    for start in range(0, outs[0].shape[0], rows):
        part = slice(start, start + rows)
        for k in range(count):
            done_ref[k, part] = bases[k][part] - step_rate * shares[k][part].astype(jnp.float32)
            writes.append(
                pltpu.make_async_copy(done_ref.at[k, part], outs[k].at[part], sems.at[len(writes)])
            )
            writes[-1].start()
    for write in writes:
        write.wait()


def stepped(bases, shares):
    units, width = bases[0].shape
    rows = 64 if units % 64 == 0 else units
    whole = pl.BlockSpec(memory_space=pltpu.VMEM)
    return pl.pallas_call(
        lambda *refs: step_kernel(rows, *refs),
        out_shape=[jax.ShapeDtypeStruct(base.shape, base.dtype) for base in bases],
        in_specs=[whole] * (2 * len(bases)),
        out_specs=[pl.BlockSpec(memory_space=pltpu.HBM)] * len(bases),
        scratch_shapes=[
            pltpu.VMEM((len(bases), units, width), jnp.float32),
            pltpu.SemaphoreType.DMA((len(bases) * (units // rows),)),
        ],
        compiler_params=pltpu.CompilerParams(vmem_limit_bytes=16 * 1024 * 1024),
        cost_estimate=pl.CostEstimate(
            flops=4 * units * width, bytes_accessed=8 * units * width, transcendentals=0
        ),
    )(*bases, *shares)


def stepped_over_dp(weights, grads):
    grads = lax.psum_scatter(
        grads.astype(jnp.bfloat16), "dp", scatter_dimension=0, tiled=True
    ).astype(jnp.float32)
    return weights - step_rate * grads


def swap(rows, mask):
    n_expert = lax.axis_size("expert")
    return lax.ppermute(rows, "expert", [(i, i ^ mask) for i in range(n_expert)])


core_bit, x_bit, y_bit, z_bit = 1, 2, 4, 8
early_masks = (x_bit | y_bit, z_bit, x_bit, y_bit)


def after(values, *others):
    return lax.optimization_barrier((others, values))[1]


def chain(blocks):
    chained = []
    for block in blocks:
        chained.append(after(block, chained[-1]) if chained else block)
    return chained


def swaps(blocks, masks):
    return [swap(block, mask) for block, mask in zip(chain(blocks), masks)]


def total(*terms):
    return sum(term.astype(jnp.float32) for term in terms).astype(jnp.bfloat16)


def split_rows(array, rows):
    return [array[k : k + rows] for k in range(0, array.shape[0], rows)]


def shards(tokens, attn_partials, expert_ids, gate, w_in, w_out):
    tok_rows, width = tokens.shape
    n_expert = lax.axis_size("expert")
    experts = n_expert // SHARDS
    capacity = 5 * tok_rows // (8 * experts)
    first = capacity // 8 * 8
    rest = experts * capacity - first
    units = w_in.shape[1]
    scale_in = width ** (-0.5)
    scale_out = FF ** (-0.5)

    def shifted(rows, hops):
        pairs = [(i, (i + SHARDS * hops) % n_expert) for i in range(n_expert)]
        return lax.ppermute(rows, "expert", pairs)

    offset = (experts - 1) * capacity - first
    own_blocks = [(0, 0, first, 0), (0, first, capacity, offset + first)]
    cross_blocks = [(s, 0, capacity, 0) for s in range(1, experts)]
    grads = summed_grads(attn_partials)
    (early_own, late_own, *sent), picks, copies = pack(
        own_blocks + cross_blocks, first, rest, capacity, experts, expert_ids, gate, tokens, grads
    )
    early_copies = handed_on(copies, sent)

    def activated(rows):
        expert_rows, grad_rows = rows[:, :width], rows[:, width:]
        pre_act = contract_cols(expert_rows, weights_in) * scale_in
        hidden = gelu_value(pre_act).astype(jnp.bfloat16)
        hidden_grad = contract_cols(grad_rows, weights_out) * scale_out
        pre_grad = (hidden_grad * gelu_slope(pre_act)).astype(jnp.bfloat16)
        return [expert_rows, grad_rows, hidden, pre_grad]

    def input_parts(pre_grad):
        parts = jnp.dot(pre_grad, weights_in, preferred_element_type=jnp.float32) * scale_in
        return parts.astype(jnp.bfloat16)

    for s in range(1, experts):
        side_by_side = jnp.concatenate(split_rows(shifted(sent[s - 1], s), capacity), axis=1)
        late_own = late_own + jnp.pad(
            side_by_side, (((s - 1) * capacity, rest - s * capacity), (0, 0))
        )
    early_xy, early_z, early_x, early_y = after(
        [swap(rows, mask) for rows, mask in zip(early_copies, early_masks)], late_own
    )
    late_x, late_y, late_z = swaps(
        [
            jnp.concatenate([late_own, early_z], axis=0),
            jnp.concatenate([late_own, early_z], axis=0),
            jnp.concatenate([late_own, early_xy], axis=0),
        ],
        (x_bit, y_bit, z_bit),
    )
    early_zx, early_yz, early_far = late_x[rest:], late_y[rest:], late_z[rest:]
    late_x, late_y, late_z = late_x[:rest], late_y[:rest], late_z[:rest]
    early_rows = [early_own, early_x, early_y, early_z, early_xy, early_yz, early_zx, early_far]

    own_weights = jnp.concatenate([whole_weights(w_in).T, whole_weights(w_out).T], axis=0)
    their_weights = swap(after(own_weights, late_own), core_bit)
    weights_in, weights_out = [
        jnp.concatenate([own_weights[part], their_weights[part]], axis=0)
        for part in (slice(0, units), slice(units, 2 * units))
    ]
    late_xy, late_far, late_yz, late_zx = swaps(
        [late_x, late_x, late_y, late_z],
        (y_bit, y_bit | z_bit, z_bit, x_bit),
    )
    early = activated(jnp.concatenate(early_rows, axis=0))
    early_parts = input_parts(early[3])
    late_far = after([late_xy, late_yz, late_zx, late_far], early_parts)
    late_rows = [late_own, late_x, late_y, late_z, *late_far]
    later = activated(jnp.concatenate(late_rows, axis=0))
    late_parts = input_parts(later[3])
    parts = [
        jnp.concatenate(pair, axis=0)
        for pair in zip(split_rows(early_parts, first), split_rows(late_parts, rest))
    ]
    own, sum_x, sum_y, sum_z, sum_xy, sum_yz, sum_zx, sum_far = parts
    back = chain([sum_far, sum_zx, sum_xy, sum_yz])
    far, zx, xy, yz = [
        swap(rows, mask) for rows, mask in zip(back, (x_bit | y_bit, x_bit, y_bit, z_bit))
    ]

    def gradients(part, awaited):
        chunks = [chunk[:2] + after(chunk[2:], awaited) for chunk in (early, later)]
        return [
            sum(contract_rows(chunk[left][:, part], chunk[right]) for chunk in chunks) * scale
            for left, right, scale in ((3, 0, scale_in), (2, 1, scale_out))
        ]

    theirs = gradients(slice(units, 2 * units), back[-1])
    theirs = [grads.astype(jnp.bfloat16) for grads in theirs]
    zx, theirs = lax.optimization_barrier((zx, theirs))
    shares = [swap(grads, core_bit) for grads in theirs]
    mine = gradients(slice(0, units), zx)
    split_width = lax.axis_size("dp") > 1
    if not split_width:
        mine = [weights.T - step_rate * grads for weights, grads in zip((w_in, w_out), mine)]
    if split_width:
        new_weights = [
            stepped_over_dp(weights, (grads + share.astype(jnp.float32)).T)
            for weights, grads, share in zip((w_in, w_out), mine, shares)
        ]
    else:
        new_weights = [weights.T for weights in stepped(mine, shares)]
    near = swaps(
        [total(sum_z, zx, far), total(sum_x, xy), total(sum_y, yz)], (z_bit, x_bit, y_bit)
    )
    sums = total(own, *near)
    early_sum, late_sum = sums[:first], sums[first:]
    half = width // 2
    returned = [early_sum, late_sum]
    for s in range(1, experts):
        rows = late_sum[(s - 1) * capacity : s * capacity]
        rows = jnp.concatenate([rows[:, :half], rows[:, half:]], axis=0)
        rows = after(shifted(rows, -s), new_weights)
        returned.append(jnp.concatenate(split_rows(rows, capacity), axis=1))
    picks = [*picks[:2], *[pick[:capacity] for pick in picks[2:]]]
    token_grad = sum(contract_rows(pick, rows) for pick, rows in zip(picks, returned))
    return (token_grad.astype(jnp.bfloat16), *new_weights)


def solution(mesh):
    in_specs = (
        P(("expert", "dp"), None),
        P("dp", "expert", None),
        P(("expert", "dp")),
        P(("expert", "dp")),
        P("dp", "expert"),
        P("dp", "expert"),
    )
    out_specs = (P(("expert", "dp"), None), P("dp", "expert"), P("dp", "expert"))
    return jax.shard_map(shards, mesh=mesh, in_specs=in_specs, out_specs=out_specs, check_vma=False)
```

```python
import jax
import jax.numpy as jnp
from jax import lax
from jax.experimental import pallas as pl
from jax.experimental.pallas import tpu as pltpu
from jax.sharding import PartitionSpec as P

FF = 5120
SHARDS = 16


gelu_coef = 0.7978845608028654
cubic_coef = 0.044715
step_rate = 0.5


def gelu_value(inputs):
    return (
        0.5
        * inputs
        * (1.0 + jnp.tanh(gelu_coef * (inputs + cubic_coef * inputs * inputs * inputs)))
    )


def gelu_slope(inputs):
    tangent = jnp.tanh(gelu_coef * (inputs + cubic_coef * inputs * inputs * inputs))
    return 0.5 * (1.0 + tangent) + 0.5 * inputs * (1.0 - tangent * tangent) * gelu_coef * (
        1.0 + 3.0 * cubic_coef * inputs * inputs
    )


def contract_rows(left, right):
    return lax.dot_general(
        left, right, (((0,), (0,)), ((), ())), preferred_element_type=jnp.float32
    )


def contract_cols(left, right):
    return lax.dot_general(
        left, right, (((1,), (1,)), ((), ())), preferred_element_type=jnp.float32
    )


def summed_grads(attn_partials):
    if lax.axis_size("dp") == 1:
        return attn_partials[0]
    return lax.psum_scatter(attn_partials[0], "dp", scatter_dimension=0, tiled=True)


def picked(pick, source):
    return jnp.dot(pick, source, preferred_element_type=jnp.float32)


def pack_kernel(blocks, experts, *refs):
    sources, (*outs, ids_ref, gate_ref, tokens_ref, grads_ref, sems) = refs[:4], refs[4:]
    fetches = [
        pltpu.make_async_copy(source, target, sems.at[k])
        for k, (source, target) in enumerate(
            zip(sources, (ids_ref, gate_ref, tokens_ref, grads_ref))
        )
    ]
    for fetch in fetches:
        fetch.start()
    for fetch in fetches[:2]:
        fetch.wait()
    n, width = tokens_ref.shape
    mine = (lax.axis_index("expert") // SHARDS).astype(jnp.float32)
    ids = ids_ref[...].astype(jnp.float32)
    relative = ids - mine
    relative = jnp.where(relative < 0.0, relative + experts, relative)
    down = lax.broadcasted_iota(jnp.int32, (n, n), 0)
    across = lax.broadcasted_iota(jnp.int32, (n, n), 1)
    ids_down = jnp.sum(jnp.where(down == across, ids, 0.0), axis=1, keepdims=True)
    gate_down = jnp.sum(jnp.where(down == across, gate_ref[...], 0.0), axis=1, keepdims=True)
    rivals = jnp.where((ids_down == ids) & (down < across), 1.0, 0.0)
    rank = jnp.sum(rivals, axis=0, keepdims=True)
    rows, picks = outs[: len(blocks)], outs[len(blocks) : 2 * len(blocks)]
    copies = outs[2 * len(blocks) :]

    def one_hot(shape, block, shift):
        expert, begin, end, row = block
        chosen = (relative == expert) & (rank >= begin) & (rank < end)
        slot = jnp.where(chosen, rank - begin + row + shift, -1.0).astype(jnp.int32)
        slots = lax.broadcasted_iota(jnp.int32, shape, 0)
        return jnp.where(slots == slot, 1.0, 0.0)

    uppers, lowers = [], []
    for k, block in enumerate(blocks):
        shape = picks[k].shape
        uppers.append(one_hot(shape, block, 0))
        lowers.append(uppers[k] if k < 2 else one_hot(shape, block, block[2]))
        picks[k][...] = uppers[k].astype(jnp.bfloat16)
    upper, lower = [jnp.concatenate(p, axis=0).astype(jnp.bfloat16) for p in (uppers, lowers)]
    for fetch in fetches[2:]:
        fetch.wait()
    gated = (gate_down * grads_ref[...].astype(jnp.float32)).astype(jnp.bfloat16)
    from_tokens, from_gated = picked(upper, tokens_ref[...]), picked(lower, gated)
    start = 0
    for k, rows_ref in enumerate(rows):
        part = slice(start, start + rows_ref.shape[0])
        start = part.stop
        if k < 2:
            rows_ref[:, :width] = from_tokens[part].astype(jnp.bfloat16)
            rows_ref[:, width:] = from_gated[part].astype(jnp.bfloat16)
        else:
            rows_ref[...] = (from_tokens[part] + from_gated[part]).astype(jnp.bfloat16)
    for copy_ref in copies:
        copy_ref[...] = rows[0][...]


def pack(blocks, first, rest, capacity, experts, ids, gate, tokens, grads):
    n, width = tokens.shape
    whole = pl.BlockSpec(memory_space=pltpu.VMEM)
    crossing = len(blocks) - 2

    def shape(rows, columns):
        return jax.ShapeDtypeStruct((rows, columns), jnp.bfloat16)

    shapes = [shape(first, 2 * width), shape(rest, 2 * width)]
    shapes += [shape(2 * capacity, width)] * crossing
    shapes += [shape(first, n), shape(rest, n)] + [shape(2 * capacity, n)] * crossing
    shapes += [shape(first, 2 * width)] * len(early_masks)
    sources = (ids.reshape(1, n), gate.reshape(1, n), tokens, grads)
    outs = pl.pallas_call(
        lambda *refs: pack_kernel(blocks, experts, *refs),
        out_shape=shapes,
        in_specs=[pl.BlockSpec(memory_space=pltpu.HBM)] * 4,
        out_specs=[whole] * len(shapes),
        scratch_shapes=[
            pltpu.VMEM((1, n), jnp.int32),
            pltpu.VMEM((1, n), jnp.float32),
            pltpu.VMEM((n, width), jnp.bfloat16),
            pltpu.VMEM((n, width), jnp.bfloat16),
            pltpu.SemaphoreType.DMA((4,)),
        ],
        compiler_params=pltpu.CompilerParams(vmem_limit_bytes=8 * 1024 * 1024),
    )(*[pltpu.with_memory_space_constraint(source, pltpu.HBM) for source in sources])
    return outs[: len(blocks)], outs[len(blocks) : 2 * len(blocks)], outs[2 * len(blocks) :]


def handed_on(copies, sent):
    anywhere = pl.BlockSpec(memory_space=pl.ANY)
    return pl.pallas_call(
        lambda *refs: None,
        out_shape=[jax.ShapeDtypeStruct(rows.shape, rows.dtype) for rows in copies],
        in_specs=[anywhere] * (len(copies) + len(sent)),
        out_specs=[anywhere] * len(copies),
        input_output_aliases={k: k for k in range(len(copies))},
        compiler_params=pltpu.CompilerParams(vmem_limit_bytes=1024 * 1024),
    )(*copies, *sent)


def whole_weights(shard):
    if lax.axis_size("dp") == 1:
        return shard.astype(jnp.bfloat16)
    return lax.all_gather(shard.astype(jnp.bfloat16), "dp", axis=0, tiled=True)


def step_kernel(rows, *refs):
    *refs, done_ref, sems = refs
    count = len(refs) // 3
    bases, shares, outs = refs[:count], refs[count : 2 * count], refs[2 * count :]
    writes = []
    for start in range(0, outs[0].shape[0], rows):
        part = slice(start, start + rows)
        for k in range(count):
            done_ref[k, part] = bases[k][part] - step_rate * shares[k][part].astype(jnp.float32)
            writes.append(
                pltpu.make_async_copy(done_ref.at[k, part], outs[k].at[part], sems.at[len(writes)])
            )
            writes[-1].start()
    for write in writes:
        write.wait()


def stepped(bases, shares):
    units, width = bases[0].shape
    rows = 64 if units % 64 == 0 else units
    whole = pl.BlockSpec(memory_space=pltpu.VMEM)
    return pl.pallas_call(
        lambda *refs: step_kernel(rows, *refs),
        out_shape=[jax.ShapeDtypeStruct(base.shape, base.dtype) for base in bases],
        in_specs=[whole] * (2 * len(bases)),
        out_specs=[pl.BlockSpec(memory_space=pltpu.HBM)] * len(bases),
        scratch_shapes=[
            pltpu.VMEM((len(bases), units, width), jnp.float32),
            pltpu.SemaphoreType.DMA((len(bases) * (units // rows),)),
        ],
        compiler_params=pltpu.CompilerParams(vmem_limit_bytes=16 * 1024 * 1024),
        cost_estimate=pl.CostEstimate(
            flops=4 * units * width, bytes_accessed=8 * units * width, transcendentals=0
        ),
    )(*bases, *shares)


def stepped_over_dp(weights, grads):
    grads = lax.psum_scatter(
        grads.astype(jnp.bfloat16), "dp", scatter_dimension=0, tiled=True
    ).astype(jnp.float32)
    return weights - step_rate * grads


def swap(rows, mask):
    n_expert = lax.axis_size("expert")
    return lax.ppermute(rows, "expert", [(i, i ^ mask) for i in range(n_expert)])


core_bit, x_bit, y_bit, z_bit = 1, 2, 4, 8
early_masks = (z_bit, x_bit | y_bit, x_bit, y_bit)


def after(values, *others):
    return lax.optimization_barrier((others, values))[1]


def chain(blocks):
    chained = []
    for block in blocks:
        chained.append(after(block, chained[-1]) if chained else block)
    return chained


def swaps(blocks, masks):
    return [swap(block, mask) for block, mask in zip(chain(blocks), masks)]


def total(*terms):
    return sum(term.astype(jnp.float32) for term in terms).astype(jnp.bfloat16)


def split_rows(array, rows):
    return [array[k : k + rows] for k in range(0, array.shape[0], rows)]


def shards(tokens, attn_partials, expert_ids, gate, w_in, w_out):
    tok_rows, width = tokens.shape
    n_expert = lax.axis_size("expert")
    experts = n_expert // SHARDS
    capacity = 5 * tok_rows // (8 * experts)
    first = capacity // 8 * 8
    rest = experts * capacity - first
    units = w_in.shape[1]
    scale_in = width ** (-0.5)
    scale_out = FF ** (-0.5)

    def shifted(rows, hops):
        pairs = [(i, (i + SHARDS * hops) % n_expert) for i in range(n_expert)]
        return lax.ppermute(rows, "expert", pairs)

    offset = (experts - 1) * capacity - first
    own_blocks = [(0, 0, first, 0), (0, first, capacity, offset + first)]
    cross_blocks = [(s, 0, capacity, 0) for s in range(1, experts)]
    grads = summed_grads(attn_partials)
    (early_own, late_own, *sent), picks, copies = pack(
        own_blocks + cross_blocks, first, rest, capacity, experts, expert_ids, gate, tokens, grads
    )
    early_copies = handed_on(copies, sent)

    def activated(rows):
        expert_rows, grad_rows = rows[:, :width], rows[:, width:]
        pre_act = contract_cols(expert_rows, weights_in) * scale_in
        hidden = gelu_value(pre_act).astype(jnp.bfloat16)
        hidden_grad = contract_cols(grad_rows, weights_out) * scale_out
        pre_grad = (hidden_grad * gelu_slope(pre_act)).astype(jnp.bfloat16)
        return [expert_rows, grad_rows, hidden, pre_grad]

    def input_parts(pre_grad):
        parts = jnp.dot(pre_grad, weights_in, preferred_element_type=jnp.float32) * scale_in
        return parts.astype(jnp.bfloat16)

    for s in range(1, experts):
        side_by_side = jnp.concatenate(split_rows(shifted(sent[s - 1], s), capacity), axis=1)
        late_own = late_own + jnp.pad(
            side_by_side, (((s - 1) * capacity, rest - s * capacity), (0, 0))
        )
    early_z, early_xy, early_x, early_y = after(
        [swap(rows, mask) for rows, mask in zip(early_copies, early_masks)], late_own
    )
    late_x, late_y, late_z = swaps(
        [
            jnp.concatenate([late_own, early_z], axis=0),
            jnp.concatenate([late_own, early_z], axis=0),
            jnp.concatenate([late_own, early_xy], axis=0),
        ],
        (x_bit, y_bit, z_bit),
    )
    early_zx, early_yz, early_far = late_x[rest:], late_y[rest:], late_z[rest:]
    late_x, late_y, late_z = late_x[:rest], late_y[:rest], late_z[:rest]
    early_rows = [early_own, early_x, early_y, early_z, early_xy, early_yz, early_zx, early_far]

    own_weights = jnp.concatenate([whole_weights(w_in).T, whole_weights(w_out).T], axis=0)
    their_weights = swap(after(own_weights, late_own), core_bit)
    weights_in, weights_out = [
        jnp.concatenate([own_weights[part], their_weights[part]], axis=0)
        for part in (slice(0, units), slice(units, 2 * units))
    ]
    late_xy, late_far, late_yz, late_zx = swaps(
        [late_x, late_x, late_y, late_z],
        (y_bit, y_bit | z_bit, z_bit, x_bit),
    )
    early = activated(jnp.concatenate(early_rows, axis=0))
    early_parts = input_parts(early[3])
    late_far = after([late_xy, late_yz, late_zx, late_far], early_parts)
    late_rows = [late_own, late_x, late_y, late_z, *late_far]
    later = activated(jnp.concatenate(late_rows, axis=0))
    late_parts = input_parts(later[3])
    parts = [
        jnp.concatenate(pair, axis=0)
        for pair in zip(split_rows(early_parts, first), split_rows(late_parts, rest))
    ]
    own, sum_x, sum_y, sum_z, sum_xy, sum_yz, sum_zx, sum_far = parts
    back = chain([sum_far, sum_zx, sum_xy, sum_yz])
    far, zx, xy, yz = [
        swap(rows, mask) for rows, mask in zip(back, (x_bit | y_bit, x_bit, y_bit, z_bit))
    ]

    def gradients(part, awaited):
        chunks = [chunk[:2] + after(chunk[2:], awaited) for chunk in (early, later)]
        return [
            sum(contract_rows(chunk[left][:, part], chunk[right]) for chunk in chunks) * scale
            for left, right, scale in ((3, 0, scale_in), (2, 1, scale_out))
        ]

    theirs = gradients(slice(units, 2 * units), back[-1])
    theirs = [grads.astype(jnp.bfloat16) for grads in theirs]
    zx, theirs = lax.optimization_barrier((zx, theirs))
    shares = [swap(grads, core_bit) for grads in theirs]
    mine = gradients(slice(0, units), zx)
    split_width = lax.axis_size("dp") > 1
    if not split_width:
        mine = [weights.T - step_rate * grads for weights, grads in zip((w_in, w_out), mine)]
    if split_width:
        new_weights = [
            stepped_over_dp(weights, (grads + share.astype(jnp.float32)).T)
            for weights, grads, share in zip((w_in, w_out), mine, shares)
        ]
    else:
        new_weights = [weights.T for weights in stepped(mine, shares)]
    near = swaps(
        [total(sum_z, zx, far), total(sum_x, xy), total(sum_y, yz)], (z_bit, x_bit, y_bit)
    )
    sums = total(own, *near)
    early_sum, late_sum = sums[:first], sums[first:]
    half = width // 2
    returned = [early_sum, late_sum]
    for s in range(1, experts):
        rows = late_sum[(s - 1) * capacity : s * capacity]
        rows = jnp.concatenate([rows[:, :half], rows[:, half:]], axis=0)
        rows = after(shifted(rows, -s), new_weights)
        returned.append(jnp.concatenate(split_rows(rows, capacity), axis=1))
    picks = [*picks[:2], *[pick[:capacity] for pick in picks[2:]]]
    token_grad = sum(contract_rows(pick, rows) for pick, rows in zip(picks, returned))
    return (token_grad.astype(jnp.bfloat16), *new_weights)


def solution(mesh):
    in_specs = (
        P(("expert", "dp"), None),
        P("dp", "expert", None),
        P(("expert", "dp")),
        P(("expert", "dp")),
        P("dp", "expert"),
        P("dp", "expert"),
    )
    out_specs = (P(("expert", "dp"), None), P("dp", "expert"), P("dp", "expert"))
    return jax.shard_map(shards, mesh=mesh, in_specs=in_specs, out_specs=out_specs, check_vma=False)
```

```python
import jax
import jax.numpy as jnp
from jax import lax
from jax.experimental import pallas as pl
from jax.experimental.pallas import tpu as pltpu
from jax.sharding import PartitionSpec as P

FF = 5120
SHARDS = 16


gelu_coef = 0.7978845608028654
cubic_coef = 0.044715
step_rate = 0.5


def gelu_value(inputs):
    return (
        0.5
        * inputs
        * (1.0 + jnp.tanh(gelu_coef * (inputs + cubic_coef * inputs * inputs * inputs)))
    )


def gelu_slope(inputs):
    tangent = jnp.tanh(gelu_coef * (inputs + cubic_coef * inputs * inputs * inputs))
    return 0.5 * (1.0 + tangent) + 0.5 * inputs * (1.0 - tangent * tangent) * gelu_coef * (
        1.0 + 3.0 * cubic_coef * inputs * inputs
    )


def contract_rows(left, right):
    return lax.dot_general(
        left, right, (((0,), (0,)), ((), ())), preferred_element_type=jnp.float32
    )


def contract_cols(left, right):
    return lax.dot_general(
        left, right, (((1,), (1,)), ((), ())), preferred_element_type=jnp.float32
    )


def summed_grads(attn_partials):
    if lax.axis_size("dp") == 1:
        return attn_partials[0]
    return lax.psum_scatter(attn_partials[0], "dp", scatter_dimension=0, tiled=True)


def picked(pick, source):
    return jnp.dot(pick, source, preferred_element_type=jnp.float32)


def pack_kernel(blocks, experts, *refs):
    sources, (*outs, ids_ref, gate_ref, tokens_ref, grads_ref, sems) = refs[:4], refs[4:]
    fetches = [
        pltpu.make_async_copy(source, target, sems.at[k])
        for k, (source, target) in enumerate(
            zip(sources, (ids_ref, gate_ref, tokens_ref, grads_ref))
        )
    ]
    for fetch in fetches:
        fetch.start()
    for fetch in fetches[:2]:
        fetch.wait()
    n, width = tokens_ref.shape
    mine = (lax.axis_index("expert") // SHARDS).astype(jnp.float32)
    ids = ids_ref[...].astype(jnp.float32)
    relative = ids - mine
    relative = jnp.where(relative < 0.0, relative + experts, relative)
    down = lax.broadcasted_iota(jnp.int32, (n, n), 0)
    across = lax.broadcasted_iota(jnp.int32, (n, n), 1)
    ids_down = jnp.sum(jnp.where(down == across, ids, 0.0), axis=1, keepdims=True)
    gate_down = jnp.sum(jnp.where(down == across, gate_ref[...], 0.0), axis=1, keepdims=True)
    rivals = jnp.where((ids_down == ids) & (down < across), 1.0, 0.0)
    rank = jnp.sum(rivals, axis=0, keepdims=True)
    rows, picks = outs[: len(blocks)], outs[len(blocks) : 2 * len(blocks)]
    copies = outs[2 * len(blocks) :]

    def one_hot(shape, block, shift):
        expert, begin, end, row = block
        chosen = (relative == expert) & (rank >= begin) & (rank < end)
        slot = jnp.where(chosen, rank - begin + row + shift, -1.0).astype(jnp.int32)
        slots = lax.broadcasted_iota(jnp.int32, shape, 0)
        return jnp.where(slots == slot, 1.0, 0.0)

    uppers, lowers = [], []
    for k, block in enumerate(blocks):
        shape = picks[k].shape
        uppers.append(one_hot(shape, block, 0))
        lowers.append(uppers[k] if k < 2 else one_hot(shape, block, block[2]))
        picks[k][...] = uppers[k].astype(jnp.bfloat16)
    upper, lower = [jnp.concatenate(p, axis=0).astype(jnp.bfloat16) for p in (uppers, lowers)]
    for fetch in fetches[2:]:
        fetch.wait()
    gated = (gate_down * grads_ref[...].astype(jnp.float32)).astype(jnp.bfloat16)
    from_tokens, from_gated = picked(upper, tokens_ref[...]), picked(lower, gated)
    start = 0
    for k, rows_ref in enumerate(rows):
        part = slice(start, start + rows_ref.shape[0])
        start = part.stop
        if k < 2:
            rows_ref[:, :width] = from_tokens[part].astype(jnp.bfloat16)
            rows_ref[:, width:] = from_gated[part].astype(jnp.bfloat16)
        else:
            rows_ref[...] = (from_tokens[part] + from_gated[part]).astype(jnp.bfloat16)
    for copy_ref in copies:
        copy_ref[...] = rows[0][...]


def pack(blocks, first, rest, capacity, experts, ids, gate, tokens, grads):
    n, width = tokens.shape
    whole = pl.BlockSpec(memory_space=pltpu.VMEM)
    crossing = len(blocks) - 2

    def shape(rows, columns):
        return jax.ShapeDtypeStruct((rows, columns), jnp.bfloat16)

    shapes = [shape(first, 2 * width), shape(rest, 2 * width)]
    shapes += [shape(2 * capacity, width)] * crossing
    shapes += [shape(first, n), shape(rest, n)] + [shape(2 * capacity, n)] * crossing
    shapes += [shape(first, 2 * width)] * len(early_masks)
    sources = (ids.reshape(1, n), gate.reshape(1, n), tokens, grads)
    outs = pl.pallas_call(
        lambda *refs: pack_kernel(blocks, experts, *refs),
        out_shape=shapes,
        in_specs=[pl.BlockSpec(memory_space=pltpu.HBM)] * 4,
        out_specs=[whole] * len(shapes),
        scratch_shapes=[
            pltpu.VMEM((1, n), jnp.int32),
            pltpu.VMEM((1, n), jnp.float32),
            pltpu.VMEM((n, width), jnp.bfloat16),
            pltpu.VMEM((n, width), jnp.bfloat16),
            pltpu.SemaphoreType.DMA((4,)),
        ],
        compiler_params=pltpu.CompilerParams(vmem_limit_bytes=8 * 1024 * 1024),
    )(*[pltpu.with_memory_space_constraint(source, pltpu.HBM) for source in sources])
    return outs[: len(blocks)], outs[len(blocks) : 2 * len(blocks)], outs[2 * len(blocks) :]


def handed_on(copies, sent):
    anywhere = pl.BlockSpec(memory_space=pl.ANY)
    return pl.pallas_call(
        lambda *refs: None,
        out_shape=[jax.ShapeDtypeStruct(rows.shape, rows.dtype) for rows in copies],
        in_specs=[anywhere] * (len(copies) + len(sent)),
        out_specs=[anywhere] * len(copies),
        input_output_aliases={k: k for k in range(len(copies))},
        compiler_params=pltpu.CompilerParams(vmem_limit_bytes=1024 * 1024),
    )(*copies, *sent)


def whole_weights(shard):
    if lax.axis_size("dp") == 1:
        return shard.astype(jnp.bfloat16)
    return lax.all_gather(shard.astype(jnp.bfloat16), "dp", axis=0, tiled=True)


def expert_kernel(scale_in, scale_out, rows_ref, in_ref, out_ref, hidden_ref, pre_ref, parts_ref):
    width = in_ref.shape[1]
    pre_act = contract_cols(rows_ref[:, :width], in_ref[...]) * scale_in
    hidden_ref[...] = gelu_value(pre_act).astype(jnp.bfloat16)
    hidden_grad = contract_cols(rows_ref[:, width:], out_ref[...]) * scale_out
    pre_grad = (hidden_grad * gelu_slope(pre_act)).astype(jnp.bfloat16)
    pre_ref[...] = pre_grad
    for start in range(0, width, 512):
        columns = slice(start, start + 512)
        parts = jnp.dot(pre_grad, in_ref[:, columns], preferred_element_type=jnp.float32)
        parts_ref[:, columns] = (parts * scale_in).astype(jnp.bfloat16)


def worked(rows, weights_in, weights_out, scale_in, scale_out):
    count, (units, width) = rows.shape[0], weights_in.shape
    whole = pl.BlockSpec(memory_space=pltpu.VMEM)
    return pl.pallas_call(
        lambda *refs: expert_kernel(scale_in, scale_out, *refs),
        out_shape=[
            jax.ShapeDtypeStruct((count, columns), jnp.bfloat16)
            for columns in (units, units, width)
        ],
        in_specs=[whole] * 3,
        out_specs=[whole] * 3,
        compiler_params=pltpu.CompilerParams(vmem_limit_bytes=20 * 1024 * 1024),
        cost_estimate=pl.CostEstimate(
            flops=6 * count * units * width,
            bytes_accessed=4 * units * width,
            transcendentals=count * units,
        ),
    )(rows, weights_in, weights_out)


def step_kernel(rows, *refs):
    *refs, done_ref, sems = refs
    count = len(refs) // 3
    bases, shares, outs = refs[:count], refs[count : 2 * count], refs[2 * count :]
    writes = []
    for start in range(0, outs[0].shape[0], rows):
        part = slice(start, start + rows)
        for k in range(count):
            done_ref[k, part] = bases[k][part] - step_rate * shares[k][part].astype(jnp.float32)
            writes.append(
                pltpu.make_async_copy(done_ref.at[k, part], outs[k].at[part], sems.at[len(writes)])
            )
            writes[-1].start()
    for write in writes:
        write.wait()


def stepped(bases, shares):
    units, width = bases[0].shape
    rows = 64 if units % 64 == 0 else units
    whole = pl.BlockSpec(memory_space=pltpu.VMEM)
    return pl.pallas_call(
        lambda *refs: step_kernel(rows, *refs),
        out_shape=[jax.ShapeDtypeStruct(base.shape, base.dtype) for base in bases],
        in_specs=[whole] * (2 * len(bases)),
        out_specs=[pl.BlockSpec(memory_space=pltpu.HBM)] * len(bases),
        scratch_shapes=[
            pltpu.VMEM((len(bases), units, width), jnp.float32),
            pltpu.SemaphoreType.DMA((len(bases) * (units // rows),)),
        ],
        compiler_params=pltpu.CompilerParams(vmem_limit_bytes=16 * 1024 * 1024),
        cost_estimate=pl.CostEstimate(
            flops=4 * units * width, bytes_accessed=8 * units * width, transcendentals=0
        ),
    )(*bases, *shares)


def stepped_over_dp(weights, grads):
    grads = lax.psum_scatter(
        grads.astype(jnp.bfloat16), "dp", scatter_dimension=0, tiled=True
    ).astype(jnp.float32)
    return weights - step_rate * grads


def swap(rows, mask):
    n_expert = lax.axis_size("expert")
    return lax.ppermute(rows, "expert", [(i, i ^ mask) for i in range(n_expert)])


core_bit, x_bit, y_bit, z_bit = 1, 2, 4, 8
early_masks = (x_bit | y_bit, z_bit, x_bit, y_bit)


def after(values, *others):
    return lax.optimization_barrier((others, values))[1]


def chain(blocks):
    chained = []
    for block in blocks:
        chained.append(after(block, chained[-1]) if chained else block)
    return chained


def swaps(blocks, masks):
    return [swap(block, mask) for block, mask in zip(chain(blocks), masks)]


def total(*terms):
    return sum(term.astype(jnp.float32) for term in terms).astype(jnp.bfloat16)


def split_rows(array, rows):
    return [array[k : k + rows] for k in range(0, array.shape[0], rows)]


def shards(tokens, attn_partials, expert_ids, gate, w_in, w_out):
    tok_rows, width = tokens.shape
    n_expert = lax.axis_size("expert")
    experts = n_expert // SHARDS
    capacity = 5 * tok_rows // (8 * experts)
    first = capacity // 8 * 8
    rest = experts * capacity - first
    units = w_in.shape[1]
    scale_in = width ** (-0.5)
    scale_out = FF ** (-0.5)

    def shifted(rows, hops):
        pairs = [(i, (i + SHARDS * hops) % n_expert) for i in range(n_expert)]
        return lax.ppermute(rows, "expert", pairs)

    offset = (experts - 1) * capacity - first
    own_blocks = [(0, 0, first, 0), (0, first, capacity, offset + first)]
    cross_blocks = [(s, 0, capacity, 0) for s in range(1, experts)]
    grads = summed_grads(attn_partials)
    (early_own, late_own, *sent), picks, copies = pack(
        own_blocks + cross_blocks, first, rest, capacity, experts, expert_ids, gate, tokens, grads
    )
    early_copies = handed_on(copies, sent)

    def activated(rows):
        expert_rows, grad_rows = rows[:, :width], rows[:, width:]
        pre_act = contract_cols(expert_rows, weights_in) * scale_in
        hidden = gelu_value(pre_act).astype(jnp.bfloat16)
        hidden_grad = contract_cols(grad_rows, weights_out) * scale_out
        pre_grad = (hidden_grad * gelu_slope(pre_act)).astype(jnp.bfloat16)
        return [expert_rows, grad_rows, hidden, pre_grad]

    def input_parts(pre_grad):
        parts = jnp.dot(pre_grad, weights_in, preferred_element_type=jnp.float32) * scale_in
        return parts.astype(jnp.bfloat16)

    for s in range(1, experts):
        side_by_side = jnp.concatenate(split_rows(shifted(sent[s - 1], s), capacity), axis=1)
        late_own = late_own + jnp.pad(
            side_by_side, (((s - 1) * capacity, rest - s * capacity), (0, 0))
        )
    early_xy, early_z, early_x, early_y = after(
        [swap(rows, mask) for rows, mask in zip(early_copies, early_masks)], late_own
    )
    late_x, late_y, late_z = swaps(
        [
            jnp.concatenate([late_own, early_z], axis=0),
            jnp.concatenate([late_own, early_z], axis=0),
            jnp.concatenate([late_own, early_xy], axis=0),
        ],
        (x_bit, y_bit, z_bit),
    )
    early_zx, early_yz, early_far = late_x[rest:], late_y[rest:], late_z[rest:]
    late_x, late_y, late_z = late_x[:rest], late_y[:rest], late_z[:rest]
    early_rows = [early_own, early_x, early_y, early_z, early_xy, early_yz, early_zx, early_far]

    own_weights = jnp.concatenate([whole_weights(w_in).T, whole_weights(w_out).T], axis=0)
    their_weights = swap(after(own_weights, late_own), core_bit)
    weights_in, weights_out = [
        jnp.concatenate([own_weights[part], their_weights[part]], axis=0)
        for part in (slice(0, units), slice(units, 2 * units))
    ]
    late_xy, late_far, late_yz, late_zx = swaps(
        [late_x, late_x, late_y, late_z],
        (y_bit, y_bit | z_bit, z_bit, x_bit),
    )
    early = activated(jnp.concatenate(early_rows, axis=0))
    early_parts = input_parts(early[3])
    late_far = after([late_xy, late_yz, late_zx, late_far], early_parts)
    late_rows = [late_own, late_x, late_y, late_z, *late_far]
    late_rows = jnp.concatenate(late_rows, axis=0)
    hidden, pre_grad, late_parts = worked(late_rows, weights_in, weights_out, scale_in, scale_out)
    later = [late_rows[:, :width], late_rows[:, width:], hidden, pre_grad]
    parts = [
        jnp.concatenate(pair, axis=0)
        for pair in zip(split_rows(early_parts, first), split_rows(late_parts, rest))
    ]
    own, sum_x, sum_y, sum_z, sum_xy, sum_yz, sum_zx, sum_far = parts
    back = chain([sum_far, sum_zx, sum_xy, sum_yz])
    far, zx, xy, yz = [
        swap(rows, mask) for rows, mask in zip(back, (x_bit | y_bit, x_bit, y_bit, z_bit))
    ]

    def gradients(part, awaited):
        chunks = [chunk[:2] + after(chunk[2:], awaited) for chunk in (early, later)]
        return [
            sum(contract_rows(chunk[left][:, part], chunk[right]) for chunk in chunks) * scale
            for left, right, scale in ((3, 0, scale_in), (2, 1, scale_out))
        ]

    theirs = gradients(slice(units, 2 * units), back[-1])
    theirs = [grads.astype(jnp.bfloat16) for grads in theirs]
    zx, theirs = lax.optimization_barrier((zx, theirs))
    shares = [swap(grads, core_bit) for grads in theirs]
    mine = gradients(slice(0, units), zx)
    split_width = lax.axis_size("dp") > 1
    if not split_width:
        mine = [weights.T - step_rate * grads for weights, grads in zip((w_in, w_out), mine)]
    if split_width:
        new_weights = [
            stepped_over_dp(weights, (grads + share.astype(jnp.float32)).T)
            for weights, grads, share in zip((w_in, w_out), mine, shares)
        ]
    else:
        new_weights = [weights.T for weights in stepped(mine, shares)]
    near = swaps(
        [total(sum_z, zx, far), total(sum_x, xy), total(sum_y, yz)], (z_bit, x_bit, y_bit)
    )
    sums = total(own, *near)
    early_sum, late_sum = sums[:first], sums[first:]
    half = width // 2
    returned = [early_sum, late_sum]
    for s in range(1, experts):
        rows = late_sum[(s - 1) * capacity : s * capacity]
        rows = jnp.concatenate([rows[:, :half], rows[:, half:]], axis=0)
        rows = after(shifted(rows, -s), new_weights)
        returned.append(jnp.concatenate(split_rows(rows, capacity), axis=1))
    picks = [*picks[:2], *[pick[:capacity] for pick in picks[2:]]]
    token_grad = sum(contract_rows(pick, rows) for pick, rows in zip(picks, returned))
    return (token_grad.astype(jnp.bfloat16), *new_weights)


def solution(mesh):
    in_specs = (
        P(("expert", "dp"), None),
        P("dp", "expert", None),
        P(("expert", "dp")),
        P(("expert", "dp")),
        P("dp", "expert"),
        P("dp", "expert"),
    )
    out_specs = (P(("expert", "dp"), None), P("dp", "expert"), P("dp", "expert"))
    return jax.shard_map(shards, mesh=mesh, in_specs=in_specs, out_specs=out_specs, check_vma=False)
```

```python
import jax
import jax.numpy as jnp
from jax import lax
from jax.experimental import pallas as pl
from jax.experimental.pallas import tpu as pltpu
from jax.sharding import PartitionSpec as P

FF = 5120
SHARDS = 16


gelu_coef = 0.7978845608028654
cubic_coef = 0.044715
step_rate = 0.5


def gelu_value(inputs):
    return (
        0.5
        * inputs
        * (1.0 + jnp.tanh(gelu_coef * (inputs + cubic_coef * inputs * inputs * inputs)))
    )


def gelu_slope(inputs):
    tangent = jnp.tanh(gelu_coef * (inputs + cubic_coef * inputs * inputs * inputs))
    return 0.5 * (1.0 + tangent) + 0.5 * inputs * (1.0 - tangent * tangent) * gelu_coef * (
        1.0 + 3.0 * cubic_coef * inputs * inputs
    )


def contract_rows(left, right):
    return lax.dot_general(
        left, right, (((0,), (0,)), ((), ())), preferred_element_type=jnp.float32
    )


def contract_cols(left, right):
    return lax.dot_general(
        left, right, (((1,), (1,)), ((), ())), preferred_element_type=jnp.float32
    )


def summed_grads(attn_partials):
    if lax.axis_size("dp") == 1:
        return attn_partials[0]
    return lax.psum_scatter(attn_partials[0], "dp", scatter_dimension=0, tiled=True)


def picked(pick, source):
    return jnp.dot(pick, source, preferred_element_type=jnp.float32)


def pack_kernel(blocks, experts, *refs):
    sources, (*outs, ids_ref, gate_ref, tokens_ref, grads_ref, sems) = refs[:4], refs[4:]
    fetches = [
        pltpu.make_async_copy(source, target, sems.at[k])
        for k, (source, target) in enumerate(
            zip(sources, (ids_ref, gate_ref, tokens_ref, grads_ref))
        )
    ]
    for fetch in fetches:
        fetch.start()
    for fetch in fetches[:2]:
        fetch.wait()
    n, width = tokens_ref.shape
    mine = (lax.axis_index("expert") // SHARDS).astype(jnp.float32)
    ids = ids_ref[...].astype(jnp.float32)
    relative = ids - mine
    relative = jnp.where(relative < 0.0, relative + experts, relative)
    down = lax.broadcasted_iota(jnp.int32, (n, n), 0)
    across = lax.broadcasted_iota(jnp.int32, (n, n), 1)
    ids_down = jnp.sum(jnp.where(down == across, ids, 0.0), axis=1, keepdims=True)
    gate_down = jnp.sum(jnp.where(down == across, gate_ref[...], 0.0), axis=1, keepdims=True)
    rivals = jnp.where((ids_down == ids) & (down < across), 1.0, 0.0)
    rank = jnp.sum(rivals, axis=0, keepdims=True)
    rows, picks = outs[: len(blocks)], outs[len(blocks) : 2 * len(blocks)]
    copies = outs[2 * len(blocks) :]

    def one_hot(shape, block, shift):
        expert, begin, end, row = block
        chosen = (relative == expert) & (rank >= begin) & (rank < end)
        slot = jnp.where(chosen, rank - begin + row + shift, -1.0).astype(jnp.int32)
        slots = lax.broadcasted_iota(jnp.int32, shape, 0)
        return jnp.where(slots == slot, 1.0, 0.0)

    uppers, lowers = [], []
    for k, block in enumerate(blocks):
        shape = picks[k].shape
        uppers.append(one_hot(shape, block, 0))
        lowers.append(uppers[k] if k < 2 else one_hot(shape, block, block[2]))
        picks[k][...] = uppers[k].astype(jnp.bfloat16)
    upper, lower = [jnp.concatenate(p, axis=0).astype(jnp.bfloat16) for p in (uppers, lowers)]
    for fetch in fetches[2:]:
        fetch.wait()
    gated = (gate_down * grads_ref[...].astype(jnp.float32)).astype(jnp.bfloat16)
    from_tokens, from_gated = picked(upper, tokens_ref[...]), picked(lower, gated)
    start = 0
    for k, rows_ref in enumerate(rows):
        part = slice(start, start + rows_ref.shape[0])
        start = part.stop
        if k < 2:
            rows_ref[:, :width] = from_tokens[part].astype(jnp.bfloat16)
            rows_ref[:, width:] = from_gated[part].astype(jnp.bfloat16)
        else:
            rows_ref[...] = (from_tokens[part] + from_gated[part]).astype(jnp.bfloat16)
    for copy_ref in copies:
        copy_ref[...] = rows[0][...]


def pack(blocks, first, rest, capacity, experts, ids, gate, tokens, grads):
    n, width = tokens.shape
    whole = pl.BlockSpec(memory_space=pltpu.VMEM)
    crossing = len(blocks) - 2

    def shape(rows, columns):
        return jax.ShapeDtypeStruct((rows, columns), jnp.bfloat16)

    shapes = [shape(first, 2 * width), shape(rest, 2 * width)]
    shapes += [shape(2 * capacity, width)] * crossing
    shapes += [shape(first, n), shape(rest, n)] + [shape(2 * capacity, n)] * crossing
    shapes += [shape(first, 2 * width)] * len(early_masks)
    sources = (ids.reshape(1, n), gate.reshape(1, n), tokens, grads)
    outs = pl.pallas_call(
        lambda *refs: pack_kernel(blocks, experts, *refs),
        out_shape=shapes,
        in_specs=[pl.BlockSpec(memory_space=pltpu.HBM)] * 4,
        out_specs=[whole] * len(shapes),
        scratch_shapes=[
            pltpu.VMEM((1, n), jnp.int32),
            pltpu.VMEM((1, n), jnp.float32),
            pltpu.VMEM((n, width), jnp.bfloat16),
            pltpu.VMEM((n, width), jnp.bfloat16),
            pltpu.SemaphoreType.DMA((4,)),
        ],
        compiler_params=pltpu.CompilerParams(vmem_limit_bytes=8 * 1024 * 1024),
    )(*[pltpu.with_memory_space_constraint(source, pltpu.HBM) for source in sources])
    return outs[: len(blocks)], outs[len(blocks) : 2 * len(blocks)], outs[2 * len(blocks) :]


def handed_on(copies, sent):
    anywhere = pl.BlockSpec(memory_space=pl.ANY)
    return pl.pallas_call(
        lambda *refs: None,
        out_shape=[jax.ShapeDtypeStruct(rows.shape, rows.dtype) for rows in copies],
        in_specs=[anywhere] * (len(copies) + len(sent)),
        out_specs=[anywhere] * len(copies),
        input_output_aliases={k: k for k in range(len(copies))},
        compiler_params=pltpu.CompilerParams(vmem_limit_bytes=1024 * 1024),
    )(*copies, *sent)


def whole_weights(shard):
    if lax.axis_size("dp") == 1:
        return shard.astype(jnp.bfloat16)
    return lax.all_gather(shard.astype(jnp.bfloat16), "dp", axis=0, tiled=True)


def expert_kernel(scale_in, scale_out, rows_ref, in_ref, out_ref, hidden_ref, pre_ref, parts_ref):
    width = in_ref.shape[1]
    pre_act = contract_cols(rows_ref[:, :width], in_ref[...]) * scale_in
    hidden_ref[...] = gelu_value(pre_act).astype(jnp.bfloat16)
    hidden_grad = contract_cols(rows_ref[:, width:], out_ref[...]) * scale_out
    pre_grad = (hidden_grad * gelu_slope(pre_act)).astype(jnp.bfloat16)
    pre_ref[...] = pre_grad
    for start in range(0, width, 512):
        columns = slice(start, start + 512)
        parts = jnp.dot(pre_grad, in_ref[:, columns], preferred_element_type=jnp.float32)
        parts_ref[:, columns] = (parts * scale_in).astype(jnp.bfloat16)


def worked(rows, weights_in, weights_out, scale_in, scale_out):
    count, (units, width) = rows.shape[0], weights_in.shape
    whole = pl.BlockSpec(memory_space=pltpu.VMEM)
    return pl.pallas_call(
        lambda *refs: expert_kernel(scale_in, scale_out, *refs),
        out_shape=[
            jax.ShapeDtypeStruct((count, columns), jnp.bfloat16)
            for columns in (units, units, width)
        ],
        in_specs=[whole] * 3,
        out_specs=[whole] * 3,
        compiler_params=pltpu.CompilerParams(vmem_limit_bytes=20 * 1024 * 1024),
        cost_estimate=pl.CostEstimate(
            flops=6 * count * units * width,
            bytes_accessed=4 * units * width,
            transcendentals=count * units,
        ),
    )(rows, weights_in, weights_out)


def step_kernel(rows, *refs):
    *refs, done_ref, sems = refs
    count = len(refs) // 3
    bases, shares, outs = refs[:count], refs[count : 2 * count], refs[2 * count :]
    writes = []
    for start in range(0, outs[0].shape[0], rows):
        part = slice(start, start + rows)
        for k in range(count):
            done_ref[k, part] = bases[k][part] - step_rate * shares[k][part].astype(jnp.float32)
            writes.append(
                pltpu.make_async_copy(done_ref.at[k, part], outs[k].at[part], sems.at[len(writes)])
            )
            writes[-1].start()
    for write in writes:
        write.wait()


def stepped(bases, shares):
    units, width = bases[0].shape
    rows = 64 if units % 64 == 0 else units
    whole = pl.BlockSpec(memory_space=pltpu.VMEM)
    return pl.pallas_call(
        lambda *refs: step_kernel(rows, *refs),
        out_shape=[jax.ShapeDtypeStruct(base.shape, base.dtype) for base in bases],
        in_specs=[whole] * (2 * len(bases)),
        out_specs=[pl.BlockSpec(memory_space=pltpu.HBM)] * len(bases),
        scratch_shapes=[
            pltpu.VMEM((len(bases), units, width), jnp.float32),
            pltpu.SemaphoreType.DMA((len(bases) * (units // rows),)),
        ],
        compiler_params=pltpu.CompilerParams(vmem_limit_bytes=16 * 1024 * 1024),
        cost_estimate=pl.CostEstimate(
            flops=4 * units * width, bytes_accessed=8 * units * width, transcendentals=0
        ),
    )(*bases, *shares)


def stepped_over_dp(weights, grads):
    grads = lax.psum_scatter(
        grads.astype(jnp.bfloat16), "dp", scatter_dimension=0, tiled=True
    ).astype(jnp.float32)
    return weights - step_rate * grads


def swap(rows, mask):
    n_expert = lax.axis_size("expert")
    return lax.ppermute(rows, "expert", [(i, i ^ mask) for i in range(n_expert)])


core_bit, x_bit, y_bit, z_bit = 1, 2, 4, 8
early_masks = (x_bit | y_bit, z_bit, x_bit, y_bit)


def after(values, *others):
    return lax.optimization_barrier((others, values))[1]


def chain(blocks):
    chained = []
    for block in blocks:
        chained.append(after(block, chained[-1]) if chained else block)
    return chained


def swaps(blocks, masks):
    return [swap(block, mask) for block, mask in zip(chain(blocks), masks)]


def total(*terms):
    return sum(term.astype(jnp.float32) for term in terms).astype(jnp.bfloat16)


def split_rows(array, rows):
    return [array[k : k + rows] for k in range(0, array.shape[0], rows)]


def shards(tokens, attn_partials, expert_ids, gate, w_in, w_out):
    tok_rows, width = tokens.shape
    n_expert = lax.axis_size("expert")
    experts = n_expert // SHARDS
    capacity = 5 * tok_rows // (8 * experts)
    first = capacity // 8 * 8
    rest = experts * capacity - first
    units = w_in.shape[1]
    scale_in = width ** (-0.5)
    scale_out = FF ** (-0.5)

    def shifted(rows, hops):
        pairs = [(i, (i + SHARDS * hops) % n_expert) for i in range(n_expert)]
        return lax.ppermute(rows, "expert", pairs)

    offset = (experts - 1) * capacity - first
    own_blocks = [(0, 0, first, 0), (0, first, capacity, offset + first)]
    cross_blocks = [(s, 0, capacity, 0) for s in range(1, experts)]
    grads = summed_grads(attn_partials)
    (early_own, late_own, *sent), picks, copies = pack(
        own_blocks + cross_blocks, first, rest, capacity, experts, expert_ids, gate, tokens, grads
    )
    early_copies = handed_on(copies, sent)

    def activated(rows):
        expert_rows, grad_rows = rows[:, :width], rows[:, width:]
        pre_act = contract_cols(expert_rows, weights_in) * scale_in
        hidden = gelu_value(pre_act).astype(jnp.bfloat16)
        hidden_grad = contract_cols(grad_rows, weights_out) * scale_out
        pre_grad = (hidden_grad * gelu_slope(pre_act)).astype(jnp.bfloat16)
        return [expert_rows, grad_rows, hidden, pre_grad]

    def input_parts(pre_grad):
        parts = jnp.dot(pre_grad, weights_in, preferred_element_type=jnp.float32) * scale_in
        return parts.astype(jnp.bfloat16)

    for s in range(1, experts):
        side_by_side = jnp.concatenate(split_rows(shifted(sent[s - 1], s), capacity), axis=1)
        late_own = late_own + jnp.pad(
            side_by_side, (((s - 1) * capacity, rest - s * capacity), (0, 0))
        )
    early_xy, early_z, early_x, early_y = after(
        [swap(rows, mask) for rows, mask in zip(early_copies, early_masks)], late_own
    )
    late_x, late_y, late_z = swaps(
        [
            jnp.concatenate([late_own, early_z], axis=0),
            jnp.concatenate([late_own, early_z], axis=0),
            jnp.concatenate([late_own, early_xy], axis=0),
        ],
        (x_bit, y_bit, z_bit),
    )
    early_zx, early_yz, early_far = late_x[rest:], late_y[rest:], late_z[rest:]
    late_x, late_y, late_z = late_x[:rest], late_y[:rest], late_z[:rest]
    early_rows = [early_own, early_x, early_y, early_z, early_xy, early_yz, early_zx, early_far]

    own_weights = jnp.concatenate([whole_weights(w_in).T, whole_weights(w_out).T], axis=0)
    their_weights = swap(after(own_weights, late_own), core_bit)
    weights_in, weights_out = [
        jnp.concatenate([own_weights[part], their_weights[part]], axis=0)
        for part in (slice(0, units), slice(units, 2 * units))
    ]
    late_xy, late_far, late_yz, late_zx = swaps(
        [late_x, late_x, late_y, late_z],
        (y_bit, y_bit | z_bit, z_bit, x_bit),
    )
    early = activated(jnp.concatenate(early_rows, axis=0))
    early_parts = input_parts(early[3])
    late_far = after([late_xy, late_yz, late_zx, late_far], early_parts)
    late_rows = [late_own, late_x, late_y, late_z, *late_far]
    late_rows = jnp.concatenate(late_rows, axis=0)
    hidden, pre_grad, late_parts = worked(late_rows, weights_in, weights_out, scale_in, scale_out)
    later = [late_rows[:, :width], late_rows[:, width:], hidden, pre_grad]
    parts = [
        jnp.concatenate(pair, axis=0)
        for pair in zip(split_rows(early_parts, first), split_rows(late_parts, rest))
    ]
    own, sum_x, sum_y, sum_z, sum_xy, sum_yz, sum_zx, sum_far = parts
    back = chain([sum_far, sum_zx, sum_yz, sum_xy])
    far, zx, yz, xy = [
        swap(rows, mask) for rows, mask in zip(back, (y_bit | z_bit, x_bit, z_bit, y_bit))
    ]

    def gradients(part, awaited):
        chunks = [chunk[:2] + after(chunk[2:], awaited) for chunk in (early, later)]
        return [
            sum(contract_rows(chunk[left][:, part], chunk[right]) for chunk in chunks) * scale
            for left, right, scale in ((3, 0, scale_in), (2, 1, scale_out))
        ]

    theirs = gradients(slice(units, 2 * units), back[-1])
    theirs = [grads.astype(jnp.bfloat16) for grads in theirs]
    zx, theirs = lax.optimization_barrier((zx, theirs))
    shares = [swap(grads, core_bit) for grads in theirs]
    mine = gradients(slice(0, units), zx)
    split_width = lax.axis_size("dp") > 1
    if not split_width:
        mine = [weights.T - step_rate * grads for weights, grads in zip((w_in, w_out), mine)]
    if split_width:
        new_weights = [
            stepped_over_dp(weights, (grads + share.astype(jnp.float32)).T)
            for weights, grads, share in zip((w_in, w_out), mine, shares)
        ]
    else:
        new_weights = [weights.T for weights in stepped(mine, shares)]
    near = swaps(
        [total(sum_z, zx), total(sum_y, yz), total(sum_x, xy, far)], (z_bit, y_bit, x_bit)
    )
    sums = total(own, *near)
    early_sum, late_sum = sums[:first], sums[first:]
    half = width // 2
    returned = [early_sum, late_sum]
    for s in range(1, experts):
        rows = late_sum[(s - 1) * capacity : s * capacity]
        rows = jnp.concatenate([rows[:, :half], rows[:, half:]], axis=0)
        rows = after(shifted(rows, -s), new_weights)
        returned.append(jnp.concatenate(split_rows(rows, capacity), axis=1))
    picks = [*picks[:2], *[pick[:capacity] for pick in picks[2:]]]
    token_grad = sum(contract_rows(pick, rows) for pick, rows in zip(picks, returned))
    return (token_grad.astype(jnp.bfloat16), *new_weights)


def solution(mesh):
    in_specs = (
        P(("expert", "dp"), None),
        P("dp", "expert", None),
        P(("expert", "dp")),
        P(("expert", "dp")),
        P("dp", "expert"),
        P("dp", "expert"),
    )
    out_specs = (P(("expert", "dp"), None), P("dp", "expert"), P("dp", "expert"))
    return jax.shard_map(shards, mesh=mesh, in_specs=in_specs, out_specs=out_specs, check_vma=False)
```

```python
import jax
import jax.numpy as jnp
from jax import lax
from jax.experimental import pallas as pl
from jax.experimental.pallas import tpu as pltpu
from jax.sharding import PartitionSpec as P

FF = 5120
SHARDS = 16


gelu_coef = 0.7978845608028654
cubic_coef = 0.044715
step_rate = 0.5


def gelu_value(inputs):
    return (
        0.5
        * inputs
        * (1.0 + jnp.tanh(gelu_coef * (inputs + cubic_coef * inputs * inputs * inputs)))
    )


def gelu_slope(inputs):
    tangent = jnp.tanh(gelu_coef * (inputs + cubic_coef * inputs * inputs * inputs))
    return 0.5 * (1.0 + tangent) + 0.5 * inputs * (1.0 - tangent * tangent) * gelu_coef * (
        1.0 + 3.0 * cubic_coef * inputs * inputs
    )


def contract_rows(left, right):
    return lax.dot_general(
        left, right, (((0,), (0,)), ((), ())), preferred_element_type=jnp.float32
    )


def contract_cols(left, right):
    return lax.dot_general(
        left, right, (((1,), (1,)), ((), ())), preferred_element_type=jnp.float32
    )


def summed_grads(attn_partials):
    if lax.axis_size("dp") == 1:
        return attn_partials[0]
    return lax.psum_scatter(attn_partials[0], "dp", scatter_dimension=0, tiled=True)


def picked(pick, source):
    return jnp.dot(pick, source, preferred_element_type=jnp.float32)


def pack_kernel(blocks, experts, *refs):
    sources, (*outs, ids_ref, gate_ref, tokens_ref, grads_ref, sems) = refs[:4], refs[4:]
    fetches = [
        pltpu.make_async_copy(source, target, sems.at[k])
        for k, (source, target) in enumerate(
            zip(sources, (ids_ref, gate_ref, tokens_ref, grads_ref))
        )
    ]
    for fetch in fetches:
        fetch.start()
    for fetch in fetches[:2]:
        fetch.wait()
    n, width = tokens_ref.shape
    mine = (lax.axis_index("expert") // SHARDS).astype(jnp.float32)
    ids = ids_ref[...].astype(jnp.float32)
    relative = ids - mine
    relative = jnp.where(relative < 0.0, relative + experts, relative)
    down = lax.broadcasted_iota(jnp.int32, (n, n), 0)
    across = lax.broadcasted_iota(jnp.int32, (n, n), 1)
    ids_down = jnp.sum(jnp.where(down == across, ids, 0.0), axis=1, keepdims=True)
    gate_down = jnp.sum(jnp.where(down == across, gate_ref[...], 0.0), axis=1, keepdims=True)
    rivals = jnp.where((ids_down == ids) & (down < across), 1.0, 0.0)
    rank = jnp.sum(rivals, axis=0, keepdims=True)
    rows, picks = outs[: len(blocks)], outs[len(blocks) : 2 * len(blocks)]
    copies = outs[2 * len(blocks) :]

    def one_hot(shape, block, shift):
        expert, begin, end, row = block
        chosen = (relative == expert) & (rank >= begin) & (rank < end)
        slot = jnp.where(chosen, rank - begin + row + shift, -1.0).astype(jnp.int32)
        slots = lax.broadcasted_iota(jnp.int32, shape, 0)
        return jnp.where(slots == slot, 1.0, 0.0)

    uppers, lowers = [], []
    for k, block in enumerate(blocks):
        shape = picks[k].shape
        uppers.append(one_hot(shape, block, 0))
        lowers.append(uppers[k] if k < 2 else one_hot(shape, block, block[2]))
        picks[k][...] = uppers[k].astype(jnp.bfloat16)
    upper, lower = [jnp.concatenate(p, axis=0).astype(jnp.bfloat16) for p in (uppers, lowers)]
    for fetch in fetches[2:]:
        fetch.wait()
    gated = (gate_down * grads_ref[...].astype(jnp.float32)).astype(jnp.bfloat16)
    from_tokens, from_gated = picked(upper, tokens_ref[...]), picked(lower, gated)
    start = 0
    for k, rows_ref in enumerate(rows):
        part = slice(start, start + rows_ref.shape[0])
        start = part.stop
        if k < 2:
            rows_ref[:, :width] = from_tokens[part].astype(jnp.bfloat16)
            rows_ref[:, width:] = from_gated[part].astype(jnp.bfloat16)
        else:
            rows_ref[...] = (from_tokens[part] + from_gated[part]).astype(jnp.bfloat16)
    for copy_ref in copies:
        copy_ref[...] = rows[0][...]


def pack(blocks, first, rest, capacity, experts, ids, gate, tokens, grads):
    n, width = tokens.shape
    whole = pl.BlockSpec(memory_space=pltpu.VMEM)
    crossing = len(blocks) - 2

    def shape(rows, columns):
        return jax.ShapeDtypeStruct((rows, columns), jnp.bfloat16)

    shapes = [shape(first, 2 * width), shape(rest, 2 * width)]
    shapes += [shape(2 * capacity, width)] * crossing
    shapes += [shape(first, n), shape(rest, n)] + [shape(2 * capacity, n)] * crossing
    shapes += [shape(first, 2 * width)] * len(early_masks)
    sources = (ids.reshape(1, n), gate.reshape(1, n), tokens, grads)
    outs = pl.pallas_call(
        lambda *refs: pack_kernel(blocks, experts, *refs),
        out_shape=shapes,
        in_specs=[pl.BlockSpec(memory_space=pltpu.HBM)] * 4,
        out_specs=[whole] * len(shapes),
        scratch_shapes=[
            pltpu.VMEM((1, n), jnp.int32),
            pltpu.VMEM((1, n), jnp.float32),
            pltpu.VMEM((n, width), jnp.bfloat16),
            pltpu.VMEM((n, width), jnp.bfloat16),
            pltpu.SemaphoreType.DMA((4,)),
        ],
        compiler_params=pltpu.CompilerParams(vmem_limit_bytes=8 * 1024 * 1024),
    )(*[pltpu.with_memory_space_constraint(source, pltpu.HBM) for source in sources])
    return outs[: len(blocks)], outs[len(blocks) : 2 * len(blocks)], outs[2 * len(blocks) :]


def handed_on(copies, sent):
    anywhere = pl.BlockSpec(memory_space=pl.ANY)
    return pl.pallas_call(
        lambda *refs: None,
        out_shape=[jax.ShapeDtypeStruct(rows.shape, rows.dtype) for rows in copies],
        in_specs=[anywhere] * (len(copies) + len(sent)),
        out_specs=[anywhere] * len(copies),
        input_output_aliases={k: k for k in range(len(copies))},
        compiler_params=pltpu.CompilerParams(vmem_limit_bytes=1024 * 1024),
    )(*copies, *sent)


def whole_weights(shard):
    if lax.axis_size("dp") == 1:
        return shard.astype(jnp.bfloat16)
    return lax.all_gather(shard.astype(jnp.bfloat16), "dp", axis=0, tiled=True)


def expert_kernel(scale_in, scale_out, rows_ref, in_ref, out_ref, hidden_ref, pre_ref, parts_ref):
    width = in_ref.shape[1]
    pre_act = contract_cols(rows_ref[:, :width], in_ref[...]) * scale_in
    hidden_ref[...] = gelu_value(pre_act).astype(jnp.bfloat16)
    hidden_grad = contract_cols(rows_ref[:, width:], out_ref[...]) * scale_out
    pre_grad = (hidden_grad * gelu_slope(pre_act)).astype(jnp.bfloat16)
    pre_ref[...] = pre_grad
    for start in range(0, width, 512):
        columns = slice(start, start + 512)
        parts = jnp.dot(pre_grad, in_ref[:, columns], preferred_element_type=jnp.float32)
        parts_ref[:, columns] = (parts * scale_in).astype(jnp.bfloat16)


def worked(rows, weights_in, weights_out, scale_in, scale_out):
    count, (units, width) = rows.shape[0], weights_in.shape
    whole = pl.BlockSpec(memory_space=pltpu.VMEM)
    return pl.pallas_call(
        lambda *refs: expert_kernel(scale_in, scale_out, *refs),
        out_shape=[
            jax.ShapeDtypeStruct((count, columns), jnp.bfloat16)
            for columns in (units, units, width)
        ],
        in_specs=[whole] * 3,
        out_specs=[whole] * 3,
        compiler_params=pltpu.CompilerParams(vmem_limit_bytes=20 * 1024 * 1024),
        cost_estimate=pl.CostEstimate(
            flops=6 * count * units * width,
            bytes_accessed=4 * units * width,
            transcendentals=count * units,
        ),
    )(rows, weights_in, weights_out)


def step_kernel(rows, *refs):
    *refs, done_ref, sems = refs
    count = len(refs) // 3
    bases, shares, outs = refs[:count], refs[count : 2 * count], refs[2 * count :]
    writes = []
    for start in range(0, outs[0].shape[0], rows):
        part = slice(start, start + rows)
        for k in range(count):
            done_ref[k, part] = bases[k][part] - step_rate * shares[k][part].astype(jnp.float32)
            writes.append(
                pltpu.make_async_copy(done_ref.at[k, part], outs[k].at[part], sems.at[len(writes)])
            )
            writes[-1].start()
    for write in writes:
        write.wait()


def stepped(bases, shares):
    units, width = bases[0].shape
    rows = 64 if units % 64 == 0 else units
    whole = pl.BlockSpec(memory_space=pltpu.VMEM)
    return pl.pallas_call(
        lambda *refs: step_kernel(rows, *refs),
        out_shape=[jax.ShapeDtypeStruct(base.shape, base.dtype) for base in bases],
        in_specs=[whole] * (2 * len(bases)),
        out_specs=[pl.BlockSpec(memory_space=pltpu.HBM)] * len(bases),
        scratch_shapes=[
            pltpu.VMEM((len(bases), units, width), jnp.float32),
            pltpu.SemaphoreType.DMA((len(bases) * (units // rows),)),
        ],
        compiler_params=pltpu.CompilerParams(vmem_limit_bytes=16 * 1024 * 1024),
        cost_estimate=pl.CostEstimate(
            flops=4 * units * width, bytes_accessed=8 * units * width, transcendentals=0
        ),
    )(*bases, *shares)


def stepped_over_dp(weights, grads):
    grads = lax.psum_scatter(
        grads.astype(jnp.bfloat16), "dp", scatter_dimension=0, tiled=True
    ).astype(jnp.float32)
    return weights - step_rate * grads


def swap(rows, mask):
    n_expert = lax.axis_size("expert")
    return lax.ppermute(rows, "expert", [(i, i ^ mask) for i in range(n_expert)])


core_bit, x_bit, y_bit, z_bit = 1, 2, 4, 8
early_masks = (x_bit | y_bit, z_bit, x_bit, y_bit)


def after(values, *others):
    return lax.optimization_barrier((others, values))[1]


def chain(blocks):
    chained = []
    for block in blocks:
        chained.append(after(block, chained[-1]) if chained else block)
    return chained


def swaps(blocks, masks):
    return [swap(block, mask) for block, mask in zip(chain(blocks), masks)]


def total(*terms):
    return sum(term.astype(jnp.float32) for term in terms).astype(jnp.bfloat16)


def split_rows(array, rows):
    return [array[k : k + rows] for k in range(0, array.shape[0], rows)]


def shards(tokens, attn_partials, expert_ids, gate, w_in, w_out):
    tok_rows, width = tokens.shape
    n_expert = lax.axis_size("expert")
    experts = n_expert // SHARDS
    capacity = 5 * tok_rows // (8 * experts)
    first = capacity // 8 * 8
    rest = experts * capacity - first
    units = w_in.shape[1]
    scale_in = width ** (-0.5)
    scale_out = FF ** (-0.5)

    def shifted(rows, hops):
        pairs = [(i, (i + SHARDS * hops) % n_expert) for i in range(n_expert)]
        return lax.ppermute(rows, "expert", pairs)

    offset = (experts - 1) * capacity - first
    own_blocks = [(0, 0, first, 0), (0, first, capacity, offset + first)]
    cross_blocks = [(s, 0, capacity, 0) for s in range(1, experts)]
    grads = summed_grads(attn_partials)
    (early_own, late_own, *sent), picks, copies = pack(
        own_blocks + cross_blocks, first, rest, capacity, experts, expert_ids, gate, tokens, grads
    )
    early_copies = handed_on(copies, sent)

    def activated(rows):
        expert_rows, grad_rows = rows[:, :width], rows[:, width:]
        pre_act = contract_cols(expert_rows, weights_in) * scale_in
        hidden = gelu_value(pre_act).astype(jnp.bfloat16)
        hidden_grad = contract_cols(grad_rows, weights_out) * scale_out
        pre_grad = (hidden_grad * gelu_slope(pre_act)).astype(jnp.bfloat16)
        return [expert_rows, grad_rows, hidden, pre_grad]

    def input_parts(pre_grad):
        parts = jnp.dot(pre_grad, weights_in, preferred_element_type=jnp.float32) * scale_in
        return parts.astype(jnp.bfloat16)

    for s in range(1, experts):
        side_by_side = jnp.concatenate(split_rows(shifted(sent[s - 1], s), capacity), axis=1)
        late_own = late_own + jnp.pad(
            side_by_side, (((s - 1) * capacity, rest - s * capacity), (0, 0))
        )
    early_xy, early_z, early_x, early_y = after(
        [swap(rows, mask) for rows, mask in zip(early_copies, early_masks)], late_own
    )
    late_x, late_y, late_z = swaps(
        [
            jnp.concatenate([late_own, early_z], axis=0),
            jnp.concatenate([late_own, early_z], axis=0),
            jnp.concatenate([late_own, early_xy], axis=0),
        ],
        (x_bit, y_bit, z_bit),
    )
    early_zx, early_yz, early_far = late_x[rest:], late_y[rest:], late_z[rest:]
    late_x, late_y, late_z = late_x[:rest], late_y[:rest], late_z[:rest]
    early_rows = [early_own, early_x, early_y, early_z, early_xy, early_yz, early_zx, early_far]

    own_weights = jnp.concatenate([whole_weights(w_in).T, whole_weights(w_out).T], axis=0)
    their_weights = swap(after(own_weights, late_own), core_bit)
    weights_in, weights_out = [
        jnp.concatenate([own_weights[part], their_weights[part]], axis=0)
        for part in (slice(0, units), slice(units, 2 * units))
    ]
    late_xy, late_far, late_yz, late_zx = swaps(
        [late_x, late_x, late_y, late_z],
        (y_bit, y_bit | z_bit, z_bit, x_bit),
    )
    early = activated(jnp.concatenate(early_rows, axis=0))
    early_parts = input_parts(early[3])
    late_far = after([late_xy, late_yz, late_zx, late_far], early_parts)
    late_rows = [late_own, late_x, late_y, late_z, *late_far]
    late_rows = jnp.concatenate(late_rows, axis=0)
    hidden, pre_grad, late_parts = worked(late_rows, weights_in, weights_out, scale_in, scale_out)
    later = [late_rows[:, :width], late_rows[:, width:], hidden, pre_grad]
    parts = [
        jnp.concatenate(pair, axis=0)
        for pair in zip(split_rows(early_parts, first), split_rows(late_parts, rest))
    ]
    own, sum_x, sum_y, sum_z, sum_xy, sum_yz, sum_zx, sum_far = parts
    back = chain([sum_zx, sum_far, sum_yz, sum_xy])
    zx, far, yz, xy = [
        swap(rows, mask) for rows, mask in zip(back, (x_bit, y_bit | z_bit, z_bit, y_bit))
    ]

    def gradients(part, awaited):
        chunks = [chunk[:2] + after(chunk[2:], awaited) for chunk in (early, later)]
        return [
            sum(contract_rows(chunk[left][:, part], chunk[right]) for chunk in chunks) * scale
            for left, right, scale in ((3, 0, scale_in), (2, 1, scale_out))
        ]

    theirs = gradients(slice(units, 2 * units), back[-1])
    theirs = [grads.astype(jnp.bfloat16) for grads in theirs]
    zx, theirs = lax.optimization_barrier((zx, theirs))
    shares = [swap(grads, core_bit) for grads in theirs]
    mine = gradients(slice(0, units), zx)
    split_width = lax.axis_size("dp") > 1
    if not split_width:
        mine = [weights.T - step_rate * grads for weights, grads in zip((w_in, w_out), mine)]
    if split_width:
        new_weights = [
            stepped_over_dp(weights, (grads + share.astype(jnp.float32)).T)
            for weights, grads, share in zip((w_in, w_out), mine, shares)
        ]
    else:
        new_weights = [weights.T for weights in stepped(mine, shares)]
    near = swaps(
        [total(sum_z, zx), total(sum_y, yz), total(sum_x, xy, far)], (z_bit, y_bit, x_bit)
    )
    sums = total(own, *near)
    early_sum, late_sum = sums[:first], sums[first:]
    half = width // 2
    returned = [early_sum, late_sum]
    for s in range(1, experts):
        rows = late_sum[(s - 1) * capacity : s * capacity]
        rows = jnp.concatenate([rows[:, :half], rows[:, half:]], axis=0)
        rows = after(shifted(rows, -s), new_weights)
        returned.append(jnp.concatenate(split_rows(rows, capacity), axis=1))
    picks = [*picks[:2], *[pick[:capacity] for pick in picks[2:]]]
    token_grad = sum(contract_rows(pick, rows) for pick, rows in zip(picks, returned))
    return (token_grad.astype(jnp.bfloat16), *new_weights)


def solution(mesh):
    in_specs = (
        P(("expert", "dp"), None),
        P("dp", "expert", None),
        P(("expert", "dp")),
        P(("expert", "dp")),
        P("dp", "expert"),
        P("dp", "expert"),
    )
    out_specs = (P(("expert", "dp"), None), P("dp", "expert"), P("dp", "expert"))
    return jax.shard_map(shards, mesh=mesh, in_specs=in_specs, out_specs=out_specs, check_vma=False)
```

```python
import jax
import jax.numpy as jnp
from jax import lax
from jax.experimental import pallas as pl
from jax.experimental.pallas import tpu as pltpu
from jax.sharding import PartitionSpec as P

FF = 5120
SHARDS = 16


gelu_coef = 0.7978845608028654
cubic_coef = 0.044715
step_rate = 0.5


def gelu_value(inputs):
    return (
        0.5
        * inputs
        * (1.0 + jnp.tanh(gelu_coef * (inputs + cubic_coef * inputs * inputs * inputs)))
    )


def gelu_slope(inputs):
    tangent = jnp.tanh(gelu_coef * (inputs + cubic_coef * inputs * inputs * inputs))
    return 0.5 * (1.0 + tangent) + 0.5 * inputs * (1.0 - tangent * tangent) * gelu_coef * (
        1.0 + 3.0 * cubic_coef * inputs * inputs
    )


def contract_rows(left, right):
    return lax.dot_general(
        left, right, (((0,), (0,)), ((), ())), preferred_element_type=jnp.float32
    )


def contract_cols(left, right):
    return lax.dot_general(
        left, right, (((1,), (1,)), ((), ())), preferred_element_type=jnp.float32
    )


def summed_grads(attn_partials):
    if lax.axis_size("dp") == 1:
        return attn_partials[0]
    return lax.psum_scatter(attn_partials[0], "dp", scatter_dimension=0, tiled=True)


def picked(pick, source):
    return jnp.dot(pick, source, preferred_element_type=jnp.float32)


def pack_kernel(blocks, experts, *refs):
    sources, (*outs, ids_ref, gate_ref, tokens_ref, grads_ref, sems) = refs[:4], refs[4:]
    fetches = [
        pltpu.make_async_copy(source, target, sems.at[k])
        for k, (source, target) in enumerate(
            zip(sources, (ids_ref, gate_ref, tokens_ref, grads_ref))
        )
    ]
    for fetch in fetches:
        fetch.start()
    for fetch in fetches[:2]:
        fetch.wait()
    n, width = tokens_ref.shape
    mine = (lax.axis_index("expert") // SHARDS).astype(jnp.float32)
    ids = ids_ref[...].astype(jnp.float32)
    relative = ids - mine
    relative = jnp.where(relative < 0.0, relative + experts, relative)
    down = lax.broadcasted_iota(jnp.int32, (n, n), 0)
    across = lax.broadcasted_iota(jnp.int32, (n, n), 1)
    ids_down = jnp.sum(jnp.where(down == across, ids, 0.0), axis=1, keepdims=True)
    gate_down = jnp.sum(jnp.where(down == across, gate_ref[...], 0.0), axis=1, keepdims=True)
    rivals = jnp.where((ids_down == ids) & (down < across), 1.0, 0.0)
    rank = jnp.sum(rivals, axis=0, keepdims=True)
    rows, picks = outs[: len(blocks)], outs[len(blocks) : 2 * len(blocks)]
    copies = outs[2 * len(blocks) :]

    def one_hot(shape, block, shift):
        expert, begin, end, row = block
        chosen = (relative == expert) & (rank >= begin) & (rank < end)
        slot = jnp.where(chosen, rank - begin + row + shift, -1.0).astype(jnp.int32)
        slots = lax.broadcasted_iota(jnp.int32, shape, 0)
        return jnp.where(slots == slot, 1.0, 0.0)

    uppers, lowers = [], []
    for k, block in enumerate(blocks):
        shape = picks[k].shape
        uppers.append(one_hot(shape, block, 0))
        lowers.append(uppers[k] if k < 2 else one_hot(shape, block, block[2]))
        picks[k][...] = uppers[k].astype(jnp.bfloat16)
    upper, lower = [jnp.concatenate(p, axis=0).astype(jnp.bfloat16) for p in (uppers, lowers)]
    for fetch in fetches[2:]:
        fetch.wait()
    gated = (gate_down * grads_ref[...].astype(jnp.float32)).astype(jnp.bfloat16)
    from_tokens, from_gated = picked(upper, tokens_ref[...]), picked(lower, gated)
    start = 0
    for k, rows_ref in enumerate(rows):
        part = slice(start, start + rows_ref.shape[0])
        start = part.stop
        if k < 2:
            rows_ref[:, :width] = from_tokens[part].astype(jnp.bfloat16)
            rows_ref[:, width:] = from_gated[part].astype(jnp.bfloat16)
        else:
            rows_ref[...] = (from_tokens[part] + from_gated[part]).astype(jnp.bfloat16)
    for copy_ref in copies:
        copy_ref[...] = rows[0][...]


def pack(blocks, first, rest, capacity, experts, ids, gate, tokens, grads):
    n, width = tokens.shape
    whole = pl.BlockSpec(memory_space=pltpu.VMEM)
    crossing = len(blocks) - 2

    def shape(rows, columns):
        return jax.ShapeDtypeStruct((rows, columns), jnp.bfloat16)

    shapes = [shape(first, 2 * width), shape(rest, 2 * width)]
    shapes += [shape(2 * capacity, width)] * crossing
    shapes += [shape(first, n), shape(rest, n)] + [shape(2 * capacity, n)] * crossing
    shapes += [shape(first, 2 * width)] * len(early_masks)
    sources = (ids.reshape(1, n), gate.reshape(1, n), tokens, grads)
    outs = pl.pallas_call(
        lambda *refs: pack_kernel(blocks, experts, *refs),
        out_shape=shapes,
        in_specs=[pl.BlockSpec(memory_space=pltpu.HBM)] * 4,
        out_specs=[whole] * len(shapes),
        scratch_shapes=[
            pltpu.VMEM((1, n), jnp.int32),
            pltpu.VMEM((1, n), jnp.float32),
            pltpu.VMEM((n, width), jnp.bfloat16),
            pltpu.VMEM((n, width), jnp.bfloat16),
            pltpu.SemaphoreType.DMA((4,)),
        ],
        compiler_params=pltpu.CompilerParams(vmem_limit_bytes=8 * 1024 * 1024),
    )(*[pltpu.with_memory_space_constraint(source, pltpu.HBM) for source in sources])
    return outs[: len(blocks)], outs[len(blocks) : 2 * len(blocks)], outs[2 * len(blocks) :]


def handed_on(copies, sent):
    anywhere = pl.BlockSpec(memory_space=pl.ANY)
    return pl.pallas_call(
        lambda *refs: None,
        out_shape=[jax.ShapeDtypeStruct(rows.shape, rows.dtype) for rows in copies],
        in_specs=[anywhere] * (len(copies) + len(sent)),
        out_specs=[anywhere] * len(copies),
        input_output_aliases={k: k for k in range(len(copies))},
        compiler_params=pltpu.CompilerParams(vmem_limit_bytes=1024 * 1024),
    )(*copies, *sent)


def whole_weights(shard):
    if lax.axis_size("dp") == 1:
        return shard.astype(jnp.bfloat16)
    return lax.all_gather(shard.astype(jnp.bfloat16), "dp", axis=0, tiled=True)


def expert_kernel(scale_in, scale_out, rows_ref, in_ref, out_ref, hidden_ref, pre_ref, parts_ref):
    width = in_ref.shape[1]
    pre_act = contract_cols(rows_ref[:, :width], in_ref[...]) * scale_in
    hidden_ref[...] = gelu_value(pre_act).astype(jnp.bfloat16)
    hidden_grad = contract_cols(rows_ref[:, width:], out_ref[...]) * scale_out
    pre_grad = (hidden_grad * gelu_slope(pre_act)).astype(jnp.bfloat16)
    pre_ref[...] = pre_grad
    for start in range(0, width, 512):
        columns = slice(start, start + 512)
        parts = jnp.dot(pre_grad, in_ref[:, columns], preferred_element_type=jnp.float32)
        parts_ref[:, columns] = (parts * scale_in).astype(jnp.bfloat16)


def worked(rows, weights_in, weights_out, scale_in, scale_out):
    count, (units, width) = rows.shape[0], weights_in.shape
    whole = pl.BlockSpec(memory_space=pltpu.VMEM)
    return pl.pallas_call(
        lambda *refs: expert_kernel(scale_in, scale_out, *refs),
        out_shape=[
            jax.ShapeDtypeStruct((count, columns), jnp.bfloat16)
            for columns in (units, units, width)
        ],
        in_specs=[whole] * 3,
        out_specs=[whole] * 3,
        compiler_params=pltpu.CompilerParams(vmem_limit_bytes=20 * 1024 * 1024),
        cost_estimate=pl.CostEstimate(
            flops=6 * count * units * width,
            bytes_accessed=4 * units * width,
            transcendentals=count * units,
        ),
    )(rows, weights_in, weights_out)


def step_kernel(rows, *refs):
    *refs, done_ref, sems = refs
    count = len(refs) // 3
    bases, shares, outs = refs[:count], refs[count : 2 * count], refs[2 * count :]
    writes = []
    for start in range(0, outs[0].shape[0], rows):
        part = slice(start, start + rows)
        for k in range(count):
            done_ref[k, part] = bases[k][part] - step_rate * shares[k][part].astype(jnp.float32)
            writes.append(
                pltpu.make_async_copy(done_ref.at[k, part], outs[k].at[part], sems.at[len(writes)])
            )
            writes[-1].start()
    for write in writes:
        write.wait()


def stepped(bases, shares):
    units, width = bases[0].shape
    rows = 64 if units % 64 == 0 else units
    whole = pl.BlockSpec(memory_space=pltpu.VMEM)
    return pl.pallas_call(
        lambda *refs: step_kernel(rows, *refs),
        out_shape=[jax.ShapeDtypeStruct(base.shape, base.dtype) for base in bases],
        in_specs=[whole] * (2 * len(bases)),
        out_specs=[pl.BlockSpec(memory_space=pltpu.HBM)] * len(bases),
        scratch_shapes=[
            pltpu.VMEM((len(bases), units, width), jnp.float32),
            pltpu.SemaphoreType.DMA((len(bases) * (units // rows),)),
        ],
        compiler_params=pltpu.CompilerParams(vmem_limit_bytes=16 * 1024 * 1024),
        cost_estimate=pl.CostEstimate(
            flops=4 * units * width, bytes_accessed=8 * units * width, transcendentals=0
        ),
    )(*bases, *shares)


def stepped_over_dp(weights, grads):
    grads = lax.psum_scatter(
        grads.astype(jnp.bfloat16), "dp", scatter_dimension=0, tiled=True
    ).astype(jnp.float32)
    return weights - step_rate * grads


def swap(rows, mask):
    n_expert = lax.axis_size("expert")
    return lax.ppermute(rows, "expert", [(i, i ^ mask) for i in range(n_expert)])


core_bit, x_bit, y_bit, z_bit = 1, 2, 4, 8
early_masks = (x_bit | y_bit, z_bit, x_bit, y_bit)


def after(values, *others):
    return lax.optimization_barrier((others, values))[1]


def chain(blocks):
    chained = []
    for block in blocks:
        chained.append(after(block, chained[-1]) if chained else block)
    return chained


def swaps(blocks, masks):
    return [swap(block, mask) for block, mask in zip(chain(blocks), masks)]


def total(*terms):
    return sum(term.astype(jnp.float32) for term in terms).astype(jnp.bfloat16)


def split_rows(array, rows):
    return [array[k : k + rows] for k in range(0, array.shape[0], rows)]


def shards(tokens, attn_partials, expert_ids, gate, w_in, w_out):
    tok_rows, width = tokens.shape
    n_expert = lax.axis_size("expert")
    experts = n_expert // SHARDS
    capacity = 5 * tok_rows // (8 * experts)
    first = capacity // 8 * 8
    rest = experts * capacity - first
    units = w_in.shape[1]
    scale_in = width ** (-0.5)
    scale_out = FF ** (-0.5)

    def shifted(rows, hops):
        pairs = [(i, (i + SHARDS * hops) % n_expert) for i in range(n_expert)]
        return lax.ppermute(rows, "expert", pairs)

    offset = (experts - 1) * capacity - first
    own_blocks = [(0, 0, first, 0), (0, first, capacity, offset + first)]
    cross_blocks = [(s, 0, capacity, 0) for s in range(1, experts)]
    grads = summed_grads(attn_partials)
    (early_own, late_own, *sent), picks, copies = pack(
        own_blocks + cross_blocks, first, rest, capacity, experts, expert_ids, gate, tokens, grads
    )
    early_copies = handed_on(copies, sent)

    def activated(rows):
        expert_rows, grad_rows = rows[:, :width], rows[:, width:]
        pre_act = contract_cols(expert_rows, weights_in) * scale_in
        hidden = gelu_value(pre_act).astype(jnp.bfloat16)
        hidden_grad = contract_cols(grad_rows, weights_out) * scale_out
        pre_grad = (hidden_grad * gelu_slope(pre_act)).astype(jnp.bfloat16)
        return [expert_rows, grad_rows, hidden, pre_grad]

    def input_parts(pre_grad):
        parts = jnp.dot(pre_grad, weights_in, preferred_element_type=jnp.float32) * scale_in
        return parts.astype(jnp.bfloat16)

    for s in range(1, experts):
        side_by_side = jnp.concatenate(split_rows(shifted(sent[s - 1], s), capacity), axis=1)
        late_own = late_own + jnp.pad(
            side_by_side, (((s - 1) * capacity, rest - s * capacity), (0, 0))
        )
    early_xy, early_z, early_x, early_y = after(
        [swap(rows, mask) for rows, mask in zip(early_copies, early_masks)], late_own
    )
    late_x, late_y, late_z = swaps(
        [
            jnp.concatenate([late_own, early_z], axis=0),
            jnp.concatenate([late_own, early_z], axis=0),
            jnp.concatenate([late_own, early_xy], axis=0),
        ],
        (x_bit, y_bit, z_bit),
    )
    early_zx, early_yz, early_far = late_x[rest:], late_y[rest:], late_z[rest:]
    late_x, late_y, late_z = late_x[:rest], late_y[:rest], late_z[:rest]
    early_rows = [early_own, early_x, early_y, early_z, early_xy, early_yz, early_zx, early_far]

    own_weights = jnp.concatenate([whole_weights(w_in).T, whole_weights(w_out).T], axis=0)
    their_weights = swap(after(own_weights, late_own), core_bit)
    weights_in, weights_out = [
        jnp.concatenate([own_weights[part], their_weights[part]], axis=0)
        for part in (slice(0, units), slice(units, 2 * units))
    ]
    late_xy, late_far, late_yz, late_zx = swaps(
        [late_x, late_x, late_y, late_z],
        (y_bit, y_bit | z_bit, z_bit, x_bit),
    )
    early = activated(jnp.concatenate(early_rows, axis=0))
    early_parts = input_parts(early[3])
    late_far = after([late_xy, late_yz, late_zx, late_far], early_parts)
    late_rows = [late_own, late_x, late_y, late_z, *late_far]
    late_rows = jnp.concatenate(late_rows, axis=0)
    hidden, pre_grad, late_parts = worked(late_rows, weights_in, weights_out, scale_in, scale_out)
    later = [late_rows[:, :width], late_rows[:, width:], hidden, pre_grad]
    parts = [
        jnp.concatenate(pair, axis=0)
        for pair in zip(split_rows(early_parts, first), split_rows(late_parts, rest))
    ]
    own, sum_x, sum_y, sum_z, sum_xy, sum_yz, sum_zx, sum_far = parts
    back = chain([sum_far, sum_zx, sum_xy, sum_yz])
    far, zx, xy, yz = [
        swap(rows, mask) for rows, mask in zip(back, (y_bit | z_bit, x_bit, y_bit, z_bit))
    ]

    def gradients(part, awaited):
        chunks = [chunk[:2] + after(chunk[2:], awaited) for chunk in (early, later)]
        return [
            sum(contract_rows(chunk[left][:, part], chunk[right]) for chunk in chunks) * scale
            for left, right, scale in ((3, 0, scale_in), (2, 1, scale_out))
        ]

    theirs = gradients(slice(units, 2 * units), back[-1])
    theirs = [grads.astype(jnp.bfloat16) for grads in theirs]
    zx, theirs = lax.optimization_barrier((zx, theirs))
    shares = [swap(grads, core_bit) for grads in theirs]
    mine = gradients(slice(0, units), zx)
    split_width = lax.axis_size("dp") > 1
    if not split_width:
        mine = [weights.T - step_rate * grads for weights, grads in zip((w_in, w_out), mine)]
    if split_width:
        new_weights = [
            stepped_over_dp(weights, (grads + share.astype(jnp.float32)).T)
            for weights, grads, share in zip((w_in, w_out), mine, shares)
        ]
    else:
        new_weights = [weights.T for weights in stepped(mine, shares)]
    near = swaps(
        [total(sum_z, zx), total(sum_x, xy, far), total(sum_y, yz)], (z_bit, x_bit, y_bit)
    )
    sums = total(own, *near)
    early_sum, late_sum = sums[:first], sums[first:]
    half = width // 2
    returned = [early_sum, late_sum]
    for s in range(1, experts):
        rows = late_sum[(s - 1) * capacity : s * capacity]
        rows = jnp.concatenate([rows[:, :half], rows[:, half:]], axis=0)
        rows = after(shifted(rows, -s), new_weights)
        returned.append(jnp.concatenate(split_rows(rows, capacity), axis=1))
    picks = [*picks[:2], *[pick[:capacity] for pick in picks[2:]]]
    token_grad = sum(contract_rows(pick, rows) for pick, rows in zip(picks, returned))
    return (token_grad.astype(jnp.bfloat16), *new_weights)


def solution(mesh):
    in_specs = (
        P(("expert", "dp"), None),
        P("dp", "expert", None),
        P(("expert", "dp")),
        P(("expert", "dp")),
        P("dp", "expert"),
        P("dp", "expert"),
    )
    out_specs = (P(("expert", "dp"), None), P("dp", "expert"), P("dp", "expert"))
    return jax.shard_map(shards, mesh=mesh, in_specs=in_specs, out_specs=out_specs, check_vma=False)
```
